32 devices in a mesh: batch: 8 (over y, x, core), expert: 4 (over z).
Axes of the slice: x: 2, y: 2, z: 4, core: 2. Of those that a mesh axis runs over, the one named last changes fastest.
Arguments:
- tokens: float32 [2, 16, 1024, 512], P(None, 'batch', 'expert'), may hold values from -6 to 6
- cotangent: float32 [2, 16, 1024, 512], P(None, 'batch', 'expert'), may hold values from -6 to 6
- query_key_value_weight: bfloat16 [512, 1536], replicated, may hold values from -0.25 to 0.25
- output_weight: bfloat16 [512, 512], replicated, may hold values from -2 to 2
- controller_weight: bfloat16 [512, 16], replicated, may hold values from -0.1875 to 0.1875
- w_first: bfloat16 [16, 512, 2048], P('expert'), may hold values from -0.5 to 0.5
- w_second: bfloat16 [16, 2048, 512], P('expert'), may hold values from -0.5 to 0.5
- gain_one: float32 [512], replicated, may hold values from 0.5 to 1.5
- gain_two: float32 [512], replicated, may hold values from 0.5 to 1.5
- group_sizes: int32 [2, 3], replicated, may hold values from 4 to 8, as said below
- live: int32 [2, 16], replicated, may hold values from 0 to 1, as said below
Outputs:
- out: float32 [2, 16, 1024, 512], P(None, 'batch', 'expert')
- grad_input: float32 [2, 16, 1024, 512], P(None, 'batch', 'expert')
- grad_qkv: float32 [512, 1536], P(('batch', 'expert'))
- grad_out: float32 [512, 512], P(('batch', 'expert'))
- grad_ctrl: float32 [512, 16], P(('batch', 'expert'))
- grad_first: float32 [16, 512, 2048], P('expert', None, 'batch')
- grad_second: float32 [16, 2048, 512], P('expert', 'batch')
- grad_gain_one: float32 [512], P(('batch', 'expert'))
- grad_gain_two: float32 [512], P(('batch', 'expert'))
The draws below stay inside these ranges and needn't reach their ends.
Inputs may be any that keep to these rules, and one draw needn't show every extreme that they name: `group_sizes`: each row sums to 16; one size is exactly 8, the others 4. `live`: each row has at least one 0, among its last 3 sequences.
All inputs are finite; a program needn't handle non-finite values.
Results may differ from the reference program's by a relative error of at most 0.019.
Values may be sent and summed in bfloat16 or wider, within the bound.
No kernel may reach another device: no remote copies, remote signals or barrier semaphores. Data moves between devices by JAX's collectives and lax.ppermute only.
A program may use at most 320 MiB of HBM per device.

```python
import functools
import jax
import jax.numpy as jnp
from jax import lax

D = 512
HEADS = 8
HDIM = 64
FFH = 2048
LEN = 1024
MB = 2
NGRP = 3
EXPERTS = 16
SEQS = 16


def draw_group_sizes(key, part):
    key = jax.random.fold_in(key, 11)
    biggest = jax.random.randint(key, (MB,), 0, NGRP)
    places = jnp.arange(NGRP, dtype=jnp.int32)
    return jnp.where(places[None, :] == biggest[:, None], SEQS // 2, SEQS // 4).astype(jnp.int32)


def draw_live(key, part):
    key = jax.random.fold_in(key, 23)
    key_coin, key_pick = jax.random.split(key)
    coins = jax.random.randint(key_coin, (MB, SEQS), 0, 10)
    alive = (coins < 7).astype(jnp.int32)
    picked = SEQS - 1 - jax.random.randint(key_pick, (MB,), 0, SEQS // 4 - 1)
    numbers = jnp.arange(SEQS, dtype=jnp.int32)
    return jnp.where(numbers[None, :] == picked[:, None], 0, alive).astype(jnp.int32)


def level_of(own_key, shape, cuts, smallest, high):
    loudness = 1.0
    for dim, parts in cuts:
        heights = jax.random.uniform(jax.random.fold_in(jax.random.fold_in(own_key, 6), dim), (parts,), jnp.float32, smallest / len(cuts), high / len(cuts))
        loudness = loudness * jnp.repeat(jnp.exp(heights), shape[dim] // parts).reshape((-1,) + (1,) * (len(shape) - 1 - dim))
    return loudness


def gaussian(rng, extent, spread, limit, cuts=(), kind=jnp.bfloat16):
    entries = spread * jax.random.normal(rng, extent, jnp.float32)
    if cuts:
        entries = entries * level_of(rng, extent, cuts, -0.22, 0.18)
    return jnp.clip(entries, -limit, limit).astype(kind)


def setup_inputs(seed: int = 0) -> dict:
    seeds = jax.random.split(jax.random.key(seed), 12)
    tokens = gaussian(seeds[0], (MB, SEQS, LEN, D), 1.0, 6.0, ((1, 8), (2, 4)), jnp.float32)
    cotangent = gaussian(seeds[1], (MB, SEQS, LEN, D), 1.0, 6.0, ((1, 8), (2, 4)), jnp.float32)
    query_key_value_weight = gaussian(seeds[2], (D, 3 * D), D ** -0.5, 0.25)
    output_weight = gaussian(seeds[3], (D, D), 8 ** -0.5, 2.0)
    controller_weight = gaussian(seeds[4], (D, EXPERTS), (2 * D) ** -0.5, 0.1875)
    w_first = gaussian(seeds[5], (EXPERTS, D, FFH), (D // 4) ** -0.5, 0.5, ((0, 4),))
    w_second = gaussian(seeds[6], (EXPERTS, FFH, D), (FFH // 16) ** -0.5, 0.5, ((0, 4),))
    gain_one = jnp.clip(1.0 + 0.1 * jax.random.normal(seeds[7], (D,), jnp.float32), 0.5, 1.5)
    gain_two = jnp.clip(1.0 + 0.1 * jax.random.normal(seeds[8], (D,), jnp.float32), 0.5, 1.5)
    group_sizes = draw_group_sizes(jax.random.fold_in(seeds[11], 71), 0)
    live = draw_live(jax.random.fold_in(seeds[11], 71), 0)
    return {"tokens": tokens, "cotangent": cotangent, "query_key_value_weight": query_key_value_weight, "output_weight": output_weight, "controller_weight": controller_weight, "w_first": w_first, "w_second": w_second, "gain_one": gain_one, "gain_two": gain_two, "group_sizes": group_sizes, "live": live}


HIGH_PRECISION = lax.Precision.HIGHEST
NEG_FILL = -1e+30

@jax.custom_vjp
def low(v):
    return lax.optimization_barrier(v.astype(jnp.bfloat16)).astype(jnp.float32)

@jax.custom_vjp
def low_back(v):
    return v

def low_keep(v):
    return (low(v), None)

def low_pass(kept, grad):
    return (grad,)

def back_keep(v):
    return (v, None)

def back_low(kept, grad):
    return (low(grad),)
low.defvjp(low_keep, low_pass)
low_back.defvjp(back_keep, back_low)

def group_tables(group_row, live_row):
    seq_count = live_row.shape[0]
    group_ends = jnp.cumsum(group_row)
    group_starts = group_ends - group_row
    numbers = jnp.arange(seq_count, dtype=jnp.int32)
    member = (numbers[:, None] >= group_starts[None, :]) & (numbers[:, None] < group_ends[None, :])
    leading = jnp.any(numbers[:, None] == group_starts[None, :], axis=1)
    taking = (live_row > 0) | leading
    return (member, taking)

def group_softmax(router_logits, member, taking):
    inside = member[:, :, None, None]
    masked = jnp.where(taking[:, None, None], router_logits, NEG_FILL)
    highest = lax.optimization_barrier(jnp.max(jnp.where(inside, masked[:, None], NEG_FILL), axis=0))
    row_high = lax.optimization_barrier(jnp.sum(jnp.where(inside, highest[None], 0.0), axis=1))
    scaled = jnp.where(taking[:, None, None], jnp.exp(router_logits - row_high), 0.0)
    group_sums = lax.optimization_barrier(jnp.sum(jnp.where(inside, scaled[:, None], 0.0), axis=0))
    row_sums = lax.optimization_barrier(jnp.sum(jnp.where(inside, group_sums[None], 0.0), axis=1))
    return scaled / row_sums

def layer_norm(values_in, scaling):
    centred = values_in - lax.optimization_barrier(jnp.mean(values_in, -1, keepdims=True))
    inverse = lax.rsqrt(lax.optimization_barrier(jnp.mean(centred * centred, -1, keepdims=True)) + 1e-05)
    return centred * inverse * scaling

def attend(pieces):
    queries, keys_in, values_in = pieces
    query_heads = queries.reshape(LEN, HEADS, HDIM)
    key_heads = keys_in.reshape(LEN, HEADS, HDIM)
    value_heads = values_in.reshape(LEN, HEADS, HDIM)
    scores = low_back(jnp.einsum('qhc,khc->hqk', query_heads, key_heads, precision=HIGH_PRECISION) * HDIM ** (-0.5))
    places = jnp.arange(LEN, dtype=jnp.int32)
    scores = jnp.where(places[None, :, None] >= places[None, None, :], scores, NEG_FILL)
    weights_soft = low(jax.nn.softmax(scores, axis=-1))
    return jnp.einsum('hqk,khc->qhc', weights_soft, value_heads, precision=HIGH_PRECISION).reshape(LEN, HEADS * HDIM)

def expert_rows(pieces):
    blended_rows, first_w, second_w = pieces
    pre_act = low_back(jnp.einsum('lkd,df->lkf', blended_rows, first_w, precision=HIGH_PRECISION))
    activated = low(jax.nn.gelu(pre_act))
    return low_back(low(jnp.einsum('lkf,fd->lkd', activated, second_w, precision=HIGH_PRECISION)))

def mot_layer(weights, pieces):
    input_rows, member, taking = pieces
    query_key_value_weight, output_weight, controller_weight, w_first, w_second, gain_one, gain_two = weights
    attention_input = low(layer_norm(input_rows, gain_one))
    projected_rows = low_back(low(jnp.einsum('mtg,gj->mtj', attention_input, query_key_value_weight, precision=HIGH_PRECISION)))
    context_rows = lax.map(jax.checkpoint(attend), (projected_rows[..., :D], projected_rows[..., D:2 * D], projected_rows[..., 2 * D:]))
    context_rows = low(low_back(context_rows))
    residual_stream = input_rows + low_back(jnp.einsum('mtg,gj->mtj', context_rows, output_weight, precision=HIGH_PRECISION))
    mixing_input = low(low_back(layer_norm(residual_stream, gain_two)))
    router_logits = jnp.einsum('mtg,gj->mtj', mixing_input, controller_weight, precision=HIGH_PRECISION)
    gate_vals = low(group_softmax(router_logits, member, taking))
    blend_weights = jnp.where(member[:, None, :, None], gate_vals[:, :, None, :], 0.0)
    blended_rows = low_back(low(jnp.einsum('znfu,znq->unfq', blend_weights, mixing_input, precision=HIGH_PRECISION)))
    expert_output = lax.map(jax.checkpoint(expert_rows), (blended_rows, w_first, w_second))
    dispersed_rows = low_back(low(jnp.einsum('acrw,wcrt->act', blend_weights, expert_output, precision=HIGH_PRECISION)))
    return residual_stream + dispersed_rows

def reference(tokens, cotangent, query_key_value_weight, output_weight, controller_weight, w_first, w_second, gain_one, gain_two, group_sizes, live):
    member, taking = jax.vmap(group_tables)(group_sizes, live)
    weights = (query_key_value_weight.astype(jnp.float32), output_weight.astype(jnp.float32), controller_weight.astype(jnp.float32), w_first.astype(jnp.float32), w_second.astype(jnp.float32), gain_one.astype(jnp.float32), gain_two.astype(jnp.float32))

    def run_layers(weight_set, tokens_in):
        return lax.map(functools.partial(mot_layer, weight_set), (tokens_in, member, taking))
    outputs, pullback = jax.vjp(run_layers, weights, tokens.astype(jnp.float32))
    grad_weights, grad_tokens = pullback(cotangent.astype(jnp.float32))
    return (outputs, grad_tokens, grad_weights[0], grad_weights[1], grad_weights[2], grad_weights[3], grad_weights[4], grad_weights[5], grad_weights[6])
```

```python
import functools

import jax
import jax.numpy as jnp
from jax import lax
from jax.experimental import pallas as pl
from jax.experimental.pallas import tpu as pltpu
from jax.sharding import PartitionSpec as P

HEADS = 8


HIGH_PRECISION = lax.Precision.HIGHEST
NEG_FILL = -1e30


def group_tables(group_row, live_row):
    seq_count = live_row.shape[0]
    group_ends = jnp.cumsum(group_row)
    group_starts = group_ends - group_row
    numbers = jnp.arange(seq_count, dtype=jnp.int32)
    member = (numbers[:, None] >= group_starts[None, :]) & (numbers[:, None] < group_ends[None, :])
    leading = jnp.any(numbers[:, None] == group_starts[None, :], axis=1)
    taking = (live_row > 0) | leading
    return (member, taking)


def group_softmax(router_logits, member, taking):
    inside = member[:, :, None, None]
    masked = jnp.where(taking[:, None, None], router_logits, NEG_FILL)
    highest = jnp.max(jnp.where(inside, masked[:, None], NEG_FILL), axis=0)
    row_high = jnp.sum(jnp.where(inside, highest[None], 0.0), axis=1)
    scaled = jnp.where(taking[:, None, None], jnp.exp(router_logits - row_high), 0.0)
    group_sums = jnp.sum(jnp.where(inside, scaled[:, None], 0.0), axis=0)
    row_sums = jnp.sum(jnp.where(inside, group_sums[None], 0.0), axis=1)
    return scaled / row_sums


def norm_forward(values_in, scaling):
    centred = values_in - jnp.mean(values_in, -1, keepdims=True)
    inverse = lax.rsqrt(jnp.mean(centred * centred, -1, keepdims=True) + 1e-05)
    normed = centred * inverse
    return (normed * scaling, normed, inverse)


def norm_backward(incoming, normed, inverse, scaling):
    scaled_grad = incoming * scaling
    returned_grad = inverse * (
        scaled_grad
        - jnp.mean(scaled_grad, -1, keepdims=True)
        - normed * jnp.mean(scaled_grad * normed, -1, keepdims=True)
    )
    return (returned_grad, jnp.sum(incoming * normed, axis=(0, 1)))


def attention_probs(query_heads, key_heads, causal, logsum, factor):
    scores = (
        jnp.einsum("sqhc,skhc->shqk", query_heads, key_heads, preferred_element_type=jnp.float32)
        * factor
    )
    return jnp.where(causal, jnp.exp(scores - logsum), 0.0)


def body_by_position(
    tokens,
    cotangent,
    query_key_value_weight,
    output_weight,
    controller_weight,
    w_first,
    w_second,
    gain_one,
    gain_two,
    group_sizes,
    live,
):
    micro_count, seq_here, local_len, model_width = tokens.shape
    head_dim = model_width // HEADS
    factor = head_dim ** (-0.5)
    length = local_len * lax.axis_size("expert")
    query_pos = lax.axis_index("expert") * local_len + jnp.arange(local_len, dtype=jnp.int32)
    key_pos = jnp.arange(length, dtype=jnp.int32)
    causal = key_pos[None, :] <= query_pos[:, None]
    ctrl_wide = controller_weight.astype(jnp.float32)
    sum_first = jnp.zeros(w_first.shape, jnp.float32)
    sum_second = jnp.zeros(w_second.shape, jnp.float32)
    sum_qkv = jnp.zeros(query_key_value_weight.shape, jnp.float32)
    sum_out = jnp.zeros(output_weight.shape, jnp.float32)
    sum_ctrl = jnp.zeros(controller_weight.shape, jnp.float32)
    sum_gain_one = jnp.zeros(gain_one.shape, jnp.float32)
    sum_gain_two = jnp.zeros(gain_two.shape, jnp.float32)
    outputs = []
    grads_in = []
    for micro_step in range(micro_count):
        member, taking = group_tables(group_sizes[micro_step], live[micro_step])
        input_rows = tokens[micro_step]
        attn_norm, normed_one, inverse_one = norm_forward(input_rows, gain_one)
        attention_input = attn_norm.astype(jnp.bfloat16)
        projected_rows = jnp.einsum(
            "mtg,gj->mtj",
            attention_input,
            query_key_value_weight,
            preferred_element_type=jnp.float32,
        ).astype(jnp.bfloat16)
        queries = projected_rows[..., :model_width]
        keys_here = projected_rows[..., model_width : 2 * model_width]
        values_here = projected_rows[..., 2 * model_width :]
        keys_all, values_all = (
            lax.all_gather(keys_here, "expert", axis=1, tiled=True),
            lax.all_gather(values_here, "expert", axis=1, tiled=True),
        )
        query_heads = queries.reshape(seq_here, local_len, HEADS, head_dim)
        key_heads = keys_all.reshape(seq_here, length, HEADS, head_dim)
        value_heads = values_all.reshape(seq_here, length, HEADS, head_dim)
        scores = (
            jnp.einsum(
                "sqhc,skhc->shqk", query_heads, key_heads, preferred_element_type=jnp.float32
            )
            * factor
        )
        scores = jnp.where(causal, scores, NEG_FILL)
        highest = jnp.max(scores, -1, keepdims=True)
        logsum = highest + jnp.log(jnp.sum(jnp.exp(scores - highest), -1, keepdims=True))
        probs_low = jnp.exp(scores - logsum).astype(jnp.bfloat16)
        context_rows = jnp.einsum(
            "shqk,skhc->sqhc", probs_low, value_heads, preferred_element_type=jnp.float32
        )
        context_rows = context_rows.reshape(seq_here, local_len, model_width).astype(jnp.bfloat16)
        residual_stream = input_rows + jnp.einsum(
            "mtg,gj->mtj", context_rows, output_weight, preferred_element_type=jnp.float32
        )
        mix_norm, normed_two, inverse_two = norm_forward(residual_stream, gain_two)
        mix_low = mix_norm.astype(jnp.bfloat16)
        mix_pos = lax.all_to_all(mix_low, "batch", split_axis=1, concat_axis=0, tiled=True)
        router_logits = jnp.einsum(
            "spd,de->spe", mix_pos, controller_weight, preferred_element_type=jnp.float32
        )
        gate_vals, gate_pull = jax.vjp(
            functools.partial(group_softmax, member=member, taking=taking), router_logits
        )
        weights_low = jnp.where(
            member[:, None, :, None],
            gate_vals.astype(jnp.bfloat16)[:, :, None, :],
            jnp.zeros((), jnp.bfloat16),
        )
        blended_rows = jnp.einsum(
            "spke,spd->pked", weights_low, mix_pos, preferred_element_type=jnp.float32
        ).astype(jnp.bfloat16)
        mixed_recv = lax.all_to_all(blended_rows, "expert", split_axis=2, concat_axis=0, tiled=True)
        pre_act = jnp.einsum(
            "pked,edf->pkef", mixed_recv, w_first, preferred_element_type=jnp.float32
        )
        activated, gelu_pull = jax.vjp(jax.nn.gelu, pre_act)
        act_low = activated.astype(jnp.bfloat16)
        expert_output = jnp.einsum(
            "pkef,efd->pked", act_low, w_second, preferred_element_type=jnp.float32
        ).astype(jnp.bfloat16)
        returned = lax.all_to_all(expert_output, "expert", split_axis=0, concat_axis=2, tiled=True)
        dispersed_rows = jnp.einsum(
            "spke,pked->spd", weights_low, returned, preferred_element_type=jnp.float32
        ).astype(jnp.bfloat16)
        spread_seq = lax.all_to_all(
            dispersed_rows, "batch", split_axis=0, concat_axis=1, tiled=True
        )
        outputs.append(residual_stream + spread_seq.astype(jnp.float32))
        cot_here = cotangent[micro_step]
        grad_spread = lax.all_to_all(
            cot_here.astype(jnp.bfloat16), "batch", split_axis=1, concat_axis=0, tiled=True
        )
        grad_weights = jnp.einsum(
            "spd,pked->spke", grad_spread, returned, preferred_element_type=jnp.float32
        )
        grad_eout = jnp.einsum(
            "spke,spd->pked", weights_low, grad_spread, preferred_element_type=jnp.float32
        ).astype(jnp.bfloat16)
        grad_eout_recv = lax.all_to_all(
            grad_eout, "expert", split_axis=2, concat_axis=0, tiled=True
        )
        grad_hidden = jnp.einsum(
            "pked,efd->pkef", grad_eout_recv, w_second, preferred_element_type=jnp.float32
        )
        step_second = jnp.einsum(
            "pkef,pked->efd", act_low, grad_eout_recv, preferred_element_type=jnp.float32
        )
        grad_pre = gelu_pull(grad_hidden)[0].astype(jnp.bfloat16)
        step_first = jnp.einsum(
            "pked,pkef->edf", mixed_recv, grad_pre, preferred_element_type=jnp.float32
        )
        sum_first = sum_first + step_first
        sum_second = sum_second + step_second
        grad_mixed = jnp.einsum(
            "pkef,edf->pked", grad_pre, w_first, preferred_element_type=jnp.float32
        ).astype(jnp.bfloat16)
        grad_mix_groups = lax.all_to_all(
            grad_mixed, "expert", split_axis=0, concat_axis=2, tiled=True
        )
        grad_weights = grad_weights + jnp.einsum(
            "pked,spd->spke", grad_mix_groups, mix_pos, preferred_element_type=jnp.float32
        )
        grad_gates = jnp.sum(jnp.where(member[:, None, :, None], grad_weights, 0.0), axis=2)
        grad_logits = gate_pull(grad_gates)[0]
        sum_ctrl = sum_ctrl + jnp.einsum(
            "spd,spe->de", mix_pos.astype(jnp.float32), grad_logits, precision=HIGH_PRECISION
        )
        grad_mix = jnp.einsum(
            "spke,pked->spd", weights_low, grad_mix_groups, preferred_element_type=jnp.float32
        )
        grad_mix = grad_mix + jnp.einsum(
            "spe,de->spd", grad_logits, ctrl_wide, precision=HIGH_PRECISION
        )
        grad_mix_seq = lax.all_to_all(
            grad_mix.astype(jnp.bfloat16), "batch", split_axis=0, concat_axis=1, tiled=True
        )
        grad_norm_two, gain_two_step = norm_backward(
            grad_mix_seq.astype(jnp.float32), normed_two, inverse_two, gain_two
        )
        sum_gain_two = sum_gain_two + gain_two_step
        grad_resid = cot_here + grad_norm_two
        attention_gradient = grad_resid.astype(jnp.bfloat16)
        sum_out = sum_out + jnp.einsum(
            "hui,huq->iq", context_rows, attention_gradient, preferred_element_type=jnp.float32
        )
        grad_context = jnp.einsum(
            "wfh,yh->wfy", attention_gradient, output_weight, preferred_element_type=jnp.float32
        ).astype(jnp.bfloat16)
        context_heads = grad_context.reshape(seq_here, local_len, HEADS, head_dim)
        probs_full = attention_probs(query_heads, key_heads, causal, logsum, factor)
        grad_probs = jnp.einsum(
            "sqhc,skhc->shqk", context_heads, value_heads, preferred_element_type=jnp.float32
        )
        row_dots = jnp.sum(grad_probs * probs_full, -1, keepdims=True)
        grad_scores = (probs_full * (grad_probs - row_dots)).astype(jnp.bfloat16)
        grad_query = (
            jnp.einsum(
                "shqk,skhc->sqhc", grad_scores, key_heads, preferred_element_type=jnp.float32
            )
            * factor
        )
        grad_query = grad_query.reshape(seq_here, local_len, model_width)
        key_terms = (
            jnp.einsum(
                "shqk,sqhc->skhc", grad_scores, query_heads, preferred_element_type=jnp.float32
            )
            * factor
        )
        value_terms = jnp.einsum(
            "shqk,sqhc->skhc",
            probs_full.astype(jnp.bfloat16),
            context_heads,
            preferred_element_type=jnp.float32,
        )
        grad_key, grad_value = (
            lax.psum_scatter(
                key_terms.reshape(seq_here, length, model_width).astype(jnp.bfloat16),
                "expert",
                scatter_dimension=1,
                tiled=True,
            ).astype(jnp.float32),
            lax.psum_scatter(
                value_terms.reshape(seq_here, length, model_width).astype(jnp.bfloat16),
                "expert",
                scatter_dimension=1,
                tiled=True,
            ).astype(jnp.float32),
        )
        query_key_value_row_gradient = jnp.concatenate(
            [grad_query, grad_key, grad_value], axis=-1
        ).astype(jnp.bfloat16)
        sum_qkv = sum_qkv + jnp.einsum(
            "hui,huq->iq",
            attention_input,
            query_key_value_row_gradient,
            preferred_element_type=jnp.float32,
        )
        grad_attn_in = jnp.einsum(
            "wfh,yh->wfy",
            query_key_value_row_gradient,
            query_key_value_weight,
            preferred_element_type=jnp.float32,
        )
        grad_norm_one, gain_one_step = norm_backward(
            grad_attn_in, normed_one, inverse_one, gain_one
        )
        sum_gain_one = sum_gain_one + gain_one_step
        grads_in.append(grad_resid + grad_norm_one)
    grad_first, grad_second = (
        lax.psum_scatter(
            sum_first.astype(jnp.bfloat16), "batch", scatter_dimension=2, tiled=True
        ).astype(jnp.float32),
        lax.psum_scatter(
            sum_second.astype(jnp.bfloat16), "batch", scatter_dimension=1, tiled=True
        ).astype(jnp.float32),
    )
    grad_qkv, grad_out, grad_ctrl, grad_gain_one, grad_gain_two = (
        lax.psum_scatter(sum_qkv, ("batch", "expert"), scatter_dimension=0, tiled=True),
        lax.psum_scatter(sum_out, ("batch", "expert"), scatter_dimension=0, tiled=True),
        lax.psum_scatter(sum_ctrl, ("batch", "expert"), scatter_dimension=0, tiled=True),
        lax.psum_scatter(sum_gain_one, ("batch", "expert"), scatter_dimension=0, tiled=True),
        lax.psum_scatter(sum_gain_two, ("batch", "expert"), scatter_dimension=0, tiled=True),
    )
    return (
        jnp.stack(outputs),
        jnp.stack(grads_in),
        grad_qkv,
        grad_out,
        grad_ctrl,
        grad_first,
        grad_second,
        grad_gain_one,
        grad_gain_two,
    )


F32 = jnp.float32
BF16 = jnp.bfloat16
PB = 16
CHUNKS = 2
VMEM_LIMIT = 60 * 1024 * 1024


def dot_nn(a, b):
    return lax.dot_general(a, b, (((1,), (0,)), ((), ())), preferred_element_type=F32)


def dot_nt(a, b):
    return lax.dot_general(a, b, (((1,), (1,)), ((), ())), preferred_element_type=F32)


def dot_tn(a, b):
    return lax.dot_general(a, b, (((0,), (0,)), ((), ())), preferred_element_type=F32)


def row_norm(rows):
    centred = rows - jnp.mean(rows, -1, keepdims=True)
    inverse = lax.rsqrt(jnp.mean(centred * centred, -1, keepdims=True) + 1e-05)
    return centred * inverse, inverse


def row_norm_back(incoming, normed, inverse, gain):
    scaled = incoming * gain
    return inverse * (
        scaled
        - jnp.mean(scaled, -1, keepdims=True)
        - normed * jnp.mean(scaled * normed, -1, keepdims=True)
    )


def head_lanes(rows, lanes, head):
    lane = lax.broadcasted_iota(jnp.int32, (rows, lanes), 1)
    return (lane < lanes // 2) if head == 0 else (lane >= lanes // 2)


def causal_tile(size):
    key = lax.broadcasted_iota(jnp.int32, (size, size), 0)
    query = lax.broadcasted_iota(jnp.int32, (size, size), 1)
    return key <= query


def attention_forward_kernel(x_ref, wqkv_ref, wo_ref, g1_ref, g2_ref,
                             qkv_ref, lse_ref, ctx_ref, attn_ref, mix_ref, ctx_pairs):
    length, width = x_ref.shape
    pairs = HEADS // 2
    lanes = width // pairs
    half = lanes // 2
    nb, quarters, piece, _ = mix_ref.shape
    tile = length // quarters
    factor = half ** (-0.5)

    def project(i, carry):
        rows = pl.ds(pl.multiple_of(i * tile, tile), tile)
        normed, _ = row_norm(x_ref[rows, :].astype(F32))
        attn_in = (normed * g1_ref[...]).astype(BF16)
        for part in range(3):
            out = dot_nn(attn_in, wqkv_ref[:, part * width:(part + 1) * width]).astype(BF16)
            for p in range(pairs):
                qkv_ref[part * pairs + p, rows, :] = out[:, p * lanes:(p + 1) * lanes]
        return carry

    lax.fori_loop(0, quarters, project, 0)

    def attend(p, carry):
        values_t = qkv_ref[2 * pairs + p].T
        for j in range(quarters):
            seen = (j + 1) * tile
            queries = qkv_ref[p, j * tile:seen, :] * jnp.asarray(factor, BF16)
            outs = []
            for h in range(2):
                masked = jnp.where(head_lanes(tile, lanes, h), queries, jnp.zeros((), BF16))
                scores = dot_nt(qkv_ref[pairs + p, :seen, :], masked)
                last = jnp.where(causal_tile(tile), scores[j * tile:], NEG_FILL)
                scores = jnp.concatenate([scores[:j * tile], last], 0) if j else last
                high = jnp.max(scores, 0, keepdims=True)
                weights = jnp.exp(scores - high)
                total = jnp.sum(weights, 0, keepdims=True)
                out = dot_nn(values_t[h * half:(h + 1) * half, :seen], weights.astype(BF16))
                outs.append(out / total)
                lse_ref[2 * p + h, :, j * tile:seen] = high + jnp.log(total)
            ctx_pairs[p, j * tile:seen, :] = jnp.concatenate(outs, 0).T.astype(BF16)
        return carry

    lax.fori_loop(0, pairs, attend, 0)

    def finish(i, carry):
        rows = pl.ds(pl.multiple_of(i * tile, tile), tile)
        context = jnp.concatenate([ctx_pairs[p, rows, :] for p in range(pairs)], -1)
        ctx_ref[rows, :] = context
        attn = dot_nn(context, wo_ref[...])
        attn_ref[rows, :] = attn
        normed, _ = row_norm(x_ref[rows, :].astype(F32) + attn)
        mix = (normed * g2_ref[...]).astype(BF16)
        for b in range(nb):
            mix_ref[b, i, :, :] = mix[b * piece:(b + 1) * piece]
        return carry

    lax.fori_loop(0, quarters, finish, 0)


def attention_forward(x, wqkv, wo, g1, g2, nb, quarters):
    length, width = x.shape
    pairs = HEADS // 2
    lanes = width // pairs
    return pl.pallas_call(
        attention_forward_kernel,
        out_shape=(
            jax.ShapeDtypeStruct((3 * pairs, length, lanes), BF16),
            jax.ShapeDtypeStruct((HEADS, 1, length), F32),
            jax.ShapeDtypeStruct((length, width), BF16),
            jax.ShapeDtypeStruct((length, width), F32),
            jax.ShapeDtypeStruct((nb, quarters, length // quarters // nb, width), BF16),
        ),
        scratch_shapes=[pltpu.VMEM((pairs, length, lanes), BF16)],
        compiler_params=pltpu.CompilerParams(vmem_limit_bytes=VMEM_LIMIT),
        cost_estimate=pl.CostEstimate(flops=15_000_000_000, bytes_accessed=12_000_000, transcendentals=5_000_000),
        name="attention_forward",
    )(x, wqkv, wo, g1, g2)


def attention_backward_kernel(gm_ref, cot_ref, x_ref, attn_ref, ctx_ref, qkv_ref, lse_ref,
                              wqkv_ref, wo_ref, g1_ref, g2_ref,
                              gin_ref, dqkv_ref, dwo_ref, dg1_ref, dg2_ref,
                              delta, ga_rows, dctx, gqkv, attn_in, dk_sum, dv_sum):
    length, width = x_ref.shape
    pairs = HEADS // 2
    lanes = width // pairs
    half = lanes // 2
    nb, quarters, piece, _ = gm_ref.shape
    tile = length // quarters
    factor = half ** (-0.5)
    dg2_ref[...] = jnp.zeros_like(dg2_ref)
    dg1_ref[...] = jnp.zeros_like(dg1_ref)

    def first(i, carry):
        rows = pl.ds(pl.multiple_of(i * tile, tile), tile)
        normed, inverse = row_norm(x_ref[rows, :].astype(F32) + attn_ref[rows, :])
        grad = jnp.concatenate([gm_ref[b, i] for b in range(nb)], 0).astype(F32)
        dg2_ref[...] += jnp.sum(grad * normed, 0, keepdims=True)
        back = row_norm_back(grad, normed, inverse, g2_ref[...])
        delta[rows, :] = back
        cot = jnp.concatenate([cot_ref[b, i] for b in range(nb)], 0).astype(F32)
        grad_attn = (cot + back).astype(BF16)
        ga_rows[rows, :] = grad_attn
        grad_ctx = dot_nt(grad_attn, wo_ref[...]).astype(BF16)
        for p in range(pairs):
            dctx[p, rows, :] = grad_ctx[:, p * lanes:(p + 1) * lanes]
        return carry

    lax.fori_loop(0, quarters, first, 0)

    dwo_ref[...] = dot_tn(ctx_ref[...], ga_rows[...])

    def attend(p, carry):
        lane0 = pl.multiple_of(p * lanes, lanes)
        keys_t = qkv_ref[pairs + p].T
        dk_sum[...] = jnp.zeros_like(dk_sum)
        dv_sum[...] = jnp.zeros_like(dv_sum)
        for j in range(quarters):
            seen = (j + 1) * tile
            queries = qkv_ref[p, j * tile:seen, :] * jnp.asarray(factor, BF16)
            grads = dctx[p, j * tile:seen, :]
            context = ctx_ref[j * tile:seen, pl.ds(lane0, lanes)]
            products = (grads.astype(F32) * context.astype(F32)).T
            outs = []
            for h in range(2):
                inside = head_lanes(tile, lanes, h)
                q_masked = jnp.where(inside, queries, jnp.zeros((), BF16))
                g_masked = jnp.where(inside, grads, jnp.zeros((), BF16))
                dots = jnp.sum(products[h * half:(h + 1) * half], 0, keepdims=True)
                scores = dot_nt(qkv_ref[pairs + p, :seen, :], q_masked)
                probs = jnp.exp(scores - lse_ref[2 * p + h, :, j * tile:seen])
                last = jnp.where(causal_tile(tile), probs[j * tile:], 0.0)
                probs = jnp.concatenate([probs[:j * tile], last], 0) if j else last
                grad_probs = dot_nt(qkv_ref[2 * pairs + p, :seen, :], g_masked)
                grad_scores = (probs * (grad_probs - dots)).astype(BF16)
                dv_sum[:seen, :] += dot_nn(probs.astype(BF16), g_masked)
                dk_sum[:seen, :] += dot_nn(grad_scores, q_masked)
                outs.append(dot_nn(keys_t[h * half:(h + 1) * half, :seen], grad_scores))
            gqkv[p, j * tile:seen, :] = (jnp.concatenate(outs, 0).T * factor).astype(BF16)
        gqkv[pairs + p] = dk_sum[...].astype(BF16)
        gqkv[2 * pairs + p] = dv_sum[...].astype(BF16)
        return carry

    lax.fori_loop(0, pairs, attend, 0)

    def last(i, carry):
        rows = pl.ds(pl.multiple_of(i * tile, tile), tile)
        normed, inverse = row_norm(x_ref[rows, :].astype(F32))
        attn_in[rows, :] = (normed * g1_ref[...]).astype(BF16)
        grads = jnp.concatenate([gqkv[c, rows, :] for c in range(3 * pairs)], -1)
        grad = dot_nt(grads, wqkv_ref[...])
        dg1_ref[...] += jnp.sum(grad * normed, 0, keepdims=True)
        gin_ref[rows, :] = (delta[rows, :] + row_norm_back(grad, normed, inverse, g1_ref[...])).astype(BF16)
        return carry

    lax.fori_loop(0, quarters, last, 0)

    for c in range(3):
        grads = jnp.concatenate([gqkv[c * pairs + p] for p in range(pairs)], -1)
        dqkv_ref[:, c * width:(c + 1) * width] = dot_tn(attn_in[...], grads)


def attention_backward(gm, cot, x, attn, ctx, qkv, lse, wqkv, wo, g1, g2):
    length, width = x.shape
    pairs = HEADS // 2
    lanes = width // pairs
    return pl.pallas_call(
        attention_backward_kernel,
        out_shape=(
            jax.ShapeDtypeStruct((length, width), BF16),
            jax.ShapeDtypeStruct((width, 3 * width), F32),
            jax.ShapeDtypeStruct((width, width), F32),
            jax.ShapeDtypeStruct((1, width), F32),
            jax.ShapeDtypeStruct((1, width), F32),
        ),
        scratch_shapes=[
            pltpu.VMEM((length, width), F32),
            pltpu.VMEM((length, width), BF16),
            pltpu.VMEM((pairs, length, lanes), BF16),
            pltpu.VMEM((3 * pairs, length, lanes), BF16),
            pltpu.VMEM((length, width), BF16),
            pltpu.VMEM((length, lanes), F32),
            pltpu.VMEM((length, lanes), F32),
        ],
        compiler_params=pltpu.CompilerParams(vmem_limit_bytes=VMEM_LIMIT),
        cost_estimate=pl.CostEstimate(flops=35_000_000_000, bytes_accessed=20_000_000, transcendentals=5_000_000),
        name="attention_backward",
    )(gm, cot, x, attn, ctx, qkv, lse, wqkv, wo, g1, g2)


def group_reduce(rows, mem, op, fill):
    result = jnp.zeros_like(rows)
    for k in range(mem.shape[0]):
        inside = mem[k:k + 1, :] > 0
        part = jnp.where(inside, rows, fill)
        shift = rows.shape[1] // 2
        while shift >= PB:
            part = op(part, pltpu.roll(part, shift, 1))
            shift //= 2
        result = jnp.where(inside, part, result)
    return result


def gelu_both(v):
    square = v * v
    tanh = jnp.tanh(0.7978845608028654 * v * (1.0 + 0.044715 * square))
    half = 0.5 * (1.0 + tanh)
    slope = half + v * (1.0 - tanh * tanh) * (0.3989422804014327 + 0.0535161223274472 * square)
    return v * half, slope


def moe_kernel(chunk, z_ref, *refs):
    n = 4
    xs_in, gs_in = refs[:n], refs[n:2 * n]
    (ctrl_ref, mem_ref, mkl_ref, take_ref, w1_ref, w2_ref,
     spread_ref, gm_ref, mixed_ref, geo_ref, hid_ref, gpre_ref, dctrl_ref,
     xs, gs, logits, gates, weights, eo, gmx, sems) = refs[2 * n:]
    planes, nb, quarters, piece, width = xs.shape
    micro = mem_ref.shape[0]
    sl = planes // micro
    lanes = mem_ref.shape[2]
    experts = mixed_ref.shape[0]
    rows = mkl_ref.shape[1]
    halves = piece // PB
    per_micro = quarters * halves
    e = pl.program_id(0)

    def x_block(m, q, h):
        at = pl.ds(pl.multiple_of(h * PB, PB), PB)
        return jnp.concatenate(
            [xs[m * sl + s, :, q, at, :].reshape(nb * PB, width) for s in range(sl)], 0)

    def g_block(m, q, h):
        at = pl.ds(pl.multiple_of(h * PB, PB), PB)
        return jnp.concatenate(
            [gs[q, :, m * sl + s, at, :].reshape(nb * PB, width) for s in range(sl)], 0)

    def store_block(ref, m, q, h, value):
        at = pl.ds(pl.multiple_of(h * PB, PB), PB)
        for s in range(sl):
            part = value[s * nb * PB:(s + 1) * nb * PB].reshape(nb, PB, width)
            ref[m * sl + s, :, q, at, :] = part

    @pl.when(e == 0)
    def _():
        z = z_ref[0]
        for k in range(n):
            source = lax.rem(z - k + n, n)
            pltpu.make_async_copy(xs_in[k], xs.at[source], sems.at[k]).start()
        for k in range(n):
            source = lax.rem(z - k + n, n)

            @pl.when(source // quarters == chunk)
            def _():
                slot = gs.at[lax.rem(source, quarters)]
                pltpu.make_async_copy(gs_in[k], slot, sems.at[n + k]).start()

        for k in range(n):
            source = lax.rem(z - k + n, n)
            pltpu.make_async_copy(xs_in[k], xs.at[source], sems.at[k]).wait()

        for m in range(micro):
            def score(i, carry):
                block = x_block(m, i // halves, lax.rem(i, halves))
                at = pl.ds(pl.multiple_of(i * 8, 8), 8)
                logits[m, at, :] = dot_nt(ctrl_ref[...], block)[:8]
                return carry

            lax.fori_loop(0, per_micro, score, 0)
            mem = mem_ref[m]
            taking = take_ref[m] > 0
            values = logits[m]
            high = group_reduce(jnp.where(taking, values, NEG_FILL), mem, jnp.maximum, NEG_FILL)
            scaled = jnp.where(taking, jnp.exp(values - high), 0.0)
            gates[m] = scaled / group_reduce(scaled, mem, jnp.add, 0.0)

        for k in range(n):
            source = lax.rem(z - k + n, n)

            @pl.when(source // quarters == chunk)
            def _():
                slot = gs.at[lax.rem(source, quarters)]
                pltpu.make_async_copy(gs_in[k], slot, sems.at[n + k]).wait()

        for m in range(micro):
            def blend(i, carry):
                q, h = i // halves, lax.rem(i, halves)
                block = m * per_micro + i
                own = gates[m, pl.ds(pl.multiple_of(i * 8, 8), 8), :]
                w = jnp.concatenate(
                    [(mkl_ref[m] * own[j:j + 1, :]).astype(BF16) for j in range(experts)], 0)
                weights[block] = w
                blended = dot_nn(w, x_block(m, q, h)).astype(BF16)
                grads = dot_nn(w, g_block(m, q, h)).astype(BF16)
                at = pl.ds(pl.multiple_of(block * rows, rows), rows)
                for j in range(experts):
                    mixed_ref[j, at, :] = blended[j * rows:(j + 1) * rows]
                    geo_ref[j, at, :] = grads[j * rows:(j + 1) * rows]
                return carry

            lax.fori_loop(0, per_micro, blend, 0)

    hidden_size = w1_ref.shape[2]
    step = 512
    blended, grads = mixed_ref[e], geo_ref[e]
    out_sum = jnp.zeros(blended.shape, F32)
    back_sum = jnp.zeros(blended.shape, F32)
    for f in range(0, hidden_size, step):
        first, second = w1_ref[0, :, f:f + step], w2_ref[0, f:f + step, :]
        value, slope = gelu_both(dot_nn(blended, first))
        hidden = value.astype(BF16)
        hid_ref[0, :, f:f + step] = hidden
        out_sum += dot_nn(hidden, second)
        grad_pre = (dot_nt(grads, second) * slope).astype(BF16)
        gpre_ref[0, :, f:f + step] = grad_pre
        back_sum += dot_nt(grad_pre, first)
    eo[e] = out_sum.astype(BF16)
    gmx[e] = back_sum.astype(BF16)

    @pl.when(e == experts - 1)
    def _():
        dctrl_ref[...] = jnp.zeros_like(dctrl_ref)
        ctrl8 = ctrl_ref[:8, :]
        ctrl_twice = jnp.concatenate([ctrl8.astype(F32), ctrl8.astype(F32)], 0).astype(BF16)
        for m in range(micro):
            def spread_out(i, carry):
                q, h = i // halves, lax.rem(i, halves)
                block = m * per_micro + i
                at = pl.ds(pl.multiple_of(block * rows, rows), rows)
                outs = jnp.concatenate([eo[j, at, :] for j in range(experts)], 0)
                backs = jnp.concatenate([gmx[j, at, :] for j in range(experts)], 0)
                w = weights[block]
                x_rows, g_rows = x_block(m, q, h), g_block(m, q, h)
                store_block(spread_ref, m, q, h, dot_tn(w, outs).astype(BF16))
                dots = dot_nt(outs, g_rows) + dot_nt(backs, x_rows)
                grad_gates = [
                    jnp.sum(dots[j * rows:(j + 1) * rows] * mkl_ref[m], 0, keepdims=True)
                    for j in range(experts)]
                if experts < 8:
                    grad_gates.append(jnp.zeros((8 - experts, lanes), F32))
                grad_gates = jnp.concatenate(grad_gates, 0)
                own = gates[m, pl.ds(pl.multiple_of(i * 8, 8), 8), :]
                inner = group_reduce(own * grad_gates, mem_ref[m], jnp.add, 0.0)
                grad_logits = own * (grad_gates - inner)
                upper = grad_logits.astype(BF16).astype(F32)
                both = jnp.concatenate([upper, grad_logits - upper], 0).astype(BF16)
                grad_mix = dot_tn(w, backs) + dot_tn(both, ctrl_twice)
                store_block(gm_ref, m, q, h, grad_mix.astype(BF16))
                dctrl_ref[...] += dot_nn(both, x_rows)
                return carry

            lax.fori_loop(0, per_micro, spread_out, 0)


def moe(chunk, z, x_parts, g_parts, ctrl, mem, mkl, take, w1, w2):
    planes = len(x_parts)
    nb, quarters, piece, width = x_parts[0].shape
    micro, groups, lanes = mem.shape
    experts, _, hidden_size = w1.shape
    rows = mkl.shape[1]
    blocks = micro * quarters * (piece // PB)
    total = blocks * rows
    whole = lambda shape: pl.BlockSpec(shape, lambda e: (0,) * len(shape))
    back_shape = (planes, nb, quarters, piece, width)
    any_spec = pl.BlockSpec(memory_space=pl.ANY)
    flops = experts * total * width * hidden_size * 8 + 4_000_000_000
    return pl.pallas_call(
        functools.partial(moe_kernel, chunk),
        grid=(experts,),
        out_shape=(
            jax.ShapeDtypeStruct(back_shape, BF16),
            jax.ShapeDtypeStruct(back_shape, BF16),
            jax.ShapeDtypeStruct((experts, total, width), BF16),
            jax.ShapeDtypeStruct((experts, total, width), BF16),
            jax.ShapeDtypeStruct((experts, total, hidden_size), BF16),
            jax.ShapeDtypeStruct((experts, total, hidden_size), BF16),
            jax.ShapeDtypeStruct((16, width), F32),
        ),
        in_specs=[pl.BlockSpec(memory_space=pltpu.SMEM)] + [any_spec] * (2 * planes) + [
            whole(ctrl.shape), whole(mem.shape), whole(mkl.shape), whole(take.shape),
            pl.BlockSpec((1, width, hidden_size), lambda e: (e, 0, 0)),
            pl.BlockSpec((1, hidden_size, width), lambda e: (e, 0, 0)),
        ],
        out_specs=(
            whole(back_shape), whole(back_shape),
            whole((experts, total, width)), whole((experts, total, width)),
            pl.BlockSpec((1, total, hidden_size), lambda e: (e, 0, 0)),
            pl.BlockSpec((1, total, hidden_size), lambda e: (e, 0, 0)),
            whole((16, width)),
        ),
        scratch_shapes=[
            pltpu.VMEM(back_shape, BF16),
            pltpu.VMEM((quarters, nb, planes, piece, width), BF16),
            pltpu.VMEM((micro, blocks // micro * 8, lanes), F32),
            pltpu.VMEM((micro, blocks // micro * 8, lanes), F32),
            pltpu.VMEM((blocks, experts * rows, lanes), BF16),
            pltpu.VMEM((experts, total, width), BF16),
            pltpu.VMEM((experts, total, width), BF16),
            pltpu.SemaphoreType.DMA((2 * planes,)),
        ],
        compiler_params=pltpu.CompilerParams(vmem_limit_bytes=VMEM_LIMIT),
        cost_estimate=pl.CostEstimate(flops=flops, bytes_accessed=50_000_000, transcendentals=experts * total * hidden_size),
        name="mixture",
    )(z, *x_parts, *g_parts, ctrl, mem, mkl, take, w1, w2)


def ring(count):
    return [(i, (i + 1) % count) for i in range(count)]


def ring_gather(block, count):
    parts = [block]
    for _ in range(count - 1):
        parts.append(lax.ppermute(parts[-1], "expert", ring(count)))
    return parts


def ring_scatter(parts, z, count):
    def own(step):
        return lax.dynamic_index_in_dim(parts, lax.rem(z - step + 2 * count, count), 0, keepdims=False)

    held = own(1)
    for step in range(1, count):
        held = lax.ppermute(held, "expert", ring(count))
        held = (held.astype(F32) + own(step + 1).astype(F32)).astype(BF16)
    return held


def body(
    tokens,
    cotangent,
    query_key_value_weight,
    output_weight,
    controller_weight,
    w_first,
    w_second,
    gain_one,
    gain_two,
    group_sizes,
    live,
):
    micro, sl, local_len, width = tokens.shape
    planes = lax.axis_size("expert")
    nb = lax.axis_size("batch")
    experts = w_first.shape[0]
    seqs = live.shape[1]
    z = lax.axis_index("expert")
    piece = local_len // nb
    if micro * sl != planes or piece % PB:
        return body_by_position(
            tokens, cotangent, query_key_value_weight, output_weight, controller_weight,
            w_first, w_second, gain_one, gain_two, group_sizes, live)
    g1, g2 = gain_one.reshape(1, width), gain_two.reshape(1, width)

    sent = tokens.astype(BF16).reshape(planes, local_len, width)
    x = lax.all_to_all(sent, "expert", split_axis=0, concat_axis=0, tiled=True)
    x = x.reshape(planes * local_len, width)

    cot = cotangent.astype(BF16).reshape(planes, nb, piece, width).transpose(1, 0, 2, 3)
    cot = lax.all_to_all(cot, "batch", split_axis=0, concat_axis=0, tiled=True)
    cot_parts = ring_gather(cot, planes)

    qkv, lse, ctx, attn, mix = attention_forward(
        x, query_key_value_weight, output_weight, g1, g2, nb, planes)

    member, taking = jax.vmap(group_tables)(group_sizes, live)
    groups = member.shape[2]
    mem = member.reshape(micro, nb, sl, groups).transpose(0, 3, 2, 1).reshape(micro, groups, seqs)
    mem = jnp.repeat(mem.astype(F32), PB, axis=2)
    take = taking.reshape(micro, nb, sl).transpose(0, 2, 1).reshape(micro, 1, seqs)
    take = jnp.repeat(take.astype(F32), PB, axis=2)
    place = jnp.arange(seqs * PB, dtype=jnp.int32) % PB
    same = (jnp.arange(PB, dtype=jnp.int32)[:, None] == place[None, :]).astype(F32)
    mkl = (mem[:, :, None, :] * same).reshape(micro, groups * PB, seqs * PB)
    ctrl = lax.dynamic_slice_in_dim(controller_weight, z * experts, experts, 1).T
    ctrl = jnp.pad(ctrl, ((0, 16 - experts), (0, 0)))
    z_arr = z.astype(jnp.int32).reshape(1)

    quarters = planes // CHUNKS
    spreads, backs, kept, dctrl = [], [], [], 0.0
    for c in range(CHUNKS):
        own = lax.all_to_all(
            mix[:, c * quarters:(c + 1) * quarters], "batch", split_axis=0, concat_axis=0, tiled=True)
        x_parts = ring_gather(own, planes)
        spread, back, mixed, geo, hid, gpre, dc = moe(
            c, z_arr, x_parts, cot_parts, ctrl, mem, mkl, take, w_first, w_second)
        back = ring_scatter(back, z, planes)
        backs.append(lax.all_to_all(back, "batch", split_axis=0, concat_axis=0, tiled=True))
        spread = ring_scatter(spread, z, planes)
        spreads.append(lax.all_to_all(spread, "batch", split_axis=0, concat_axis=0, tiled=True))
        kept.append((mixed, geo, hid, gpre))
        dctrl = dctrl + dc[:8] + dc[8:]
    back = jnp.concatenate(backs, 1)
    spread = jnp.concatenate(spreads, 1)

    mixed, geo, hid, gpre = [jnp.concatenate(parts, 1) for parts in zip(*kept)]
    sum_first = jnp.einsum("erd,erf->edf", mixed, gpre, preferred_element_type=F32).astype(BF16)
    sum_second = jnp.einsum("erf,erd->efd", hid, geo, preferred_element_type=F32).astype(BF16)
    grad_first = lax.psum_scatter(sum_first, "batch", scatter_dimension=2, tiled=True).astype(F32)
    grad_second = lax.psum_scatter(sum_second, "batch", scatter_dimension=1, tiled=True).astype(F32)

    cot_all = jnp.stack(cot_parts)
    order = lax.rem(z - jnp.arange(planes) + planes, planes)
    cot_own = lax.dynamic_index_in_dim(cot_all, z, 2, keepdims=False)
    cot_own = jnp.take(cot_own, order, axis=0).transpose(1, 0, 2, 3)
    cot_own = lax.all_to_all(cot_own, "batch", split_axis=0, concat_axis=0, tiled=True)

    gin, dqkv, dwo, dg1, dg2 = attention_backward(
        back, cot_own, x, attn, ctx, qkv, lse, query_key_value_weight, output_weight, g1, g2)

    spread = spread.transpose(1, 0, 2, 3).reshape(planes, local_len, width)
    out = (attn.reshape(planes, local_len, width) + spread.astype(F32)).astype(BF16)
    out = lax.all_to_all(out, "expert", split_axis=0, concat_axis=0, tiled=True)
    out = tokens + out.reshape(tokens.shape).astype(F32)
    gin = lax.all_to_all(
        gin.reshape(planes, local_len, width), "expert", split_axis=0, concat_axis=0, tiled=True)
    grad_in = cotangent + gin.reshape(tokens.shape).astype(F32)

    dctrl_all = jnp.zeros((planes, experts, width), F32)
    dctrl_all = lax.dynamic_update_slice(dctrl_all, dctrl[None, :experts], (z, 0, 0))
    dctrl_all = dctrl_all.reshape(planes * experts, width).T
    axes = ("batch", "expert")
    flat = jnp.concatenate([dqkv, dwo, dctrl_all, dg1.T, dg2.T], 1)
    flat = lax.psum_scatter(flat, axes, scatter_dimension=0, tiled=True)
    ends = [3 * width, 4 * width, 4 * width + planes * experts]
    grad_qkv, grad_out, grad_ctrl = flat[:, :ends[0]], flat[:, ends[0]:ends[1]], flat[:, ends[1]:ends[2]]
    return (out, grad_in, grad_qkv, grad_out, grad_ctrl, grad_first, grad_second,
            flat[:, ends[2]], flat[:, ends[2] + 1])


def solution(mesh):
    placed = (
        P(None, "batch", "expert", None),
        P(None, "batch", "expert", None),
        P(),
        P(),
        P(),
        P("expert", None, None),
        P("expert", None, None),
        P(),
        P(),
        P(),
        P(),
    )
    return jax.shard_map(
        body,
        mesh=mesh,
        in_specs=placed,
        out_specs=(
            P(None, "batch", "expert", None),
            P(None, "batch", "expert", None),
            P(("batch", "expert"), None),
            P(("batch", "expert"), None),
            P(("batch", "expert"), None),
            P("expert", None, "batch"),
            P("expert", "batch", None),
            P(("batch", "expert")),
            P(("batch", "expert")),
        ),
        check_vma=False,
    )
```

```python
import functools

import jax
import jax.numpy as jnp
from jax import lax
from jax.experimental import pallas as pl
from jax.experimental.pallas import tpu as pltpu
from jax.sharding import PartitionSpec as P

HEADS = 8


HIGH_PRECISION = lax.Precision.HIGHEST
NEG_FILL = -1e30


def group_tables(group_row, live_row):
    seq_count = live_row.shape[0]
    group_ends = jnp.cumsum(group_row)
    group_starts = group_ends - group_row
    numbers = jnp.arange(seq_count, dtype=jnp.int32)
    member = (numbers[:, None] >= group_starts[None, :]) & (numbers[:, None] < group_ends[None, :])
    leading = jnp.any(numbers[:, None] == group_starts[None, :], axis=1)
    taking = (live_row > 0) | leading
    return (member, taking)


def group_softmax(router_logits, member, taking):
    inside = member[:, :, None, None]
    masked = jnp.where(taking[:, None, None], router_logits, NEG_FILL)
    highest = jnp.max(jnp.where(inside, masked[:, None], NEG_FILL), axis=0)
    row_high = jnp.sum(jnp.where(inside, highest[None], 0.0), axis=1)
    scaled = jnp.where(taking[:, None, None], jnp.exp(router_logits - row_high), 0.0)
    group_sums = jnp.sum(jnp.where(inside, scaled[:, None], 0.0), axis=0)
    row_sums = jnp.sum(jnp.where(inside, group_sums[None], 0.0), axis=1)
    return scaled / row_sums


def norm_forward(values_in, scaling):
    centred = values_in - jnp.mean(values_in, -1, keepdims=True)
    inverse = lax.rsqrt(jnp.mean(centred * centred, -1, keepdims=True) + 1e-05)
    normed = centred * inverse
    return (normed * scaling, normed, inverse)


def norm_backward(incoming, normed, inverse, scaling):
    scaled_grad = incoming * scaling
    returned_grad = inverse * (
        scaled_grad
        - jnp.mean(scaled_grad, -1, keepdims=True)
        - normed * jnp.mean(scaled_grad * normed, -1, keepdims=True)
    )
    return (returned_grad, jnp.sum(incoming * normed, axis=(0, 1)))


def attention_probs(query_heads, key_heads, causal, logsum, factor):
    scores = (
        jnp.einsum("sqhc,skhc->shqk", query_heads, key_heads, preferred_element_type=jnp.float32)
        * factor
    )
    return jnp.where(causal, jnp.exp(scores - logsum), 0.0)


def body_by_position(
    tokens,
    cotangent,
    query_key_value_weight,
    output_weight,
    controller_weight,
    w_first,
    w_second,
    gain_one,
    gain_two,
    group_sizes,
    live,
):
    micro_count, seq_here, local_len, model_width = tokens.shape
    head_dim = model_width // HEADS
    factor = head_dim ** (-0.5)
    length = local_len * lax.axis_size("expert")
    query_pos = lax.axis_index("expert") * local_len + jnp.arange(local_len, dtype=jnp.int32)
    key_pos = jnp.arange(length, dtype=jnp.int32)
    causal = key_pos[None, :] <= query_pos[:, None]
    ctrl_wide = controller_weight.astype(jnp.float32)
    sum_first = jnp.zeros(w_first.shape, jnp.float32)
    sum_second = jnp.zeros(w_second.shape, jnp.float32)
    sum_qkv = jnp.zeros(query_key_value_weight.shape, jnp.float32)
    sum_out = jnp.zeros(output_weight.shape, jnp.float32)
    sum_ctrl = jnp.zeros(controller_weight.shape, jnp.float32)
    sum_gain_one = jnp.zeros(gain_one.shape, jnp.float32)
    sum_gain_two = jnp.zeros(gain_two.shape, jnp.float32)
    outputs = []
    grads_in = []
    for micro_step in range(micro_count):
        member, taking = group_tables(group_sizes[micro_step], live[micro_step])
        input_rows = tokens[micro_step]
        attn_norm, normed_one, inverse_one = norm_forward(input_rows, gain_one)
        attention_input = attn_norm.astype(jnp.bfloat16)
        projected_rows = jnp.einsum(
            "mtg,gj->mtj",
            attention_input,
            query_key_value_weight,
            preferred_element_type=jnp.float32,
        ).astype(jnp.bfloat16)
        queries = projected_rows[..., :model_width]
        keys_here = projected_rows[..., model_width : 2 * model_width]
        values_here = projected_rows[..., 2 * model_width :]
        keys_all, values_all = (
            lax.all_gather(keys_here, "expert", axis=1, tiled=True),
            lax.all_gather(values_here, "expert", axis=1, tiled=True),
        )
        query_heads = queries.reshape(seq_here, local_len, HEADS, head_dim)
        key_heads = keys_all.reshape(seq_here, length, HEADS, head_dim)
        value_heads = values_all.reshape(seq_here, length, HEADS, head_dim)
        scores = (
            jnp.einsum(
                "sqhc,skhc->shqk", query_heads, key_heads, preferred_element_type=jnp.float32
            )
            * factor
        )
        scores = jnp.where(causal, scores, NEG_FILL)
        highest = jnp.max(scores, -1, keepdims=True)
        logsum = highest + jnp.log(jnp.sum(jnp.exp(scores - highest), -1, keepdims=True))
        probs_low = jnp.exp(scores - logsum).astype(jnp.bfloat16)
        context_rows = jnp.einsum(
            "shqk,skhc->sqhc", probs_low, value_heads, preferred_element_type=jnp.float32
        )
        context_rows = context_rows.reshape(seq_here, local_len, model_width).astype(jnp.bfloat16)
        residual_stream = input_rows + jnp.einsum(
            "mtg,gj->mtj", context_rows, output_weight, preferred_element_type=jnp.float32
        )
        mix_norm, normed_two, inverse_two = norm_forward(residual_stream, gain_two)
        mix_low = mix_norm.astype(jnp.bfloat16)
        mix_pos = lax.all_to_all(mix_low, "batch", split_axis=1, concat_axis=0, tiled=True)
        router_logits = jnp.einsum(
            "spd,de->spe", mix_pos, controller_weight, preferred_element_type=jnp.float32
        )
        gate_vals, gate_pull = jax.vjp(
            functools.partial(group_softmax, member=member, taking=taking), router_logits
        )
        weights_low = jnp.where(
            member[:, None, :, None],
            gate_vals.astype(jnp.bfloat16)[:, :, None, :],
            jnp.zeros((), jnp.bfloat16),
        )
        blended_rows = jnp.einsum(
            "spke,spd->pked", weights_low, mix_pos, preferred_element_type=jnp.float32
        ).astype(jnp.bfloat16)
        mixed_recv = lax.all_to_all(blended_rows, "expert", split_axis=2, concat_axis=0, tiled=True)
        pre_act = jnp.einsum(
            "pked,edf->pkef", mixed_recv, w_first, preferred_element_type=jnp.float32
        )
        activated, gelu_pull = jax.vjp(jax.nn.gelu, pre_act)
        act_low = activated.astype(jnp.bfloat16)
        expert_output = jnp.einsum(
            "pkef,efd->pked", act_low, w_second, preferred_element_type=jnp.float32
        ).astype(jnp.bfloat16)
        returned = lax.all_to_all(expert_output, "expert", split_axis=0, concat_axis=2, tiled=True)
        dispersed_rows = jnp.einsum(
            "spke,pked->spd", weights_low, returned, preferred_element_type=jnp.float32
        ).astype(jnp.bfloat16)
        spread_seq = lax.all_to_all(
            dispersed_rows, "batch", split_axis=0, concat_axis=1, tiled=True
        )
        outputs.append(residual_stream + spread_seq.astype(jnp.float32))
        cot_here = cotangent[micro_step]
        grad_spread = lax.all_to_all(
            cot_here.astype(jnp.bfloat16), "batch", split_axis=1, concat_axis=0, tiled=True
        )
        grad_weights = jnp.einsum(
            "spd,pked->spke", grad_spread, returned, preferred_element_type=jnp.float32
        )
        grad_eout = jnp.einsum(
            "spke,spd->pked", weights_low, grad_spread, preferred_element_type=jnp.float32
        ).astype(jnp.bfloat16)
        grad_eout_recv = lax.all_to_all(
            grad_eout, "expert", split_axis=2, concat_axis=0, tiled=True
        )
        grad_hidden = jnp.einsum(
            "pked,efd->pkef", grad_eout_recv, w_second, preferred_element_type=jnp.float32
        )
        step_second = jnp.einsum(
            "pkef,pked->efd", act_low, grad_eout_recv, preferred_element_type=jnp.float32
        )
        grad_pre = gelu_pull(grad_hidden)[0].astype(jnp.bfloat16)
        step_first = jnp.einsum(
            "pked,pkef->edf", mixed_recv, grad_pre, preferred_element_type=jnp.float32
        )
        sum_first = sum_first + step_first
        sum_second = sum_second + step_second
        grad_mixed = jnp.einsum(
            "pkef,edf->pked", grad_pre, w_first, preferred_element_type=jnp.float32
        ).astype(jnp.bfloat16)
        grad_mix_groups = lax.all_to_all(
            grad_mixed, "expert", split_axis=0, concat_axis=2, tiled=True
        )
        grad_weights = grad_weights + jnp.einsum(
            "pked,spd->spke", grad_mix_groups, mix_pos, preferred_element_type=jnp.float32
        )
        grad_gates = jnp.sum(jnp.where(member[:, None, :, None], grad_weights, 0.0), axis=2)
        grad_logits = gate_pull(grad_gates)[0]
        sum_ctrl = sum_ctrl + jnp.einsum(
            "spd,spe->de", mix_pos.astype(jnp.float32), grad_logits, precision=HIGH_PRECISION
        )
        grad_mix = jnp.einsum(
            "spke,pked->spd", weights_low, grad_mix_groups, preferred_element_type=jnp.float32
        )
        grad_mix = grad_mix + jnp.einsum(
            "spe,de->spd", grad_logits, ctrl_wide, precision=HIGH_PRECISION
        )
        grad_mix_seq = lax.all_to_all(
            grad_mix.astype(jnp.bfloat16), "batch", split_axis=0, concat_axis=1, tiled=True
        )
        grad_norm_two, gain_two_step = norm_backward(
            grad_mix_seq.astype(jnp.float32), normed_two, inverse_two, gain_two
        )
        sum_gain_two = sum_gain_two + gain_two_step
        grad_resid = cot_here + grad_norm_two
        attention_gradient = grad_resid.astype(jnp.bfloat16)
        sum_out = sum_out + jnp.einsum(
            "hui,huq->iq", context_rows, attention_gradient, preferred_element_type=jnp.float32
        )
        grad_context = jnp.einsum(
            "wfh,yh->wfy", attention_gradient, output_weight, preferred_element_type=jnp.float32
        ).astype(jnp.bfloat16)
        context_heads = grad_context.reshape(seq_here, local_len, HEADS, head_dim)
        probs_full = attention_probs(query_heads, key_heads, causal, logsum, factor)
        grad_probs = jnp.einsum(
            "sqhc,skhc->shqk", context_heads, value_heads, preferred_element_type=jnp.float32
        )
        row_dots = jnp.sum(grad_probs * probs_full, -1, keepdims=True)
        grad_scores = (probs_full * (grad_probs - row_dots)).astype(jnp.bfloat16)
        grad_query = (
            jnp.einsum(
                "shqk,skhc->sqhc", grad_scores, key_heads, preferred_element_type=jnp.float32
            )
            * factor
        )
        grad_query = grad_query.reshape(seq_here, local_len, model_width)
        key_terms = (
            jnp.einsum(
                "shqk,sqhc->skhc", grad_scores, query_heads, preferred_element_type=jnp.float32
            )
            * factor
        )
        value_terms = jnp.einsum(
            "shqk,sqhc->skhc",
            probs_full.astype(jnp.bfloat16),
            context_heads,
            preferred_element_type=jnp.float32,
        )
        grad_key, grad_value = (
            lax.psum_scatter(
                key_terms.reshape(seq_here, length, model_width).astype(jnp.bfloat16),
                "expert",
                scatter_dimension=1,
                tiled=True,
            ).astype(jnp.float32),
            lax.psum_scatter(
                value_terms.reshape(seq_here, length, model_width).astype(jnp.bfloat16),
                "expert",
                scatter_dimension=1,
                tiled=True,
            ).astype(jnp.float32),
        )
        query_key_value_row_gradient = jnp.concatenate(
            [grad_query, grad_key, grad_value], axis=-1
        ).astype(jnp.bfloat16)
        sum_qkv = sum_qkv + jnp.einsum(
            "hui,huq->iq",
            attention_input,
            query_key_value_row_gradient,
            preferred_element_type=jnp.float32,
        )
        grad_attn_in = jnp.einsum(
            "wfh,yh->wfy",
            query_key_value_row_gradient,
            query_key_value_weight,
            preferred_element_type=jnp.float32,
        )
        grad_norm_one, gain_one_step = norm_backward(
            grad_attn_in, normed_one, inverse_one, gain_one
        )
        sum_gain_one = sum_gain_one + gain_one_step
        grads_in.append(grad_resid + grad_norm_one)
    grad_first, grad_second = (
        lax.psum_scatter(
            sum_first.astype(jnp.bfloat16), "batch", scatter_dimension=2, tiled=True
        ).astype(jnp.float32),
        lax.psum_scatter(
            sum_second.astype(jnp.bfloat16), "batch", scatter_dimension=1, tiled=True
        ).astype(jnp.float32),
    )
    grad_qkv, grad_out, grad_ctrl, grad_gain_one, grad_gain_two = (
        lax.psum_scatter(sum_qkv, ("batch", "expert"), scatter_dimension=0, tiled=True),
        lax.psum_scatter(sum_out, ("batch", "expert"), scatter_dimension=0, tiled=True),
        lax.psum_scatter(sum_ctrl, ("batch", "expert"), scatter_dimension=0, tiled=True),
        lax.psum_scatter(sum_gain_one, ("batch", "expert"), scatter_dimension=0, tiled=True),
        lax.psum_scatter(sum_gain_two, ("batch", "expert"), scatter_dimension=0, tiled=True),
    )
    return (
        jnp.stack(outputs),
        jnp.stack(grads_in),
        grad_qkv,
        grad_out,
        grad_ctrl,
        grad_first,
        grad_second,
        grad_gain_one,
        grad_gain_two,
    )


F32 = jnp.float32
BF16 = jnp.bfloat16
PB = 16
CHUNKS = 2
VMEM_LIMIT = 60 * 1024 * 1024
KERNEL_COST = pl.CostEstimate(flops=30_000_000_000, bytes_accessed=100_000, transcendentals=0)
SMALL_COST = pl.CostEstimate(flops=1_000_000, bytes_accessed=100_000, transcendentals=0)


def dot_nn(a, b):
    return lax.dot_general(a, b, (((1,), (0,)), ((), ())), preferred_element_type=F32)


def dot_nt(a, b):
    return lax.dot_general(a, b, (((1,), (1,)), ((), ())), preferred_element_type=F32)


def dot_tn(a, b):
    return lax.dot_general(a, b, (((0,), (0,)), ((), ())), preferred_element_type=F32)


def row_norm(rows):
    centred = rows - jnp.mean(rows, -1, keepdims=True)
    inverse = lax.rsqrt(jnp.mean(centred * centred, -1, keepdims=True) + 1e-05)
    return centred * inverse, inverse


def row_norm_back(incoming, normed, inverse, gain):
    scaled = incoming * gain
    return inverse * (
        scaled
        - jnp.mean(scaled, -1, keepdims=True)
        - normed * jnp.mean(scaled * normed, -1, keepdims=True)
    )


def head_lanes(rows, lanes, head):
    lane = lax.broadcasted_iota(jnp.int32, (rows, lanes), 1)
    return (lane < lanes // 2) if head == 0 else (lane >= lanes // 2)


def causal_tile(size):
    key = lax.broadcasted_iota(jnp.int32, (size, size), 0)
    query = lax.broadcasted_iota(jnp.int32, (size, size), 1)
    return key <= query


def attention_forward_kernel(z_ref, *refs):
    quarters = 4
    parts = refs[:quarters]
    (wqkv_ref, wo_ref, g1_ref, g2_ref, x_ref, qkv_ref, lse_ref, ctx_ref, attn_ref, mix_ref, more_ref) = refs[quarters:-2]
    ctx_pairs, sems = refs[-2:]
    length, width = x_ref.shape
    pairs = HEADS // 2
    lanes = width // pairs
    half = lanes // 2
    nb = mix_ref.shape[0]
    tile = length // quarters
    factor = half ** (-0.5)
    copies = []
    for k in range(quarters):
        source = lax.rem(z_ref[0] - k + quarters, quarters)
        rows = pl.ds(pl.multiple_of(source * tile, tile), tile)
        copies.append(pltpu.make_async_copy(parts[k], x_ref.at[rows, :], sems.at[k]))
        copies[-1].start()
    for copy in copies:
        copy.wait()

    def project(i, carry):
        rows = pl.ds(pl.multiple_of(i * tile, tile), tile)
        normed, _ = row_norm(x_ref[rows, :].astype(F32))
        attn_in = (normed * g1_ref[...]).astype(BF16)
        for part in range(3):
            out = dot_nn(attn_in, wqkv_ref[:, part * width:(part + 1) * width]).astype(BF16)
            for p in range(pairs):
                qkv_ref[part * pairs + p, rows, :] = out[:, p * lanes:(p + 1) * lanes]
        return carry

    lax.fori_loop(0, quarters, project, 0, unroll=True)

    def attend(p, carry):
        values_t = qkv_ref[2 * pairs + p].T
        for j in range(quarters):
            seen = (j + 1) * tile
            queries = qkv_ref[p, j * tile:seen, :] * jnp.asarray(factor, BF16)
            outs = []
            for h in range(2):
                masked = jnp.where(head_lanes(tile, lanes, h), queries, jnp.zeros((), BF16))
                scores = dot_nt(qkv_ref[pairs + p, :seen, :], masked)
                last = jnp.where(causal_tile(tile), scores[j * tile:], NEG_FILL)
                scores = jnp.concatenate([scores[:j * tile], last], 0) if j else last
                high = jnp.max(scores, 0, keepdims=True)
                weights = jnp.exp(scores - high)
                total = jnp.sum(weights, 0, keepdims=True)
                out = dot_nn(values_t[h * half:(h + 1) * half, :seen], weights.astype(BF16))
                outs.append(out / total)
                lse_ref[2 * p + h, :, j * tile:seen] = high + jnp.log(total)
            ctx_pairs[p, j * tile:seen, :] = jnp.concatenate(outs, 0).T.astype(BF16)
        return carry

    lax.fori_loop(0, pairs, attend, 0)

    def finish(i, carry):
        rows = pl.ds(pl.multiple_of(i * tile, tile), tile)
        context = jnp.concatenate([ctx_pairs[p, rows, :] for p in range(pairs)], -1)
        ctx_ref[rows, :] = context
        attn = dot_nn(context, wo_ref[...])
        attn_ref[rows, :] = attn
        normed, _ = row_norm(x_ref[rows, :].astype(F32) + attn)
        mix = (normed * g2_ref[...]).astype(BF16)
        low = attn.astype(BF16)
        for b in range(nb):
            at = b * CHUNKS * PB
            mix_ref[b, i] = mix[at:at + PB]
            more_ref[b, 0, i] = mix[at + PB:at + 2 * PB]
            more_ref[b, 1, i] = low[at:at + PB]
            more_ref[b, 2, i] = low[at + PB:at + 2 * PB]
        return carry

    lax.fori_loop(0, quarters, finish, 0, unroll=True)


def attention_forward(z, parts, wqkv, wo, g1, g2, nb):
    quarters = len(parts)
    tile, width = parts[0].shape
    length = quarters * tile
    pairs = HEADS // 2
    lanes = width // pairs
    vmem = pl.BlockSpec(memory_space=pltpu.VMEM)
    return pl.pallas_call(
        attention_forward_kernel,
        in_specs=[pl.BlockSpec(memory_space=pltpu.SMEM)]
        + [pl.BlockSpec(memory_space=pl.ANY)] * quarters + [vmem] * 4,
        out_shape=(
            jax.ShapeDtypeStruct((length, width), BF16),
            jax.ShapeDtypeStruct((3 * pairs, length, lanes), BF16),
            jax.ShapeDtypeStruct((HEADS, 1, length), F32),
            jax.ShapeDtypeStruct((length, width), BF16),
            jax.ShapeDtypeStruct((length, width), F32),
            jax.ShapeDtypeStruct((nb, quarters, PB, width), BF16),
            jax.ShapeDtypeStruct((nb, 3, quarters, PB, width), BF16),
        ),
        scratch_shapes=[
            pltpu.VMEM((pairs, length, lanes), BF16),
            pltpu.SemaphoreType.DMA((quarters,)),
        ],
        compiler_params=pltpu.CompilerParams(vmem_limit_bytes=VMEM_LIMIT),
        cost_estimate=KERNEL_COST,
        name="attention_forward",
    )(z, *parts, wqkv, wo, g1, g2)


def attention_backward_kernel(count, *refs):
    attention_backward_body(*refs[:11], *refs[11 + count:])


def attention_backward_body(gm_ref, cot_ref, x_ref, attn_ref, ctx_ref, qkv_ref, lse_ref,
                              wqkv_ref, wo_ref, g1_ref, g2_ref,
                              gin_ref, dw_ref, dg1_ref, dg2_ref,
                              delta, ga_rows, dctx, gqkv, attn_in, dk_sum, dv_sum):
    length, width = x_ref.shape
    pairs = HEADS // 2
    lanes = width // pairs
    half = lanes // 2
    nb, _, quarters, _, _ = gm_ref.shape
    tile = length // quarters
    factor = half ** (-0.5)
    dg2_ref[...] = jnp.zeros_like(dg2_ref)
    dg1_ref[...] = jnp.zeros_like(dg1_ref)

    def first(i, carry):
        rows = pl.ds(pl.multiple_of(i * tile, tile), tile)
        normed, inverse = row_norm(x_ref[rows, :].astype(F32) + attn_ref[rows, :])
        grad = jnp.concatenate([gm_ref[b, c, i] for b in range(nb) for c in range(CHUNKS)], 0).astype(F32)
        dg2_ref[...] += jnp.sum(grad * normed, 0, keepdims=True)
        back = row_norm_back(grad, normed, inverse, g2_ref[...])
        delta[rows, :] = back
        cot = jnp.concatenate([cot_ref[b, i] for b in range(nb)], 0).astype(F32)
        grad_attn = (cot + back).astype(BF16)
        ga_rows[rows, :] = grad_attn
        grad_ctx = dot_nt(grad_attn, wo_ref[...]).astype(BF16)
        for p in range(pairs):
            dctx[p, rows, :] = grad_ctx[:, p * lanes:(p + 1) * lanes]
        return carry

    lax.fori_loop(0, quarters, first, 0, unroll=True)

    dw_ref[:, 3 * width:] = dot_tn(ctx_ref[...], ga_rows[...]).astype(BF16)

    def attend(p, carry):
        lane0 = pl.multiple_of(p * lanes, lanes)
        keys_t = qkv_ref[pairs + p].T
        dk_sum[...] = jnp.zeros_like(dk_sum)
        dv_sum[...] = jnp.zeros_like(dv_sum)
        for j in range(quarters):
            seen = (j + 1) * tile
            queries = qkv_ref[p, j * tile:seen, :] * jnp.asarray(factor, BF16)
            grads = dctx[p, j * tile:seen, :]
            context = ctx_ref[j * tile:seen, pl.ds(lane0, lanes)]
            products = (grads.astype(F32) * context.astype(F32)).T
            outs = []
            for h in range(2):
                inside = head_lanes(tile, lanes, h)
                q_masked = jnp.where(inside, queries, jnp.zeros((), BF16))
                g_masked = jnp.where(inside, grads, jnp.zeros((), BF16))
                dots = jnp.sum(products[h * half:(h + 1) * half], 0, keepdims=True)
                scores = dot_nt(qkv_ref[pairs + p, :seen, :], q_masked)
                probs = jnp.exp(scores - lse_ref[2 * p + h, :, j * tile:seen])
                last = jnp.where(causal_tile(tile), probs[j * tile:], 0.0)
                probs = jnp.concatenate([probs[:j * tile], last], 0) if j else last
                grad_probs = dot_nt(qkv_ref[2 * pairs + p, :seen, :], g_masked)
                grad_scores = (probs * (grad_probs - dots)).astype(BF16)
                dv_sum[:seen, :] += dot_nn(probs.astype(BF16), g_masked)
                dk_sum[:seen, :] += dot_nn(grad_scores, q_masked)
                outs.append(dot_nn(keys_t[h * half:(h + 1) * half, :seen], grad_scores))
            gqkv[p, j * tile:seen, :] = (jnp.concatenate(outs, 0).T * factor).astype(BF16)
        gqkv[pairs + p] = dk_sum[...].astype(BF16)
        gqkv[2 * pairs + p] = dv_sum[...].astype(BF16)
        return carry

    lax.fori_loop(0, pairs, attend, 0)

    def last(i, carry):
        rows = pl.ds(pl.multiple_of(i * tile, tile), tile)
        normed, inverse = row_norm(x_ref[rows, :].astype(F32))
        attn_in[rows, :] = (normed * g1_ref[...]).astype(BF16)
        grads = jnp.concatenate([gqkv[c, rows, :] for c in range(3 * pairs)], -1)
        grad = dot_nt(grads, wqkv_ref[...])
        dg1_ref[...] += jnp.sum(grad * normed, 0, keepdims=True)
        gin_ref[rows, :] = (delta[rows, :] + row_norm_back(grad, normed, inverse, g1_ref[...])).astype(BF16)
        return carry

    lax.fori_loop(0, quarters, last, 0, unroll=True)

    for c in range(3):
        grads = jnp.concatenate([gqkv[c * pairs + p] for p in range(pairs)], -1)
        dw_ref[:, c * width:(c + 1) * width] = dot_tn(attn_in[...], grads).astype(BF16)


def attention_backward(gm, cot, x, attn, ctx, qkv, lse, wqkv, wo, g1, g2, waits=()):
    length, width = x.shape
    pairs = HEADS // 2
    lanes = width // pairs
    return pl.pallas_call(
        functools.partial(attention_backward_kernel, len(waits)),
        in_specs=[pl.BlockSpec(memory_space=pltpu.VMEM)] * 11 + [pl.BlockSpec(memory_space=pl.ANY)] * len(waits),
        out_shape=(
            jax.ShapeDtypeStruct((length, width), BF16),
            jax.ShapeDtypeStruct((width, 4 * width), BF16),
            jax.ShapeDtypeStruct((1, width), F32),
            jax.ShapeDtypeStruct((1, width), F32),
        ),
        scratch_shapes=[
            pltpu.VMEM((length, width), F32),
            pltpu.VMEM((length, width), BF16),
            pltpu.VMEM((pairs, length, lanes), BF16),
            pltpu.VMEM((3 * pairs, length, lanes), BF16),
            pltpu.VMEM((length, width), BF16),
            pltpu.VMEM((length, lanes), F32),
            pltpu.VMEM((length, lanes), F32),
        ],
        compiler_params=pltpu.CompilerParams(vmem_limit_bytes=VMEM_LIMIT),
        cost_estimate=SMALL_COST,
        name="attention_backward",
    )(gm, cot, x, attn, ctx, qkv, lse, wqkv, wo, g1, g2, *waits)


def group_reduce(rows, mem, op, fill):
    result = jnp.zeros_like(rows)
    for k in range(mem.shape[0]):
        inside = mem[k:k + 1, :] > 0
        part = jnp.where(inside, rows, fill)
        shift = rows.shape[1] // 2
        while shift >= PB:
            part = op(part, pltpu.roll(part, shift, 1))
            shift //= 2
        result = jnp.where(inside, part, result)
    return result


def gelu_both(v):
    square = v * v
    tanh = jnp.tanh(0.7978845608028654 * v * (1.0 + 0.044715 * square))
    half = 0.5 * (1.0 + tanh)
    slope = half + v * (1.0 - tanh * tanh) * (0.3989422804014327 + 0.0535161223274472 * square)
    return v * half, slope


def start(copy):
    copy.start()


def wait(copy):
    copy.wait()


def arrivals(z, sources, sems, base, act, place):
    n = (len(sources) + 1) // 2
    act(pltpu.make_async_copy(*place(sources[0], z), sems.at[base]))
    for k in range(1, n):
        @pl.when(z >= k)
        def _():
            act(pltpu.make_async_copy(*place(sources[k], z - k), sems.at[base + k]))

        @pl.when(z + k < n)
        def _():
            act(pltpu.make_async_copy(*place(sources[n - 1 + k], z + k), sems.at[base + n - 1 + k]))


def x_rows(xs, m, q, sl):
    planes, nb, quarters, piece, width = xs.shape
    return jnp.concatenate([xs[m * sl + s, :, q].reshape(nb * piece, width) for s in range(sl)], 0)


def g_rows(gs, m, q, sl):
    quarters, nb, planes, piece, width = gs.shape
    return jnp.concatenate([gs[q, :, m * sl + s].reshape(nb * piece, width) for s in range(sl)], 0)


def mixture_forward_kernel(chunk, parts, waits, z_ref, *refs):
    x_in, refs = refs[:parts], refs[parts + waits:]
    (a_in, ctrl_ref, mem_ref, mkl_ref, take_ref, w1_ref, w2_ref,
     spread_ref, mixed_ref, hid_ref, slope_ref, eo_ref, weights_ref, gates_ref,
     xs, attn, logits, sems) = refs
    planes, nb, quarters, piece, width = xs.shape
    micro = mem_ref.shape[0]
    sl = planes // micro
    experts = mixed_ref.shape[0]
    rows = mkl_ref.shape[1]
    e = pl.program_id(0)
    z = z_ref[0]
    x_place = lambda ref, plane: (ref, xs.at[plane])
    a_copy = pltpu.make_async_copy(a_in.at[:, 1 + chunk], attn, sems.at[parts])

    @pl.when(e == 0)
    def _():
        arrivals(z, x_in, sems, 0, start, x_place)
        a_copy.start()
        arrivals(z, x_in, sems, 0, wait, x_place)
        for m in range(micro):
            for q in range(quarters):
                logits[m, q * 8:(q + 1) * 8, :] = dot_nt(ctrl_ref[...], x_rows(xs, m, q, sl))[:8]
            mem = mem_ref[m]
            taking = take_ref[m] > 0
            values = logits[m]
            high = group_reduce(jnp.where(taking, values, NEG_FILL), mem, jnp.maximum, NEG_FILL)
            scaled = jnp.where(taking, jnp.exp(values - high), 0.0)
            gates_ref[m] = scaled / group_reduce(scaled, mem, jnp.add, 0.0)
        for m in range(micro):
            for q in range(quarters):
                block = m * quarters + q
                own = gates_ref[m, q * 8:(q + 1) * 8, :]
                w = jnp.concatenate(
                    [(mkl_ref[m] * own[j:j + 1, :]).astype(BF16) for j in range(experts)], 0)
                weights_ref[block] = w
                blended = dot_nn(w, x_rows(xs, m, q, sl)).astype(BF16)
                for j in range(experts):
                    mixed_ref[j, block * rows:(block + 1) * rows, :] = blended[j * rows:(j + 1) * rows]

    value, slope = gelu_both(dot_nn(mixed_ref[e], w1_ref[0]))
    hidden = value.astype(BF16)
    hid_ref[0] = hidden
    slope_ref[0] = slope.astype(BF16)
    eo_ref[e] = dot_nn(hidden, w2_ref[0]).astype(BF16)

    @pl.when(e == experts - 1)
    def _():
        for m in range(micro):
            for q in range(quarters):
                block = m * quarters + q
                outs = jnp.concatenate(
                    [eo_ref[j, block * rows:(block + 1) * rows, :] for j in range(experts)], 0)
                spread = dot_tn(weights_ref[block], outs).astype(BF16)
                for s in range(sl):
                    at = slice(s * nb * PB, (s + 1) * nb * PB)
                    spread_ref[q, :, m * sl + s] = spread[at].reshape(nb, PB, width)
        a_copy.wait()
        for q in range(quarters):
            spread_ref[q, :, z] = (spread_ref[q, :, z].astype(F32) + attn[:, q].astype(F32)).astype(BF16)


def mixture_backward_kernel(chunk, parts, waits, z_ref, *refs):
    x_in, g_in, refs = refs[:parts], refs[parts:2 * parts], refs[2 * parts + waits:]
    (ctrl_ref, mem_ref, mkl_ref, weights_ref, gates_ref, eo_ref, slope_ref, w1_ref, w2_ref,
     gm_ref, geo_ref, gpre_ref, dctrl_ref, xs, gs, gmx, sems) = refs
    planes, nb, quarters, piece, width = xs.shape
    micro, _, lanes = mem_ref.shape
    sl = planes // micro
    experts = geo_ref.shape[0]
    rows = mkl_ref.shape[1]
    e = pl.program_id(0)
    z = z_ref[0]
    mine = pl.ds(chunk * PB, PB)
    x_place = lambda ref, plane: (ref, xs.at[plane])
    g_place = lambda ref, plane: (ref.at[:, :, mine, :], gs.at[plane])

    @pl.when(e == 0)
    def _():
        arrivals(z, g_in, sems, 0, start, g_place)
        arrivals(z, x_in, sems, parts, start, x_place)
        arrivals(z, g_in, sems, 0, wait, g_place)
        for m in range(micro):
            for q in range(quarters):
                block = m * quarters + q
                grads = dot_nn(weights_ref[block], g_rows(gs, m, q, sl)).astype(BF16)
                for j in range(experts):
                    geo_ref[j, block * rows:(block + 1) * rows, :] = grads[j * rows:(j + 1) * rows]
        arrivals(z, x_in, sems, parts, wait, x_place)

    grad_pre = (dot_nt(geo_ref[e], w2_ref[0]) * slope_ref[0].astype(F32)).astype(BF16)
    gpre_ref[0] = grad_pre
    gmx[e] = dot_nt(grad_pre, w1_ref[0]).astype(BF16)

    @pl.when(e == experts - 1)
    def _():
        dctrl = jnp.zeros(dctrl_ref.shape, F32)
        ctrl8 = ctrl_ref[:8, :].astype(F32)
        ctrl_twice = jnp.concatenate([ctrl8, ctrl8], 0).astype(BF16)
        for m in range(micro):
            for q in range(quarters):
                block = m * quarters + q
                at = slice(block * rows, (block + 1) * rows)
                outs = jnp.concatenate([eo_ref[j, at, :] for j in range(experts)], 0)
                backs = jnp.concatenate([gmx[j, at, :] for j in range(experts)], 0)
                w = weights_ref[block]
                inputs = x_rows(xs, m, q, sl)
                dots = dot_nt(outs, g_rows(gs, m, q, sl)) + dot_nt(backs, inputs)
                grad_gates = [
                    jnp.sum(dots[j * rows:(j + 1) * rows] * mkl_ref[m], 0, keepdims=True)
                    for j in range(experts)]
                if experts < 8:
                    grad_gates.append(jnp.zeros((8 - experts, lanes), F32))
                grad_gates = jnp.concatenate(grad_gates, 0)
                own = gates_ref[m, q * 8:(q + 1) * 8, :]
                inner = group_reduce(own * grad_gates, mem_ref[m], jnp.add, 0.0)
                grad_logits = own * (grad_gates - inner)
                upper = grad_logits.astype(BF16).astype(F32)
                both = jnp.concatenate([upper, grad_logits - upper], 0).astype(BF16)
                grad_mix = (dot_tn(w, backs) + dot_tn(both, ctrl_twice)).astype(BF16)
                for s in range(sl):
                    part = slice(s * nb * PB, (s + 1) * nb * PB)
                    gm_ref[m * sl + s, :, q] = grad_mix[part].reshape(nb, PB, width)
                dctrl += dot_nn(both, inputs)
        dctrl_ref[...] = dctrl


def whole(shape):
    return pl.BlockSpec(shape, lambda e: (0,) * len(shape))


def by_expert(shape):
    return pl.BlockSpec((1,) + shape[1:], lambda e: (e, 0, 0))


def mixture_sizes(x_parts, mem, mkl, w1):
    nb, quarters, piece, width = x_parts[0].shape
    planes = quarters
    experts, _, hidden_size = w1.shape
    total = mem.shape[0] * quarters * mkl.shape[1]
    back = (planes, nb, quarters, piece, width)
    return back, (experts, total, width), (experts, total, hidden_size)


def mixture_forward(chunk, z, x_parts, a_all, ctrl, mem, mkl, take, w1, w2, waits=()):
    back, narrow, wide = mixture_sizes(x_parts, mem, mkl, w1)
    micro, _, lanes = mem.shape
    quarters = back[2]
    weights = (micro * quarters, narrow[0] * mkl.shape[1], lanes)
    gates = (micro, quarters * 8, lanes)
    any_spec = pl.BlockSpec(memory_space=pl.ANY)
    return pl.pallas_call(
        functools.partial(mixture_forward_kernel, chunk, len(x_parts), len(waits)),
        grid=(narrow[0],),
        out_shape=(
            jax.ShapeDtypeStruct(back, BF16),
            jax.ShapeDtypeStruct(narrow, BF16),
            jax.ShapeDtypeStruct(wide, BF16),
            jax.ShapeDtypeStruct(wide, BF16),
            jax.ShapeDtypeStruct(narrow, BF16),
            jax.ShapeDtypeStruct(weights, BF16),
            jax.ShapeDtypeStruct(gates, F32),
        ),
        in_specs=[pl.BlockSpec(memory_space=pltpu.SMEM)]
        + [any_spec] * (len(x_parts) + len(waits) + 1)
        + [whole(ctrl.shape), whole(mem.shape), whole(mkl.shape), whole(take.shape),
           by_expert(w1.shape), by_expert(w2.shape)],
        out_specs=(whole(back), whole(narrow), by_expert(wide), by_expert(wide),
                   whole(narrow), whole(weights), whole(gates)),
        scratch_shapes=[
            pltpu.VMEM(back, BF16),
            pltpu.VMEM(back[1:], BF16),
            pltpu.VMEM(gates, F32),
            pltpu.SemaphoreType.DMA((len(x_parts) + 1,)),
        ],
        compiler_params=pltpu.CompilerParams(vmem_limit_bytes=VMEM_LIMIT),
        cost_estimate=KERNEL_COST,
        name="mixture_forward",
    )(z, *x_parts, *waits, a_all, ctrl, mem, mkl, take, w1, w2)


def mixture_backward(chunk, z, x_parts, g_parts, ctrl, mem, mkl, weights, gates, eo, slope, w1, w2, waits=()):
    back, narrow, wide = mixture_sizes(x_parts, mem, mkl, w1)
    parts = len(x_parts)
    any_spec = pl.BlockSpec(memory_space=pl.ANY)
    return pl.pallas_call(
        functools.partial(mixture_backward_kernel, chunk, parts, len(waits)),
        grid=(narrow[0],),
        out_shape=(
            jax.ShapeDtypeStruct(back, BF16),
            jax.ShapeDtypeStruct(narrow, BF16),
            jax.ShapeDtypeStruct(wide, BF16),
            jax.ShapeDtypeStruct((16, back[4]), F32),
        ),
        in_specs=[pl.BlockSpec(memory_space=pltpu.SMEM)]
        + [any_spec] * (2 * parts + len(waits))
        + [whole(ctrl.shape), whole(mem.shape), whole(mkl.shape), whole(weights.shape),
           whole(gates.shape), whole(narrow), by_expert(wide), by_expert(w1.shape), by_expert(w2.shape)],
        out_specs=(whole(back), whole(narrow), by_expert(wide), whole((16, back[4]))),
        scratch_shapes=[
            pltpu.VMEM(back, BF16),
            pltpu.VMEM(back, BF16),
            pltpu.VMEM(narrow, BF16),
            pltpu.SemaphoreType.DMA((2 * parts,)),
        ],
        compiler_params=pltpu.CompilerParams(vmem_limit_bytes=VMEM_LIMIT),
        cost_estimate=KERNEL_COST,
        name="mixture_backward",
    )(z, *x_parts, *g_parts, *waits, ctrl, mem, mkl, weights, gates, eo, slope, w1, w2)


def own_cotangent_kernel(parts, z_ref, *refs):
    g_in, (cot_ref, sems) = refs[:parts], refs[-2:]
    z = z_ref[0]
    place = lambda ref, plane: (ref.at[:, z], cot_ref.at[:, plane])
    arrivals(z, g_in, sems, 0, start, place)
    arrivals(z, g_in, sems, 0, wait, place)


def own_cotangent(z, g_parts, waits=()):
    nb, planes, piece, width = g_parts[0].shape
    any_spec = pl.BlockSpec(memory_space=pl.ANY)
    return pl.pallas_call(
        functools.partial(own_cotangent_kernel, len(g_parts)),
        out_shape=jax.ShapeDtypeStruct((nb, planes, piece, width), BF16),
        in_specs=[pl.BlockSpec(memory_space=pltpu.SMEM)] + [any_spec] * (len(g_parts) + len(waits)),
        scratch_shapes=[pltpu.SemaphoreType.DMA((len(g_parts),))],
        cost_estimate=SMALL_COST,
        compiler_params=pltpu.CompilerParams(vmem_limit_bytes=VMEM_LIMIT),
        name="own_cotangent",
    )(z, *g_parts, *waits)


def weight_grads_kernel(z_ref, m0, m1, p0, p1, h0, h1, o0, o1, *refs):
    keep_ref, send_ref = refs[-2:]
    width, step = keep_ref.shape[-2:]
    crossed = pl.program_id(0) >= pl.num_programs(0) // 2
    core = lax.rem(z_ref[1], 2)
    left1 = m0[0].T, m1[0].T
    left2 = o0[0].T, o1[0].T
    for t in range(p0.shape[2] // step // 2):
        x, y = t % 2, t // 2
        hop1, hop2 = jnp.where(crossed, y, x), jnp.where(crossed, x, y)
        for ref, part in ((keep_ref, core), (send_ref, 1 - core)):
            at = pl.ds(pl.multiple_of((2 * t + part) * step, step), step)
            first = dot_nn(left1[0], p0[0, :, at]) + dot_nn(left1[1], p1[0, :, at])
            ref[0, 0, hop1, hop2, 0] = first.astype(BF16)
            second = dot_nn(left2[0], h0[0, :, at]) + dot_nn(left2[1], h1[0, :, at])
            ref[0, 0, hop1, hop2, 1] = second.astype(BF16)


def weight_grads(z, mixed, gpre, hid, geo, nb, waits=()):
    experts, total, width = mixed[0].shape
    hidden_size = gpre[0].shape[2]
    step = hidden_size // nb
    half = experts // 2
    row = pl.BlockSpec((1, total, width), lambda e: (e, 0, 0))
    wide = pl.BlockSpec((1, total, hidden_size), lambda e: (e, 0, 0))
    out = pl.BlockSpec((1, 1, 2, 2, 2, width, step), lambda e: (e // half, e % half, 0, 0, 0, 0, 0))
    return pl.pallas_call(
        weight_grads_kernel,
        grid=(experts,),
        in_specs=[pl.BlockSpec(memory_space=pltpu.SMEM)]
        + [row] * 2 + [wide] * 4 + [row] * 2 + [pl.BlockSpec(memory_space=pl.ANY)] * len(waits),
        out_shape=(jax.ShapeDtypeStruct((2, half, 2, 2, 2, width, step), BF16),) * 2,
        out_specs=(out, out),
        compiler_params=pltpu.CompilerParams(vmem_limit_bytes=VMEM_LIMIT),
        cost_estimate=SMALL_COST,
        name="weight_grads",
    )(z, *mixed, *gpre, *hid, *geo, *waits)


def pick(parts, index):
    return lax.dynamic_index_in_dim(parts, index, 0, keepdims=False)


def pass_on(*refs):
    pass


def after(value, *others):
    spec = pl.BlockSpec(memory_space=pl.ANY)
    return pl.pallas_call(
        pass_on,
        out_shape=jax.ShapeDtypeStruct(value.shape, value.dtype),
        in_specs=[spec] * (1 + len(others)),
        out_specs=spec,
        input_output_aliases={0: 0},
        name="after",
        cost_estimate=SMALL_COST,
    )(value, *others)


def line_step(ups, downs, count):
    up = [(i, i + 1) for i in range(count - 1)]
    down = [(i + 1, i) for i in range(count - 1)]
    return (ups + [lax.ppermute(ups[-1], "expert", up)],
            downs + [lax.ppermute(downs[-1], "expert", down)])


def line_scatter(parts, z, count):
    up = [(i, i + 1) for i in range(count - 1)]
    down = [(i + 1, i) for i in range(count - 1)]

    def own(index):
        return pick(parts, jnp.clip(index, 0, count - 1)).astype(F32)

    rising, falling = own(z + count - 1).astype(BF16), own(z - count + 1).astype(BF16)
    for step in range(1, count):
        rising = lax.ppermute(rising, "expert", up).astype(F32)
        falling = lax.ppermute(falling, "expert", down).astype(F32)
        if step < count - 1:
            rising = (rising + own(z + count - 1 - step)).astype(BF16)
            falling = (falling + own(z - count + 1 + step)).astype(BF16)
    return (rising + falling + own(z)).astype(BF16)


def to_planes(parts, z, count):
    got = [pick(parts, z)]
    for k in range(1, count):
        part = pick(parts, lax.rem(z + k, count))
        got.append(lax.ppermute(part, "expert", [(i, (i + k) % count) for i in range(count)]))
    return got


def swap_halves(blocks, bit, count):
    mine = lax.rem(lax.axis_index("batch") >> bit, 2)
    other = lax.ppermute(pick(blocks, 1 - mine), "batch", [(i, i ^ (1 << bit)) for i in range(count)])
    return (pick(blocks, mine).astype(F32) + other.astype(F32)).astype(BF16)


def first_halves(keep, came):
    own = lax.axis_index("batch")
    mine = [lax.rem(own >> bit, 2) for bit in (1, 2)]

    def part(half, expert, index):
        return (pick(keep[half, expert], index).astype(F32) + pick(came[half, expert], index).astype(F32)).astype(BF16)

    experts = range(keep.shape[1])
    return ([[part(i, e, mine[i]) for e in experts] for i in range(2)],
            [[part(i, e, 1 - mine[i]) for e in experts] for i in range(2)])


def hop(keep, send, bit):
    came = lax.ppermute(send, "batch", [(j, j ^ (1 << bit)) for j in range(8)])
    return (keep.astype(F32) + came.astype(F32)).astype(BF16)


def second_hop(held):
    both = [swap_halves(part, 2 - i, 8) for i in range(2) for part in held[i]]
    both = jnp.stack(both).astype(F32)
    return both[:, 0], both[:, 1].transpose(0, 2, 1)


def body(
    tokens,
    cotangent,
    query_key_value_weight,
    output_weight,
    controller_weight,
    w_first,
    w_second,
    gain_one,
    gain_two,
    group_sizes,
    live,
):
    micro, sl, local_len, width = tokens.shape
    planes = lax.axis_size("expert")
    nb = lax.axis_size("batch")
    experts = w_first.shape[0]
    seqs = live.shape[1]
    z = lax.axis_index("expert")
    piece = local_len // nb
    if micro * sl != planes or piece != CHUNKS * PB or nb != 8:
        return body_by_position(
            tokens, cotangent, query_key_value_weight, output_weight, controller_weight,
            w_first, w_second, gain_one, gain_two, group_sizes, live)
    g1, g2 = gain_one.reshape(1, width), gain_two.reshape(1, width)

    own = lax.axis_index("batch")
    z_arr = jnp.stack([z, own]).astype(jnp.int32)
    x_parts = to_planes(tokens.reshape(planes, local_len, width).astype(BF16), z, planes)

    cot = cotangent.reshape(planes, nb, piece, width)
    pieces = []
    for k in range(nb):
        part = lax.dynamic_index_in_dim(cot, own ^ k, 1, keepdims=False).astype(BF16)
        if k:
            part = lax.ppermute(part, "batch", [(i, i ^ k) for i in range(nb)])
        pieces.append(part)
    pieces[1] = after(pieces[1], *x_parts[1:])
    cot = jnp.take(jnp.stack(pieces), own ^ jnp.arange(nb), axis=0)
    g_up, g_down = line_step([cot], [cot], planes)

    x, qkv, lse, ctx, attn, mix, more = attention_forward(
        z_arr, x_parts, query_key_value_weight, output_weight, g1, g2, nb)

    member, taking = jax.vmap(group_tables)(group_sizes, live)
    groups = member.shape[2]
    mem = member.reshape(micro, nb, sl, groups).transpose(0, 3, 2, 1).reshape(micro, groups, seqs)
    mem = jnp.repeat(mem.astype(F32), PB, axis=2)
    take = taking.reshape(micro, nb, sl).transpose(0, 2, 1).reshape(micro, 1, seqs)
    take = jnp.repeat(take.astype(F32), PB, axis=2)
    place = jnp.arange(seqs * PB, dtype=jnp.int32) % PB
    same = (jnp.arange(PB, dtype=jnp.int32)[:, None] == place[None, :]).astype(F32)
    mkl = (mem[:, :, None, :] * same).reshape(micro, groups * PB, seqs * PB)
    ctrl = lax.dynamic_slice_in_dim(controller_weight, z * experts, experts, 1).T
    ctrl = jnp.pad(ctrl, ((0, 16 - experts), (0, 0)))

    def over_batch(block):
        return lax.all_to_all(block, "batch", split_axis=0, concat_axis=0, tiled=True)

    def over_expert(blocks):
        return lax.all_to_all(blocks, "expert", split_axis=0, concat_axis=0, tiled=True)

    own0 = over_batch(after(mix, g_up[1], g_down[1]))
    g_up, g_down = line_step(g_up, g_down, planes)
    up0, down0 = line_step([own0], [own0], planes)
    more = over_batch(after(more, own0))
    own1 = more[:, 0]
    up1, down1 = line_step([own1], [own1], planes)
    up0, down0 = line_step(up0, down0, planes)
    up0[-1] = after(up0[-1], up1[-1], down1[-1])
    g_up[-1] = after(g_up[-1], up0[-2], down0[-2])
    g_up, g_down = line_step(g_up, g_down, planes)
    up0, down0 = line_step(up0, down0, planes)
    up1, down1 = line_step(up1, down1, planes)
    second = up1[-1], down1[-1]
    up1, down1 = line_step(up1, down1, planes)
    g_parts = g_up + g_down[1:]
    x0, x1 = up0 + down0[1:], up1 + down1[1:]

    spread0, mixed0, hid0, slope0, eo0, weights0, gates0 = mixture_forward(
        0, z_arr, x0, more, ctrl, mem, mkl, take, w_first, w_second)
    cot_picked = own_cotangent(z_arr, g_parts, waits=(eo0,) + second)
    spread0 = lax.psum_scatter(after(spread0, cot_picked), "expert", scatter_dimension=0, tiled=False)
    cot_own = over_batch(cot_picked)
    back0, geo0, gpre0, dctrl0 = mixture_backward(
        0, z_arr, x0, g_parts, ctrl, mem, mkl, weights0, gates0, eo0, slope0, w_first, w_second,
        waits=(cot_picked,))
    back0 = over_expert(after(back0, cot_own, up1[-1], down1[-1]))
    spread1, mixed1, hid1, slope1, eo1, weights1, gates1 = mixture_forward(
        1, z_arr, x1, more, ctrl, mem, mkl, take, w_first, w_second, waits=(dctrl0, spread0))
    back1, geo1, gpre1, dctrl1 = mixture_backward(
        1, z_arr, x1, g_parts, ctrl, mem, mkl, weights1, gates1, eo1, slope1, w_first, w_second)
    back0 = after(back0, dctrl1)
    back1 = after(back1, back0)
    dctrl = dctrl0[:8] + dctrl0[8:] + dctrl1[:8] + dctrl1[8:]
    keep, send = weight_grads(
        z_arr, (mixed0, mixed1), (gpre0, gpre1), (hid0, hid1), (geo0, geo1), nb, waits=(back1,))
    back1 = after(over_expert(back1), send)
    spread1 = lax.psum_scatter(after(spread1, back1), "expert", scatter_dimension=0, tiled=False)
    back = jnp.stack([back0, back1], 2)
    back = jnp.sum(back.astype(F32), 0).astype(BF16)
    back = over_batch(back)
    came = lax.ppermute(after(send, back1), "batch", [(i, i ^ 1) for i in range(nb)])
    keeps, sends = first_halves(keep, came)

    gin, dw, dg1, dg2 = attention_backward(
        back, cot_own, x, attn, ctx, qkv, lse, query_key_value_weight, output_weight, g1, g2,
        waits=tuple(sends[0] + sends[1]))
    held = [[hop(keeps[i][e], sends[i][e], 1 + i) for e in range(len(sends[i]))] for i in range(2)]
    gin = after(gin, held[0][0], held[1][0])
    dw = after(dw, held[0][0], held[1][0])
    grad_first, grad_second = second_hop(held)

    got = jnp.stack(to_planes(gin.reshape(planes, local_len, width), z, planes))
    gin = jnp.take(got, lax.rem(z - jnp.arange(planes) + planes, planes), axis=0)
    grad_in = cotangent + gin.reshape(tokens.shape).astype(F32)

    dctrl_all = jnp.zeros((planes, experts, width), F32)
    dctrl_all = lax.dynamic_update_slice(dctrl_all, dctrl[None, :experts], (z, 0, 0))
    dctrl_all = dctrl_all.reshape(planes * experts, width).T
    extra = jnp.concatenate([dctrl_all, dg1.T, dg2.T], 1)
    extra = jnp.pad(extra, ((0, 0), (0, 128 - extra.shape[1]))).astype(BF16)
    flat = jnp.concatenate([dw, extra], 1)
    flat = flat.reshape(nb // 2, 2, -1, flat.shape[1]).transpose(1, 0, 2, 3)
    flat = swap_halves(flat, 0, nb)
    chips = [[c + 2 * i for i in range(nb // 2)] for c in range(2)]
    flat = lax.all_to_all(flat, "batch", split_axis=0, concat_axis=0, tiled=True, axis_index_groups=chips)
    flat = jnp.sum(flat.astype(F32), 0).astype(BF16)
    spread = jnp.stack([after(spread0, flat), spread1], 1)
    spread = over_batch(spread)
    out = tokens + spread.transpose(2, 0, 1, 3, 4).reshape(tokens.shape).astype(F32)
    flat = flat.reshape(planes, -1, flat.shape[1])
    flat = lax.all_to_all(flat, "expert", split_axis=0, concat_axis=0, tiled=True)
    flat = jnp.sum(flat.astype(F32), 0)
    ends = [3 * width, 4 * width, 4 * width + planes * experts]
    grad_qkv, grad_out, grad_ctrl = flat[:, :ends[0]], flat[:, ends[0]:ends[1]], flat[:, ends[1]:ends[2]]
    return (out, grad_in, grad_qkv, grad_out, grad_ctrl, grad_first, grad_second,
            flat[:, ends[2]], flat[:, ends[2] + 1])


def solution(mesh):
    placed = (
        P(None, "batch", "expert", None),
        P(None, "batch", "expert", None),
        P(),
        P(),
        P(),
        P("expert", None, None),
        P("expert", None, None),
        P(),
        P(),
        P(),
        P(),
    )
    return jax.shard_map(
        body,
        mesh=mesh,
        in_specs=placed,
        out_specs=(
            P(None, "batch", "expert", None),
            P(None, "batch", "expert", None),
            P(("batch", "expert"), None),
            P(("batch", "expert"), None),
            P(("batch", "expert"), None),
            P("expert", None, "batch"),
            P("expert", "batch", None),
            P(("batch", "expert")),
            P(("batch", "expert")),
        ),
        check_vma=False,
    )
```

```python
import functools

import jax
import jax.numpy as jnp
from jax import lax
from jax.experimental import pallas as pl
from jax.experimental.pallas import tpu as pltpu
from jax.sharding import PartitionSpec as P

HEADS = 8


HIGH_PRECISION = lax.Precision.HIGHEST
NEG_FILL = -1e30


def group_tables(group_row, live_row):
    seq_count = live_row.shape[0]
    group_ends = jnp.cumsum(group_row)
    group_starts = group_ends - group_row
    numbers = jnp.arange(seq_count, dtype=jnp.int32)
    member = (numbers[:, None] >= group_starts[None, :]) & (numbers[:, None] < group_ends[None, :])
    leading = jnp.any(numbers[:, None] == group_starts[None, :], axis=1)
    taking = (live_row > 0) | leading
    return (member, taking)


def group_softmax(router_logits, member, taking):
    inside = member[:, :, None, None]
    masked = jnp.where(taking[:, None, None], router_logits, NEG_FILL)
    highest = jnp.max(jnp.where(inside, masked[:, None], NEG_FILL), axis=0)
    row_high = jnp.sum(jnp.where(inside, highest[None], 0.0), axis=1)
    scaled = jnp.where(taking[:, None, None], jnp.exp(router_logits - row_high), 0.0)
    group_sums = jnp.sum(jnp.where(inside, scaled[:, None], 0.0), axis=0)
    row_sums = jnp.sum(jnp.where(inside, group_sums[None], 0.0), axis=1)
    return scaled / row_sums


def norm_forward(values_in, scaling):
    centred = values_in - jnp.mean(values_in, -1, keepdims=True)
    inverse = lax.rsqrt(jnp.mean(centred * centred, -1, keepdims=True) + 1e-05)
    normed = centred * inverse
    return (normed * scaling, normed, inverse)


def norm_backward(incoming, normed, inverse, scaling):
    scaled_grad = incoming * scaling
    returned_grad = inverse * (
        scaled_grad
        - jnp.mean(scaled_grad, -1, keepdims=True)
        - normed * jnp.mean(scaled_grad * normed, -1, keepdims=True)
    )
    return (returned_grad, jnp.sum(incoming * normed, axis=(0, 1)))


def attention_probs(query_heads, key_heads, causal, logsum, factor):
    scores = (
        jnp.einsum("sqhc,skhc->shqk", query_heads, key_heads, preferred_element_type=jnp.float32)
        * factor
    )
    return jnp.where(causal, jnp.exp(scores - logsum), 0.0)


def body_by_position(
    tokens,
    cotangent,
    query_key_value_weight,
    output_weight,
    controller_weight,
    w_first,
    w_second,
    gain_one,
    gain_two,
    group_sizes,
    live,
):
    micro_count, seq_here, local_len, model_width = tokens.shape
    head_dim = model_width // HEADS
    factor = head_dim ** (-0.5)
    length = local_len * lax.axis_size("expert")
    query_pos = lax.axis_index("expert") * local_len + jnp.arange(local_len, dtype=jnp.int32)
    key_pos = jnp.arange(length, dtype=jnp.int32)
    causal = key_pos[None, :] <= query_pos[:, None]
    ctrl_wide = controller_weight.astype(jnp.float32)
    sum_first = jnp.zeros(w_first.shape, jnp.float32)
    sum_second = jnp.zeros(w_second.shape, jnp.float32)
    sum_qkv = jnp.zeros(query_key_value_weight.shape, jnp.float32)
    sum_out = jnp.zeros(output_weight.shape, jnp.float32)
    sum_ctrl = jnp.zeros(controller_weight.shape, jnp.float32)
    sum_gain_one = jnp.zeros(gain_one.shape, jnp.float32)
    sum_gain_two = jnp.zeros(gain_two.shape, jnp.float32)
    outputs = []
    grads_in = []
    for micro_step in range(micro_count):
        member, taking = group_tables(group_sizes[micro_step], live[micro_step])
        input_rows = tokens[micro_step]
        attn_norm, normed_one, inverse_one = norm_forward(input_rows, gain_one)
        attention_input = attn_norm.astype(jnp.bfloat16)
        projected_rows = jnp.einsum(
            "mtg,gj->mtj",
            attention_input,
            query_key_value_weight,
            preferred_element_type=jnp.float32,
        ).astype(jnp.bfloat16)
        queries = projected_rows[..., :model_width]
        keys_here = projected_rows[..., model_width : 2 * model_width]
        values_here = projected_rows[..., 2 * model_width :]
        keys_all, values_all = (
            lax.all_gather(keys_here, "expert", axis=1, tiled=True),
            lax.all_gather(values_here, "expert", axis=1, tiled=True),
        )
        query_heads = queries.reshape(seq_here, local_len, HEADS, head_dim)
        key_heads = keys_all.reshape(seq_here, length, HEADS, head_dim)
        value_heads = values_all.reshape(seq_here, length, HEADS, head_dim)
        scores = (
            jnp.einsum(
                "sqhc,skhc->shqk", query_heads, key_heads, preferred_element_type=jnp.float32
            )
            * factor
        )
        scores = jnp.where(causal, scores, NEG_FILL)
        highest = jnp.max(scores, -1, keepdims=True)
        logsum = highest + jnp.log(jnp.sum(jnp.exp(scores - highest), -1, keepdims=True))
        probs_low = jnp.exp(scores - logsum).astype(jnp.bfloat16)
        context_rows = jnp.einsum(
            "shqk,skhc->sqhc", probs_low, value_heads, preferred_element_type=jnp.float32
        )
        context_rows = context_rows.reshape(seq_here, local_len, model_width).astype(jnp.bfloat16)
        residual_stream = input_rows + jnp.einsum(
            "mtg,gj->mtj", context_rows, output_weight, preferred_element_type=jnp.float32
        )
        mix_norm, normed_two, inverse_two = norm_forward(residual_stream, gain_two)
        mix_low = mix_norm.astype(jnp.bfloat16)
        mix_pos = lax.all_to_all(mix_low, "batch", split_axis=1, concat_axis=0, tiled=True)
        router_logits = jnp.einsum(
            "spd,de->spe", mix_pos, controller_weight, preferred_element_type=jnp.float32
        )
        gate_vals, gate_pull = jax.vjp(
            functools.partial(group_softmax, member=member, taking=taking), router_logits
        )
        weights_low = jnp.where(
            member[:, None, :, None],
            gate_vals.astype(jnp.bfloat16)[:, :, None, :],
            jnp.zeros((), jnp.bfloat16),
        )
        blended_rows = jnp.einsum(
            "spke,spd->pked", weights_low, mix_pos, preferred_element_type=jnp.float32
        ).astype(jnp.bfloat16)
        mixed_recv = lax.all_to_all(blended_rows, "expert", split_axis=2, concat_axis=0, tiled=True)
        pre_act = jnp.einsum(
            "pked,edf->pkef", mixed_recv, w_first, preferred_element_type=jnp.float32
        )
        activated, gelu_pull = jax.vjp(jax.nn.gelu, pre_act)
        act_low = activated.astype(jnp.bfloat16)
        expert_output = jnp.einsum(
            "pkef,efd->pked", act_low, w_second, preferred_element_type=jnp.float32
        ).astype(jnp.bfloat16)
        returned = lax.all_to_all(expert_output, "expert", split_axis=0, concat_axis=2, tiled=True)
        dispersed_rows = jnp.einsum(
            "spke,pked->spd", weights_low, returned, preferred_element_type=jnp.float32
        ).astype(jnp.bfloat16)
        spread_seq = lax.all_to_all(
            dispersed_rows, "batch", split_axis=0, concat_axis=1, tiled=True
        )
        outputs.append(residual_stream + spread_seq.astype(jnp.float32))
        cot_here = cotangent[micro_step]
        grad_spread = lax.all_to_all(
            cot_here.astype(jnp.bfloat16), "batch", split_axis=1, concat_axis=0, tiled=True
        )
        grad_weights = jnp.einsum(
            "spd,pked->spke", grad_spread, returned, preferred_element_type=jnp.float32
        )
        grad_eout = jnp.einsum(
            "spke,spd->pked", weights_low, grad_spread, preferred_element_type=jnp.float32
        ).astype(jnp.bfloat16)
        grad_eout_recv = lax.all_to_all(
            grad_eout, "expert", split_axis=2, concat_axis=0, tiled=True
        )
        grad_hidden = jnp.einsum(
            "pked,efd->pkef", grad_eout_recv, w_second, preferred_element_type=jnp.float32
        )
        step_second = jnp.einsum(
            "pkef,pked->efd", act_low, grad_eout_recv, preferred_element_type=jnp.float32
        )
        grad_pre = gelu_pull(grad_hidden)[0].astype(jnp.bfloat16)
        step_first = jnp.einsum(
            "pked,pkef->edf", mixed_recv, grad_pre, preferred_element_type=jnp.float32
        )
        sum_first = sum_first + step_first
        sum_second = sum_second + step_second
        grad_mixed = jnp.einsum(
            "pkef,edf->pked", grad_pre, w_first, preferred_element_type=jnp.float32
        ).astype(jnp.bfloat16)
        grad_mix_groups = lax.all_to_all(
            grad_mixed, "expert", split_axis=0, concat_axis=2, tiled=True
        )
        grad_weights = grad_weights + jnp.einsum(
            "pked,spd->spke", grad_mix_groups, mix_pos, preferred_element_type=jnp.float32
        )
        grad_gates = jnp.sum(jnp.where(member[:, None, :, None], grad_weights, 0.0), axis=2)
        grad_logits = gate_pull(grad_gates)[0]
        sum_ctrl = sum_ctrl + jnp.einsum(
            "spd,spe->de", mix_pos.astype(jnp.float32), grad_logits, precision=HIGH_PRECISION
        )
        grad_mix = jnp.einsum(
            "spke,pked->spd", weights_low, grad_mix_groups, preferred_element_type=jnp.float32
        )
        grad_mix = grad_mix + jnp.einsum(
            "spe,de->spd", grad_logits, ctrl_wide, precision=HIGH_PRECISION
        )
        grad_mix_seq = lax.all_to_all(
            grad_mix.astype(jnp.bfloat16), "batch", split_axis=0, concat_axis=1, tiled=True
        )
        grad_norm_two, gain_two_step = norm_backward(
            grad_mix_seq.astype(jnp.float32), normed_two, inverse_two, gain_two
        )
        sum_gain_two = sum_gain_two + gain_two_step
        grad_resid = cot_here + grad_norm_two
        attention_gradient = grad_resid.astype(jnp.bfloat16)
        sum_out = sum_out + jnp.einsum(
            "hui,huq->iq", context_rows, attention_gradient, preferred_element_type=jnp.float32
        )
        grad_context = jnp.einsum(
            "wfh,yh->wfy", attention_gradient, output_weight, preferred_element_type=jnp.float32
        ).astype(jnp.bfloat16)
        context_heads = grad_context.reshape(seq_here, local_len, HEADS, head_dim)
        probs_full = attention_probs(query_heads, key_heads, causal, logsum, factor)
        grad_probs = jnp.einsum(
            "sqhc,skhc->shqk", context_heads, value_heads, preferred_element_type=jnp.float32
        )
        row_dots = jnp.sum(grad_probs * probs_full, -1, keepdims=True)
        grad_scores = (probs_full * (grad_probs - row_dots)).astype(jnp.bfloat16)
        grad_query = (
            jnp.einsum(
                "shqk,skhc->sqhc", grad_scores, key_heads, preferred_element_type=jnp.float32
            )
            * factor
        )
        grad_query = grad_query.reshape(seq_here, local_len, model_width)
        key_terms = (
            jnp.einsum(
                "shqk,sqhc->skhc", grad_scores, query_heads, preferred_element_type=jnp.float32
            )
            * factor
        )
        value_terms = jnp.einsum(
            "shqk,sqhc->skhc",
            probs_full.astype(jnp.bfloat16),
            context_heads,
            preferred_element_type=jnp.float32,
        )
        grad_key, grad_value = (
            lax.psum_scatter(
                key_terms.reshape(seq_here, length, model_width).astype(jnp.bfloat16),
                "expert",
                scatter_dimension=1,
                tiled=True,
            ).astype(jnp.float32),
            lax.psum_scatter(
                value_terms.reshape(seq_here, length, model_width).astype(jnp.bfloat16),
                "expert",
                scatter_dimension=1,
                tiled=True,
            ).astype(jnp.float32),
        )
        query_key_value_row_gradient = jnp.concatenate(
            [grad_query, grad_key, grad_value], axis=-1
        ).astype(jnp.bfloat16)
        sum_qkv = sum_qkv + jnp.einsum(
            "hui,huq->iq",
            attention_input,
            query_key_value_row_gradient,
            preferred_element_type=jnp.float32,
        )
        grad_attn_in = jnp.einsum(
            "wfh,yh->wfy",
            query_key_value_row_gradient,
            query_key_value_weight,
            preferred_element_type=jnp.float32,
        )
        grad_norm_one, gain_one_step = norm_backward(
            grad_attn_in, normed_one, inverse_one, gain_one
        )
        sum_gain_one = sum_gain_one + gain_one_step
        grads_in.append(grad_resid + grad_norm_one)
    grad_first, grad_second = (
        lax.psum_scatter(
            sum_first.astype(jnp.bfloat16), "batch", scatter_dimension=2, tiled=True
        ).astype(jnp.float32),
        lax.psum_scatter(
            sum_second.astype(jnp.bfloat16), "batch", scatter_dimension=1, tiled=True
        ).astype(jnp.float32),
    )
    grad_qkv, grad_out, grad_ctrl, grad_gain_one, grad_gain_two = (
        lax.psum_scatter(sum_qkv, ("batch", "expert"), scatter_dimension=0, tiled=True),
        lax.psum_scatter(sum_out, ("batch", "expert"), scatter_dimension=0, tiled=True),
        lax.psum_scatter(sum_ctrl, ("batch", "expert"), scatter_dimension=0, tiled=True),
        lax.psum_scatter(sum_gain_one, ("batch", "expert"), scatter_dimension=0, tiled=True),
        lax.psum_scatter(sum_gain_two, ("batch", "expert"), scatter_dimension=0, tiled=True),
    )
    return (
        jnp.stack(outputs),
        jnp.stack(grads_in),
        grad_qkv,
        grad_out,
        grad_ctrl,
        grad_first,
        grad_second,
        grad_gain_one,
        grad_gain_two,
    )


F32 = jnp.float32
BF16 = jnp.bfloat16
PB = 16
CHUNKS = 2
VMEM_LIMIT = 60 * 1024 * 1024
KERNEL_COST = pl.CostEstimate(flops=30_000_000_000, bytes_accessed=100_000, transcendentals=0)
SMALL_COST = pl.CostEstimate(flops=1_000_000, bytes_accessed=100_000, transcendentals=0)


def dot_nn(a, b):
    return lax.dot_general(a, b, (((1,), (0,)), ((), ())), preferred_element_type=F32)


def dot_nt(a, b):
    return lax.dot_general(a, b, (((1,), (1,)), ((), ())), preferred_element_type=F32)


def dot_tn(a, b):
    return lax.dot_general(a, b, (((0,), (0,)), ((), ())), preferred_element_type=F32)


def row_norm(rows):
    centred = rows - jnp.mean(rows, -1, keepdims=True)
    inverse = lax.rsqrt(jnp.mean(centred * centred, -1, keepdims=True) + 1e-05)
    return centred * inverse, inverse


def row_norm_back(incoming, normed, inverse, gain):
    scaled = incoming * gain
    return inverse * (
        scaled
        - jnp.mean(scaled, -1, keepdims=True)
        - normed * jnp.mean(scaled * normed, -1, keepdims=True)
    )


def head_lanes(rows, lanes, head):
    lane = lax.broadcasted_iota(jnp.int32, (rows, lanes), 1)
    return (lane < lanes // 2) if head == 0 else (lane >= lanes // 2)


def causal_tile(size):
    key = lax.broadcasted_iota(jnp.int32, (size, size), 0)
    query = lax.broadcasted_iota(jnp.int32, (size, size), 1)
    return key <= query


def attention_forward_kernel(waits, z_ref, *refs):
    quarters = 4
    parts, refs = refs[:quarters], refs[:quarters] + refs[quarters + waits:]
    (wqkv_ref, wo_ref, g1_ref, g2_ref, x_ref, qkv_ref, lse_ref, ctx_ref, attn_ref, mix_ref, more_ref) = refs[quarters:-2]
    ctx_pairs, sems = refs[-2:]
    length, width = x_ref.shape
    pairs = HEADS // 2
    lanes = width // pairs
    half = lanes // 2
    nb = mix_ref.shape[0]
    tile = length // quarters
    factor = half ** (-0.5)
    copies = []
    for k in range(quarters):
        source = lax.rem(z_ref[0] - k + quarters, quarters)
        rows = pl.ds(pl.multiple_of(source * tile, tile), tile)
        copies.append(pltpu.make_async_copy(parts[k], x_ref.at[rows, :], sems.at[k]))
        copies[-1].start()
    for copy in copies:
        copy.wait()

    def project(i, carry):
        rows = pl.ds(pl.multiple_of(i * tile, tile), tile)
        normed, _ = row_norm(x_ref[rows, :].astype(F32))
        attn_in = (normed * g1_ref[...]).astype(BF16)
        for part in range(3):
            out = dot_nn(attn_in, wqkv_ref[:, part * width:(part + 1) * width]).astype(BF16)
            for p in range(pairs):
                qkv_ref[part * pairs + p, rows, :] = out[:, p * lanes:(p + 1) * lanes]
        return carry

    lax.fori_loop(0, quarters, project, 0, unroll=True)

    def attend(p, carry):
        values_t = qkv_ref[2 * pairs + p].T
        for j in range(quarters):
            seen = (j + 1) * tile
            queries = qkv_ref[p, j * tile:seen, :] * jnp.asarray(factor, BF16)
            outs = []
            for h in range(2):
                masked = jnp.where(head_lanes(tile, lanes, h), queries, jnp.zeros((), BF16))
                scores = dot_nt(qkv_ref[pairs + p, :seen, :], masked)
                last = jnp.where(causal_tile(tile), scores[j * tile:], NEG_FILL)
                scores = jnp.concatenate([scores[:j * tile], last], 0) if j else last
                high = jnp.max(scores, 0, keepdims=True)
                weights = jnp.exp(scores - high)
                total = jnp.sum(weights, 0, keepdims=True)
                out = dot_nn(values_t[h * half:(h + 1) * half, :seen], weights.astype(BF16))
                outs.append(out / total)
                lse_ref[2 * p + h, :, j * tile:seen] = high + jnp.log(total)
            ctx_pairs[p, j * tile:seen, :] = jnp.concatenate(outs, 0).T.astype(BF16)
        return carry

    lax.fori_loop(0, pairs, attend, 0)

    def finish(i, carry):
        rows = pl.ds(pl.multiple_of(i * tile, tile), tile)
        context = jnp.concatenate([ctx_pairs[p, rows, :] for p in range(pairs)], -1)
        ctx_ref[rows, :] = context
        attn = dot_nn(context, wo_ref[...])
        attn_ref[rows, :] = attn
        normed, _ = row_norm(x_ref[rows, :].astype(F32) + attn)
        mix = (normed * g2_ref[...]).astype(BF16)
        low = attn.astype(BF16)
        for b in range(nb):
            at = b * CHUNKS * PB
            mix_ref[b, i] = mix[at:at + PB]
            more_ref[b, 0, i] = mix[at + PB:at + 2 * PB]
            more_ref[b, 1, i] = low[at:at + PB]
            more_ref[b, 2, i] = low[at + PB:at + 2 * PB]
        return carry

    lax.fori_loop(0, quarters, finish, 0, unroll=True)


def attention_forward(z, parts, wqkv, wo, g1, g2, nb, waits=()):
    quarters = len(parts)
    tile, width = parts[0].shape
    length = quarters * tile
    pairs = HEADS // 2
    lanes = width // pairs
    vmem = pl.BlockSpec(memory_space=pltpu.VMEM)
    return pl.pallas_call(
        functools.partial(attention_forward_kernel, len(waits)),
        in_specs=[pl.BlockSpec(memory_space=pltpu.SMEM)]
        + [pl.BlockSpec(memory_space=pl.ANY)] * (quarters + len(waits)) + [vmem] * 4,
        out_shape=(
            jax.ShapeDtypeStruct((length, width), BF16),
            jax.ShapeDtypeStruct((3 * pairs, length, lanes), BF16),
            jax.ShapeDtypeStruct((HEADS, 1, length), F32),
            jax.ShapeDtypeStruct((length, width), BF16),
            jax.ShapeDtypeStruct((length, width), F32),
            jax.ShapeDtypeStruct((nb, quarters, PB, width), BF16),
            jax.ShapeDtypeStruct((nb, 3, quarters, PB, width), BF16),
        ),
        scratch_shapes=[
            pltpu.VMEM((pairs, length, lanes), BF16),
            pltpu.SemaphoreType.DMA((quarters,)),
        ],
        compiler_params=pltpu.CompilerParams(vmem_limit_bytes=VMEM_LIMIT),
        cost_estimate=SMALL_COST,
        name="attention_forward",
    )(z, *parts, *waits, wqkv, wo, g1, g2)


def attention_backward_kernel(count, *refs):
    attention_backward_body(*refs[:12], *refs[12 + count:])


def attention_backward_body(gm0_ref, gm1_ref, cot_ref, x_ref, attn_ref, ctx_ref, qkv_ref, lse_ref,
                              wqkv_ref, wo_ref, g1_ref, g2_ref,
                              gin_ref, dw_ref, dg1_ref, dg2_ref,
                              delta, ga_rows, dctx, gqkv, attn_in, dk_sum, dv_sum):
    length, width = x_ref.shape
    pairs = HEADS // 2
    lanes = width // pairs
    half = lanes // 2
    nb, quarters, _, _ = gm0_ref.shape
    tile = length // quarters
    factor = half ** (-0.5)
    dg2_ref[...] = jnp.zeros_like(dg2_ref)
    dg1_ref[...] = jnp.zeros_like(dg1_ref)

    def first(i, carry):
        rows = pl.ds(pl.multiple_of(i * tile, tile), tile)
        normed, inverse = row_norm(x_ref[rows, :].astype(F32) + attn_ref[rows, :])
        grad = jnp.concatenate([r[b, i] for b in range(nb) for r in (gm0_ref, gm1_ref)], 0).astype(F32)
        dg2_ref[...] += jnp.sum(grad * normed, 0, keepdims=True)
        back = row_norm_back(grad, normed, inverse, g2_ref[...])
        delta[rows, :] = back
        cot = jnp.concatenate([cot_ref[b, i] for b in range(nb)], 0).astype(F32)
        grad_attn = (cot + back).astype(BF16)
        ga_rows[rows, :] = grad_attn
        grad_ctx = dot_nt(grad_attn, wo_ref[...]).astype(BF16)
        for p in range(pairs):
            dctx[p, rows, :] = grad_ctx[:, p * lanes:(p + 1) * lanes]
        return carry

    lax.fori_loop(0, quarters, first, 0, unroll=True)

    dw_ref[:, 3 * width:] = dot_tn(ctx_ref[...], ga_rows[...]).astype(BF16)

    def attend(p, carry):
        lane0 = pl.multiple_of(p * lanes, lanes)
        keys_t = qkv_ref[pairs + p].T
        dk_sum[...] = jnp.zeros_like(dk_sum)
        dv_sum[...] = jnp.zeros_like(dv_sum)
        for j in range(quarters):
            seen = (j + 1) * tile
            queries = qkv_ref[p, j * tile:seen, :] * jnp.asarray(factor, BF16)
            grads = dctx[p, j * tile:seen, :]
            context = ctx_ref[j * tile:seen, pl.ds(lane0, lanes)]
            products = (grads.astype(F32) * context.astype(F32)).T
            outs = []
            for h in range(2):
                inside = head_lanes(tile, lanes, h)
                q_masked = jnp.where(inside, queries, jnp.zeros((), BF16))
                g_masked = jnp.where(inside, grads, jnp.zeros((), BF16))
                dots = jnp.sum(products[h * half:(h + 1) * half], 0, keepdims=True)
                scores = dot_nt(qkv_ref[pairs + p, :seen, :], q_masked)
                probs = jnp.exp(scores - lse_ref[2 * p + h, :, j * tile:seen])
                last = jnp.where(causal_tile(tile), probs[j * tile:], 0.0)
                probs = jnp.concatenate([probs[:j * tile], last], 0) if j else last
                grad_probs = dot_nt(qkv_ref[2 * pairs + p, :seen, :], g_masked)
                grad_scores = (probs * (grad_probs - dots)).astype(BF16)
                dv_sum[:seen, :] += dot_nn(probs.astype(BF16), g_masked)
                dk_sum[:seen, :] += dot_nn(grad_scores, q_masked)
                outs.append(dot_nn(keys_t[h * half:(h + 1) * half, :seen], grad_scores))
            gqkv[p, j * tile:seen, :] = (jnp.concatenate(outs, 0).T * factor).astype(BF16)
        gqkv[pairs + p] = dk_sum[...].astype(BF16)
        gqkv[2 * pairs + p] = dv_sum[...].astype(BF16)
        return carry

    lax.fori_loop(0, pairs, attend, 0)

    def last(i, carry):
        rows = pl.ds(pl.multiple_of(i * tile, tile), tile)
        normed, inverse = row_norm(x_ref[rows, :].astype(F32))
        attn_in[rows, :] = (normed * g1_ref[...]).astype(BF16)
        grads = jnp.concatenate([gqkv[c, rows, :] for c in range(3 * pairs)], -1)
        grad = dot_nt(grads, wqkv_ref[...])
        dg1_ref[...] += jnp.sum(grad * normed, 0, keepdims=True)
        gin_ref[rows, :] = (delta[rows, :] + row_norm_back(grad, normed, inverse, g1_ref[...])).astype(BF16)
        return carry

    lax.fori_loop(0, quarters, last, 0, unroll=True)

    for c in range(3):
        grads = jnp.concatenate([gqkv[c * pairs + p] for p in range(pairs)], -1)
        dw_ref[:, c * width:(c + 1) * width] = dot_tn(attn_in[...], grads).astype(BF16)


def attention_backward(gm0, gm1, cot, x, attn, ctx, qkv, lse, wqkv, wo, g1, g2, waits=()):
    length, width = x.shape
    pairs = HEADS // 2
    lanes = width // pairs
    return pl.pallas_call(
        functools.partial(attention_backward_kernel, len(waits)),
        in_specs=[pl.BlockSpec(memory_space=pltpu.VMEM)] * 12 + [pl.BlockSpec(memory_space=pl.ANY)] * len(waits),
        out_shape=(
            jax.ShapeDtypeStruct((length, width), BF16),
            jax.ShapeDtypeStruct((width, 4 * width), BF16),
            jax.ShapeDtypeStruct((1, width), F32),
            jax.ShapeDtypeStruct((1, width), F32),
        ),
        scratch_shapes=[
            pltpu.VMEM((length, width), F32),
            pltpu.VMEM((length, width), BF16),
            pltpu.VMEM((pairs, length, lanes), BF16),
            pltpu.VMEM((3 * pairs, length, lanes), BF16),
            pltpu.VMEM((length, width), BF16),
            pltpu.VMEM((length, lanes), F32),
            pltpu.VMEM((length, lanes), F32),
        ],
        compiler_params=pltpu.CompilerParams(vmem_limit_bytes=VMEM_LIMIT),
        cost_estimate=SMALL_COST,
        name="attention_backward",
    )(gm0, gm1, cot, x, attn, ctx, qkv, lse, wqkv, wo, g1, g2, *waits)


def group_reduce(rows, mem, op, fill):
    result = jnp.zeros_like(rows)
    for k in range(mem.shape[0]):
        inside = mem[k:k + 1, :] > 0
        part = jnp.where(inside, rows, fill)
        shift = rows.shape[1] // 2
        while shift >= PB:
            part = op(part, pltpu.roll(part, shift, 1))
            shift //= 2
        result = jnp.where(inside, part, result)
    return result


def gelu_both(v):
    square = v * v
    tanh = jnp.tanh(0.7978845608028654 * v * (1.0 + 0.044715 * square))
    half = 0.5 * (1.0 + tanh)
    slope = half + v * (1.0 - tanh * tanh) * (0.3989422804014327 + 0.0535161223274472 * square)
    return v * half, slope


def start(copy):
    copy.start()


def wait(copy):
    copy.wait()


def arrivals(z, sources, sems, base, act, place):
    if len(sources) == 1:
        act(pltpu.make_async_copy(*place(sources[0], None), sems.at[base]))
        return
    n = (len(sources) + 1) // 2
    act(pltpu.make_async_copy(*place(sources[0], z), sems.at[base]))
    for k in range(1, n):
        @pl.when(z >= k)
        def _():
            act(pltpu.make_async_copy(*place(sources[k], z - k), sems.at[base + k]))

        @pl.when(z + k < n)
        def _():
            act(pltpu.make_async_copy(*place(sources[n - 1 + k], z + k), sems.at[base + n - 1 + k]))


def x_rows(xs, m, q, sl):
    planes, nb, quarters, piece, width = xs.shape
    return jnp.concatenate([xs[m * sl + s, :, q].reshape(nb * piece, width) for s in range(sl)], 0)


def g_rows(gs, m, q, sl):
    quarters, nb, planes, piece, width = gs.shape
    return jnp.concatenate([gs[q, :, m * sl + s].reshape(nb * piece, width) for s in range(sl)], 0)


def mixture_forward_kernel(chunk, parts, waits, z_ref, *refs):
    x_in, refs = refs[:parts], refs[parts + waits:]
    (a_in, ctrl_ref, mem_ref, mkl_ref, take_ref, w1_ref, w2_ref,
     spread_ref, mixed_ref, hid_ref, slope_ref, eo_ref, weights_ref, gates_ref,
     xs, attn, logits, sems) = refs
    planes, nb, quarters, piece, width = xs.shape
    micro = mem_ref.shape[0]
    sl = planes // micro
    experts = mixed_ref.shape[0]
    rows = mkl_ref.shape[1]
    e = pl.program_id(0)
    z = z_ref[0]
    x_place = lambda ref, plane: (ref, xs if plane is None else xs.at[plane])
    a_copy = pltpu.make_async_copy(a_in.at[:, 1 + chunk], attn, sems.at[parts])

    @pl.when(e == 0)
    def _():
        arrivals(z, x_in, sems, 0, start, x_place)
        a_copy.start()
        arrivals(z, x_in, sems, 0, wait, x_place)
        for m in range(micro):
            for q in range(quarters):
                logits[m, q * 8:(q + 1) * 8, :] = dot_nt(ctrl_ref[...], x_rows(xs, m, q, sl))[:8]
            mem = mem_ref[m]
            taking = take_ref[m] > 0
            values = logits[m]
            high = group_reduce(jnp.where(taking, values, NEG_FILL), mem, jnp.maximum, NEG_FILL)
            scaled = jnp.where(taking, jnp.exp(values - high), 0.0)
            gates_ref[m] = scaled / group_reduce(scaled, mem, jnp.add, 0.0)
        for m in range(micro):
            for q in range(quarters):
                block = m * quarters + q
                own = gates_ref[m, q * 8:(q + 1) * 8, :]
                w = jnp.concatenate(
                    [(mkl_ref[m] * own[j:j + 1, :]).astype(BF16) for j in range(experts)], 0)
                weights_ref[block] = w
                blended = dot_nn(w, x_rows(xs, m, q, sl)).astype(BF16)
                for j in range(experts):
                    mixed_ref[j, block * rows:(block + 1) * rows, :] = blended[j * rows:(j + 1) * rows]

    value, slope = gelu_both(dot_nn(mixed_ref[e], w1_ref[0]))
    hidden = value.astype(BF16)
    hid_ref[0] = hidden
    slope_ref[0] = slope.astype(BF16)
    eo_ref[e] = dot_nn(hidden, w2_ref[0]).astype(BF16)

    @pl.when(e == experts - 1)
    def _():
        for m in range(micro):
            for q in range(quarters):
                block = m * quarters + q
                outs = jnp.concatenate(
                    [eo_ref[j, block * rows:(block + 1) * rows, :] for j in range(experts)], 0)
                spread = dot_tn(weights_ref[block], outs).astype(BF16)
                for s in range(sl):
                    at = slice(s * nb * PB, (s + 1) * nb * PB)
                    spread_ref[q, :, 0, m * sl + s] = spread[at].reshape(nb, PB, width)
        a_copy.wait()
        for q in range(quarters):
            mine = spread_ref[q, :, 0, z].astype(F32) + attn[:, q].astype(F32)
            spread_ref[q, :, 0, z] = mine.astype(BF16)


def mixture_backward_kernel(chunk, parts, waits, z_ref, *refs):
    x_in, g_in, refs = refs[:parts], refs[parts:2 * parts], refs[2 * parts + waits:]
    (ctrl_ref, mem_ref, mkl_ref, weights_ref, gates_ref, eo_ref, slope_ref, w1_ref, w2_ref,
     gm_ref, geo_ref, gpre_ref, dctrl_ref, xs, gs, gmx, sems) = refs
    planes, nb, quarters, piece, width = xs.shape
    micro, _, lanes = mem_ref.shape
    sl = planes // micro
    experts = geo_ref.shape[0]
    rows = mkl_ref.shape[1]
    e = pl.program_id(0)
    z = z_ref[0]
    mine = pl.ds(chunk * PB, PB)
    x_place = lambda ref, plane: (ref, xs if plane is None else xs.at[plane])
    g_place = lambda ref, plane: (ref.at[..., mine, :], gs if plane is None else gs.at[plane])

    @pl.when(e == 0)
    def _():
        arrivals(z, g_in, sems, 0, start, g_place)
        arrivals(z, x_in, sems, parts, start, x_place)
        arrivals(z, g_in, sems, 0, wait, g_place)
        for m in range(micro):
            for q in range(quarters):
                block = m * quarters + q
                grads = dot_nn(weights_ref[block], g_rows(gs, m, q, sl)).astype(BF16)
                for j in range(experts):
                    geo_ref[j, block * rows:(block + 1) * rows, :] = grads[j * rows:(j + 1) * rows]
        arrivals(z, x_in, sems, parts, wait, x_place)

    grad_pre = (dot_nt(geo_ref[e], w2_ref[0]) * slope_ref[0].astype(F32)).astype(BF16)
    gpre_ref[0] = grad_pre
    gmx[e] = dot_nt(grad_pre, w1_ref[0]).astype(BF16)

    @pl.when(e == experts - 1)
    def _():
        dctrl = jnp.zeros(dctrl_ref.shape, F32)
        ctrl8 = ctrl_ref[:8, :].astype(F32)
        ctrl_twice = jnp.concatenate([ctrl8, ctrl8], 0).astype(BF16)
        for m in range(micro):
            for q in range(quarters):
                block = m * quarters + q
                at = slice(block * rows, (block + 1) * rows)
                outs = jnp.concatenate([eo_ref[j, at, :] for j in range(experts)], 0)
                backs = jnp.concatenate([gmx[j, at, :] for j in range(experts)], 0)
                w = weights_ref[block]
                inputs = x_rows(xs, m, q, sl)
                dots = dot_nt(outs, g_rows(gs, m, q, sl)) + dot_nt(backs, inputs)
                grad_gates = [
                    jnp.sum(dots[j * rows:(j + 1) * rows] * mkl_ref[m], 0, keepdims=True)
                    for j in range(experts)]
                if experts < 8:
                    grad_gates.append(jnp.zeros((8 - experts, lanes), F32))
                grad_gates = jnp.concatenate(grad_gates, 0)
                own = gates_ref[m, q * 8:(q + 1) * 8, :]
                inner = group_reduce(own * grad_gates, mem_ref[m], jnp.add, 0.0)
                grad_logits = own * (grad_gates - inner)
                upper = grad_logits.astype(BF16).astype(F32)
                both = jnp.concatenate([upper, grad_logits - upper], 0).astype(BF16)
                grad_mix = (dot_tn(w, backs) + dot_tn(both, ctrl_twice)).astype(BF16)
                for s in range(sl):
                    part = slice(s * nb * PB, (s + 1) * nb * PB)
                    gm_ref[m * sl + s, :, q] = grad_mix[part].reshape(nb, PB, width)
                dctrl += dot_nn(both, inputs)
        dctrl_ref[...] = dctrl


def whole(shape):
    return pl.BlockSpec(shape, lambda e: (0,) * len(shape))


def by_expert(shape):
    return pl.BlockSpec((1,) + shape[1:], lambda e: (e, 0, 0))


def mixture_sizes(x_parts, mem, mkl, w1):
    nb, quarters, piece, width = x_parts[0].shape[-4:]
    planes = quarters
    experts, _, hidden_size = w1.shape
    total = mem.shape[0] * quarters * mkl.shape[1]
    back = (planes, nb, quarters, piece, width)
    return back, (experts, total, width), (experts, total, hidden_size)


def mixture_forward(chunk, z, x_parts, a_all, ctrl, mem, mkl, take, w1, w2, waits=()):
    back, narrow, wide = mixture_sizes(x_parts, mem, mkl, w1)
    micro, _, lanes = mem.shape
    quarters = back[2]
    weights = (micro * quarters, narrow[0] * mkl.shape[1], lanes)
    gates = (micro, quarters * 8, lanes)
    any_spec = pl.BlockSpec(memory_space=pl.ANY)
    return pl.pallas_call(
        functools.partial(mixture_forward_kernel, chunk, len(x_parts), len(waits)),
        grid=(narrow[0],),
        input_output_aliases={1 + len(x_parts): 0} if chunk else {},
        out_shape=(
            jax.ShapeDtypeStruct(back[:2] + (CHUNKS,) + back[2:], BF16),
            jax.ShapeDtypeStruct(narrow, BF16),
            jax.ShapeDtypeStruct(wide, BF16),
            jax.ShapeDtypeStruct(wide, BF16),
            jax.ShapeDtypeStruct(narrow, BF16),
            jax.ShapeDtypeStruct(weights, BF16),
            jax.ShapeDtypeStruct(gates, F32),
        ),
        in_specs=[pl.BlockSpec(memory_space=pltpu.SMEM)]
        + [any_spec] * (len(x_parts) + len(waits) + 1)
        + [whole(ctrl.shape), whole(mem.shape), whole(mkl.shape), whole(take.shape),
           by_expert(w1.shape), by_expert(w2.shape)],
        out_specs=(pl.BlockSpec(back[:2] + (1,) + back[2:], lambda e: (0, 0, chunk, 0, 0, 0)), whole(narrow), by_expert(wide), by_expert(wide),
                   whole(narrow), whole(weights), whole(gates)),
        scratch_shapes=[
            pltpu.VMEM(back, BF16),
            pltpu.VMEM(back[1:], BF16),
            pltpu.VMEM(gates, F32),
            pltpu.SemaphoreType.DMA((len(x_parts) + 1,)),
        ],
        compiler_params=pltpu.CompilerParams(vmem_limit_bytes=VMEM_LIMIT),
        cost_estimate=SMALL_COST,
        name="mixture_forward",
    )(z, *x_parts, *waits, a_all, ctrl, mem, mkl, take, w1, w2)


def mixture_backward(chunk, z, x_parts, g_parts, ctrl, mem, mkl, weights, gates, eo, slope, w1, w2, waits=()):
    back, narrow, wide = mixture_sizes(x_parts, mem, mkl, w1)
    parts = len(x_parts)
    any_spec = pl.BlockSpec(memory_space=pl.ANY)
    return pl.pallas_call(
        functools.partial(mixture_backward_kernel, chunk, parts, len(waits)),
        grid=(narrow[0],),
        out_shape=(
            jax.ShapeDtypeStruct(back, BF16),
            jax.ShapeDtypeStruct(narrow, BF16),
            jax.ShapeDtypeStruct(wide, BF16),
            jax.ShapeDtypeStruct((16, back[4]), F32),
        ),
        in_specs=[pl.BlockSpec(memory_space=pltpu.SMEM)]
        + [any_spec] * (2 * parts + len(waits))
        + [whole(ctrl.shape), whole(mem.shape), whole(mkl.shape), whole(weights.shape),
           whole(gates.shape), whole(narrow), by_expert(wide), by_expert(w1.shape), by_expert(w2.shape)],
        out_specs=(whole(back), whole(narrow), by_expert(wide), whole((16, back[4]))),
        scratch_shapes=[
            pltpu.VMEM(back, BF16),
            pltpu.VMEM(back, BF16),
            pltpu.VMEM(narrow, BF16),
            pltpu.SemaphoreType.DMA((2 * parts,)),
        ],
        compiler_params=pltpu.CompilerParams(vmem_limit_bytes=VMEM_LIMIT),
        cost_estimate=SMALL_COST,
        name="mixture_backward",
    )(z, *x_parts, *g_parts, *waits, ctrl, mem, mkl, weights, gates, eo, slope, w1, w2)


def weight_grads_kernel(z_ref, m0, m1, p0, p1, h0, h1, o0, o1, *refs):
    keep_ref, send_ref = refs[-2:]
    width, step = keep_ref.shape[-2:]
    crossed = pl.program_id(0) >= pl.num_programs(0) // 2
    core = lax.rem(z_ref[1], 2)
    left1 = m0[0].T, m1[0].T
    left2 = o0[0].T, o1[0].T
    for t in range(p0.shape[2] // step // 2):
        x, y = t % 2, t // 2
        hop1, hop2 = jnp.where(crossed, y, x), jnp.where(crossed, x, y)
        for ref, part in ((keep_ref, core), (send_ref, 1 - core)):
            at = pl.ds(pl.multiple_of((2 * t + part) * step, step), step)
            first = dot_nn(left1[0], p0[0, :, at]) + dot_nn(left1[1], p1[0, :, at])
            ref[0, 0, hop1, hop2, 0] = first.astype(BF16)
            second = dot_nn(left2[0], h0[0, :, at]) + dot_nn(left2[1], h1[0, :, at])
            ref[0, 0, hop1, hop2, 1] = second.astype(BF16)


def weight_grads(z, mixed, gpre, hid, geo, nb, waits=()):
    experts, total, width = mixed[0].shape
    hidden_size = gpre[0].shape[2]
    step = hidden_size // nb
    half = experts // 2
    row = pl.BlockSpec((1, total, width), lambda e: (e, 0, 0))
    wide = pl.BlockSpec((1, total, hidden_size), lambda e: (e, 0, 0))
    out = pl.BlockSpec((1, 1, 2, 2, 2, width, step), lambda e: (e // half, e % half, 0, 0, 0, 0, 0))
    return pl.pallas_call(
        weight_grads_kernel,
        grid=(experts,),
        in_specs=[pl.BlockSpec(memory_space=pltpu.SMEM)]
        + [row] * 2 + [wide] * 4 + [row] * 2 + [pl.BlockSpec(memory_space=pl.ANY)] * len(waits),
        out_shape=(jax.ShapeDtypeStruct((2, half, 2, 2, 2, width, step), BF16),) * 2,
        out_specs=(out, out),
        compiler_params=pltpu.CompilerParams(vmem_limit_bytes=VMEM_LIMIT),
        cost_estimate=SMALL_COST,
        name="weight_grads",
    )(z, *mixed, *gpre, *hid, *geo, *waits)


def pick(parts, index):
    return lax.dynamic_index_in_dim(parts, index, 0, keepdims=False)


def pass_on(*refs):
    pass


def after(value, *others):
    spec = pl.BlockSpec(memory_space=pl.ANY)
    return pl.pallas_call(
        pass_on,
        out_shape=jax.ShapeDtypeStruct(value.shape, value.dtype),
        in_specs=[spec] * (1 + len(others)),
        out_specs=spec,
        input_output_aliases={0: 0},
        name="after",
        cost_estimate=SMALL_COST,
    )(value, *others)


def line_step(ups, downs, count):
    up = [(i, i + 1) for i in range(count - 1)]
    down = [(i + 1, i) for i in range(count - 1)]
    return (ups + [lax.ppermute(ups[-1], "expert", up)],
            downs + [lax.ppermute(downs[-1], "expert", down)])


def line_scatter(parts, z, count):
    up = [(i, i + 1) for i in range(count - 1)]
    down = [(i + 1, i) for i in range(count - 1)]

    def own(index):
        return pick(parts, jnp.clip(index, 0, count - 1)).astype(F32)

    rising, falling = own(z + count - 1).astype(BF16), own(z - count + 1).astype(BF16)
    for step in range(1, count):
        rising = lax.ppermute(rising, "expert", up).astype(F32)
        falling = lax.ppermute(falling, "expert", down).astype(F32)
        if step < count - 1:
            rising = (rising + own(z + count - 1 - step)).astype(BF16)
            falling = (falling + own(z - count + 1 + step)).astype(BF16)
    return (rising + falling + own(z)).astype(BF16)


def to_planes(parts, z, count):
    got = [pick(parts, z)]
    for k in range(1, count):
        part = pick(parts, lax.rem(z + k, count))
        got.append(lax.ppermute(part, "expert", [(i, (i + k) % count) for i in range(count)]))
    return got


def swap_halves(blocks, bit, count):
    mine = lax.rem(lax.axis_index("batch") >> bit, 2)
    other = lax.ppermute(pick(blocks, 1 - mine), "batch", [(i, i ^ (1 << bit)) for i in range(count)])
    return (pick(blocks, mine).astype(F32) + other.astype(F32)).astype(BF16)


def first_halves(keep, came):
    own = lax.axis_index("batch")
    mine = [lax.rem(own >> bit, 2) for bit in (1, 2)]

    def part(half, expert, index):
        return (pick(keep[half, expert], index).astype(F32) + pick(came[half, expert], index).astype(F32)).astype(BF16)

    experts = range(keep.shape[1])
    return ([[part(i, e, mine[i]) for e in experts] for i in range(2)],
            [[part(i, e, 1 - mine[i]) for e in experts] for i in range(2)])


def hop(keep, send, bit):
    came = lax.ppermute(send, "batch", [(j, j ^ (1 << bit)) for j in range(8)])
    return (keep.astype(F32) + came.astype(F32)).astype(BF16)


def second_hop(held):
    both = [swap_halves(part, 2 - i, 8) for i in range(2) for part in held[i]]
    both = jnp.stack(both).astype(F32)
    return both[:, 0], both[:, 1].transpose(0, 2, 1)


def body(
    tokens,
    cotangent,
    query_key_value_weight,
    output_weight,
    controller_weight,
    w_first,
    w_second,
    gain_one,
    gain_two,
    group_sizes,
    live,
):
    micro, sl, local_len, width = tokens.shape
    planes = lax.axis_size("expert")
    nb = lax.axis_size("batch")
    experts = w_first.shape[0]
    seqs = live.shape[1]
    z = lax.axis_index("expert")
    piece = local_len // nb
    if micro * sl != planes or piece != CHUNKS * PB or nb != 8:
        return body_by_position(
            tokens, cotangent, query_key_value_weight, output_weight, controller_weight,
            w_first, w_second, gain_one, gain_two, group_sizes, live)
    g1, g2 = gain_one.reshape(1, width), gain_two.reshape(1, width)

    own = lax.axis_index("batch")
    z_arr = jnp.stack([z, own]).astype(jnp.int32)
    x_parts = to_planes(tokens.reshape(planes, local_len, width).astype(BF16), z, planes)

    cot = cotangent.reshape(planes, nb, piece, width)
    pieces = []
    for k in range(nb):
        part = lax.dynamic_index_in_dim(cot, own ^ k, 1, keepdims=False).astype(BF16)
        if k:
            part = lax.ppermute(part, "batch", [(i, i ^ k) for i in range(nb)])
        pieces.append(part)
    pieces[1] = after(pieces[1], *x_parts[1:])
    cot = jnp.take(jnp.stack(pieces), own ^ jnp.arange(nb), axis=0)
    g_all = lax.all_gather(cot, "expert", axis=0, tiled=False)

    x, qkv, lse, ctx, attn, mix, more = attention_forward(
        z_arr, x_parts, query_key_value_weight, output_weight, g1, g2, nb, waits=(cot,))

    member, taking = jax.vmap(group_tables)(group_sizes, live)
    groups = member.shape[2]
    mem = member.reshape(micro, nb, sl, groups).transpose(0, 3, 2, 1).reshape(micro, groups, seqs)
    mem = jnp.repeat(mem.astype(F32), PB, axis=2)
    take = taking.reshape(micro, nb, sl).transpose(0, 2, 1).reshape(micro, 1, seqs)
    take = jnp.repeat(take.astype(F32), PB, axis=2)
    place = jnp.arange(seqs * PB, dtype=jnp.int32) % PB
    same = (jnp.arange(PB, dtype=jnp.int32)[:, None] == place[None, :]).astype(F32)
    mkl = (mem[:, :, None, :] * same).reshape(micro, groups * PB, seqs * PB)
    ctrl = lax.dynamic_slice_in_dim(controller_weight, z * experts, experts, 1).T
    ctrl = jnp.pad(ctrl, ((0, 16 - experts), (0, 0)))

    def over_batch(block):
        return lax.all_to_all(block, "batch", split_axis=0, concat_axis=0, tiled=True)

    def over_expert(blocks):
        return lax.all_to_all(blocks, "expert", split_axis=0, concat_axis=0, tiled=True)

    own0 = over_batch(mix)
    x0 = [lax.all_gather(own0, "expert", axis=0, tiled=False)]
    more = over_batch(after(more, own0))
    x1 = [lax.all_gather(more[:, 0], "expert", axis=0, tiled=False)]
    g_parts = [g_all]

    cot_own = lax.dynamic_index_in_dim(g_all, z, 2, keepdims=False).transpose(1, 0, 2, 3)
    cot_own = over_batch(cot_own)
    spread0, mixed0, hid0, slope0, eo0, weights0, gates0 = mixture_forward(
        0, z_arr, x0, more, ctrl, mem, mkl, take, w_first, w_second, waits=(cot_own,))
    back0, geo0, gpre0, dctrl0 = mixture_backward(
        0, z_arr, x0, g_parts, ctrl, mem, mkl, weights0, gates0, eo0, slope0, w_first, w_second,
        waits=())
    back0 = lax.psum_scatter(after(back0, x1[0]), "expert", scatter_dimension=0, tiled=False)
    spread, mixed1, hid1, slope1, eo1, weights1, gates1 = mixture_forward(
        1, z_arr, x1, more, ctrl, mem, mkl, take, w_first, w_second, waits=(spread0, dctrl0))
    back1, geo1, gpre1, dctrl1 = mixture_backward(
        1, z_arr, x1, g_parts, ctrl, mem, mkl, weights1, gates1, eo1, slope1, w_first, w_second)
    dctrl = dctrl0[:8] + dctrl0[8:] + dctrl1[:8] + dctrl1[8:]
    back1 = lax.psum_scatter(after(back1, back0), "expert", scatter_dimension=0, tiled=False)
    back0 = over_batch(back0)
    keep, send = weight_grads(
        z_arr, (mixed0, mixed1), (gpre0, gpre1), (hid0, hid1), (geo0, geo1), nb, waits=(back0,))
    spread = lax.psum_scatter(after(spread, back1), "expert", scatter_dimension=0, tiled=False)
    send = after(send, back1)
    back1 = over_batch(back1)
    came = lax.ppermute(send, "batch", [(i, i ^ 1) for i in range(nb)])
    keeps, sends = first_halves(keep, came)

    gin, dw, dg1, dg2 = attention_backward(
        back0, back1, cot_own, x, attn, ctx, qkv, lse, query_key_value_weight, output_weight, g1, g2,
        waits=(sends[0][0], sends[1][0]))
    sends = [[part if e == 0 else after(part, dg1) for e, part in enumerate(parts)] for parts in sends]
    held = [[hop(keeps[i][e], sends[i][e], 1 + i) for e in range(len(sends[i]))] for i in range(2)]
    gin = after(gin, held[0][0], held[1][0])
    dw = after(dw, held[0][0], held[1][0])
    grad_first, grad_second = second_hop(held)

    got = jnp.stack(to_planes(gin.reshape(planes, local_len, width), z, planes))
    gin = jnp.take(got, lax.rem(z - jnp.arange(planes) + planes, planes), axis=0)
    grad_in = cotangent + gin.reshape(tokens.shape).astype(F32)

    dctrl_all = jnp.zeros((planes, experts, width), F32)
    dctrl_all = lax.dynamic_update_slice(dctrl_all, dctrl[None, :experts], (z, 0, 0))
    dctrl_all = dctrl_all.reshape(planes * experts, width).T
    extra = jnp.concatenate([dctrl_all, dg1.T, dg2.T], 1)
    extra = jnp.pad(extra, ((0, 0), (0, 128 - extra.shape[1]))).astype(BF16)
    flat = jnp.concatenate([dw, extra], 1)
    flat = flat.reshape(nb // 2, 2, -1, flat.shape[1]).transpose(1, 0, 2, 3)
    flat = swap_halves(flat, 0, nb)
    chips = [[c + 2 * i for i in range(nb // 2)] for c in range(2)]
    flat = lax.all_to_all(flat, "batch", split_axis=0, concat_axis=0, tiled=True, axis_index_groups=chips)
    flat = jnp.sum(flat.astype(F32), 0).astype(BF16)
    spread = over_batch(after(spread, flat))
    out = tokens + spread.transpose(2, 0, 1, 3, 4).reshape(tokens.shape).astype(F32)
    flat = flat.reshape(planes, -1, flat.shape[1])
    flat = lax.all_to_all(flat, "expert", split_axis=0, concat_axis=0, tiled=True)
    flat = jnp.sum(flat.astype(F32), 0)
    ends = [3 * width, 4 * width, 4 * width + planes * experts]
    grad_qkv, grad_out, grad_ctrl = flat[:, :ends[0]], flat[:, ends[0]:ends[1]], flat[:, ends[1]:ends[2]]
    return (out, grad_in, grad_qkv, grad_out, grad_ctrl, grad_first, grad_second,
            flat[:, ends[2]], flat[:, ends[2] + 1])


def solution(mesh):
    placed = (
        P(None, "batch", "expert", None),
        P(None, "batch", "expert", None),
        P(),
        P(),
        P(),
        P("expert", None, None),
        P("expert", None, None),
        P(),
        P(),
        P(),
        P(),
    )
    return jax.shard_map(
        body,
        mesh=mesh,
        in_specs=placed,
        out_specs=(
            P(None, "batch", "expert", None),
            P(None, "batch", "expert", None),
            P(("batch", "expert"), None),
            P(("batch", "expert"), None),
            P(("batch", "expert"), None),
            P("expert", None, "batch"),
            P("expert", "batch", None),
            P(("batch", "expert")),
            P(("batch", "expert")),
        ),
        check_vma=False,
    )
```

```python
import functools

import jax
import jax.numpy as jnp
from jax import lax
from jax.experimental import pallas as pl
from jax.experimental.pallas import tpu as pltpu
from jax.sharding import PartitionSpec as P

HEADS = 8


HIGH_PRECISION = lax.Precision.HIGHEST
NEG_FILL = -1e30


def group_tables(group_row, live_row):
    seq_count = live_row.shape[0]
    group_ends = jnp.cumsum(group_row)
    group_starts = group_ends - group_row
    numbers = jnp.arange(seq_count, dtype=jnp.int32)
    member = (numbers[:, None] >= group_starts[None, :]) & (numbers[:, None] < group_ends[None, :])
    leading = jnp.any(numbers[:, None] == group_starts[None, :], axis=1)
    taking = (live_row > 0) | leading
    return (member, taking)


def group_softmax(router_logits, member, taking):
    inside = member[:, :, None, None]
    masked = jnp.where(taking[:, None, None], router_logits, NEG_FILL)
    highest = jnp.max(jnp.where(inside, masked[:, None], NEG_FILL), axis=0)
    row_high = jnp.sum(jnp.where(inside, highest[None], 0.0), axis=1)
    scaled = jnp.where(taking[:, None, None], jnp.exp(router_logits - row_high), 0.0)
    group_sums = jnp.sum(jnp.where(inside, scaled[:, None], 0.0), axis=0)
    row_sums = jnp.sum(jnp.where(inside, group_sums[None], 0.0), axis=1)
    return scaled / row_sums


def norm_forward(values_in, scaling):
    centred = values_in - jnp.mean(values_in, -1, keepdims=True)
    inverse = lax.rsqrt(jnp.mean(centred * centred, -1, keepdims=True) + 1e-05)
    normed = centred * inverse
    return (normed * scaling, normed, inverse)


def norm_backward(incoming, normed, inverse, scaling):
    scaled_grad = incoming * scaling
    returned_grad = inverse * (
        scaled_grad
        - jnp.mean(scaled_grad, -1, keepdims=True)
        - normed * jnp.mean(scaled_grad * normed, -1, keepdims=True)
    )
    return (returned_grad, jnp.sum(incoming * normed, axis=(0, 1)))


def attention_probs(query_heads, key_heads, causal, logsum, factor):
    scores = (
        jnp.einsum("sqhc,skhc->shqk", query_heads, key_heads, preferred_element_type=jnp.float32)
        * factor
    )
    return jnp.where(causal, jnp.exp(scores - logsum), 0.0)


def body_by_position(
    tokens,
    cotangent,
    query_key_value_weight,
    output_weight,
    controller_weight,
    w_first,
    w_second,
    gain_one,
    gain_two,
    group_sizes,
    live,
):
    micro_count, seq_here, local_len, model_width = tokens.shape
    head_dim = model_width // HEADS
    factor = head_dim ** (-0.5)
    length = local_len * lax.axis_size("expert")
    query_pos = lax.axis_index("expert") * local_len + jnp.arange(local_len, dtype=jnp.int32)
    key_pos = jnp.arange(length, dtype=jnp.int32)
    causal = key_pos[None, :] <= query_pos[:, None]
    ctrl_wide = controller_weight.astype(jnp.float32)
    sum_first = jnp.zeros(w_first.shape, jnp.float32)
    sum_second = jnp.zeros(w_second.shape, jnp.float32)
    sum_qkv = jnp.zeros(query_key_value_weight.shape, jnp.float32)
    sum_out = jnp.zeros(output_weight.shape, jnp.float32)
    sum_ctrl = jnp.zeros(controller_weight.shape, jnp.float32)
    sum_gain_one = jnp.zeros(gain_one.shape, jnp.float32)
    sum_gain_two = jnp.zeros(gain_two.shape, jnp.float32)
    outputs = []
    grads_in = []
    for micro_step in range(micro_count):
        member, taking = group_tables(group_sizes[micro_step], live[micro_step])
        input_rows = tokens[micro_step]
        attn_norm, normed_one, inverse_one = norm_forward(input_rows, gain_one)
        attention_input = attn_norm.astype(jnp.bfloat16)
        projected_rows = jnp.einsum(
            "mtg,gj->mtj",
            attention_input,
            query_key_value_weight,
            preferred_element_type=jnp.float32,
        ).astype(jnp.bfloat16)
        queries = projected_rows[..., :model_width]
        keys_here = projected_rows[..., model_width : 2 * model_width]
        values_here = projected_rows[..., 2 * model_width :]
        keys_all, values_all = (
            lax.all_gather(keys_here, "expert", axis=1, tiled=True),
            lax.all_gather(values_here, "expert", axis=1, tiled=True),
        )
        query_heads = queries.reshape(seq_here, local_len, HEADS, head_dim)
        key_heads = keys_all.reshape(seq_here, length, HEADS, head_dim)
        value_heads = values_all.reshape(seq_here, length, HEADS, head_dim)
        scores = (
            jnp.einsum(
                "sqhc,skhc->shqk", query_heads, key_heads, preferred_element_type=jnp.float32
            )
            * factor
        )
        scores = jnp.where(causal, scores, NEG_FILL)
        highest = jnp.max(scores, -1, keepdims=True)
        logsum = highest + jnp.log(jnp.sum(jnp.exp(scores - highest), -1, keepdims=True))
        probs_low = jnp.exp(scores - logsum).astype(jnp.bfloat16)
        context_rows = jnp.einsum(
            "shqk,skhc->sqhc", probs_low, value_heads, preferred_element_type=jnp.float32
        )
        context_rows = context_rows.reshape(seq_here, local_len, model_width).astype(jnp.bfloat16)
        residual_stream = input_rows + jnp.einsum(
            "mtg,gj->mtj", context_rows, output_weight, preferred_element_type=jnp.float32
        )
        mix_norm, normed_two, inverse_two = norm_forward(residual_stream, gain_two)
        mix_low = mix_norm.astype(jnp.bfloat16)
        mix_pos = lax.all_to_all(mix_low, "batch", split_axis=1, concat_axis=0, tiled=True)
        router_logits = jnp.einsum(
            "spd,de->spe", mix_pos, controller_weight, preferred_element_type=jnp.float32
        )
        gate_vals, gate_pull = jax.vjp(
            functools.partial(group_softmax, member=member, taking=taking), router_logits
        )
        weights_low = jnp.where(
            member[:, None, :, None],
            gate_vals.astype(jnp.bfloat16)[:, :, None, :],
            jnp.zeros((), jnp.bfloat16),
        )
        blended_rows = jnp.einsum(
            "spke,spd->pked", weights_low, mix_pos, preferred_element_type=jnp.float32
        ).astype(jnp.bfloat16)
        mixed_recv = lax.all_to_all(blended_rows, "expert", split_axis=2, concat_axis=0, tiled=True)
        pre_act = jnp.einsum(
            "pked,edf->pkef", mixed_recv, w_first, preferred_element_type=jnp.float32
        )
        activated, gelu_pull = jax.vjp(jax.nn.gelu, pre_act)
        act_low = activated.astype(jnp.bfloat16)
        expert_output = jnp.einsum(
            "pkef,efd->pked", act_low, w_second, preferred_element_type=jnp.float32
        ).astype(jnp.bfloat16)
        returned = lax.all_to_all(expert_output, "expert", split_axis=0, concat_axis=2, tiled=True)
        dispersed_rows = jnp.einsum(
            "spke,pked->spd", weights_low, returned, preferred_element_type=jnp.float32
        ).astype(jnp.bfloat16)
        spread_seq = lax.all_to_all(
            dispersed_rows, "batch", split_axis=0, concat_axis=1, tiled=True
        )
        outputs.append(residual_stream + spread_seq.astype(jnp.float32))
        cot_here = cotangent[micro_step]
        grad_spread = lax.all_to_all(
            cot_here.astype(jnp.bfloat16), "batch", split_axis=1, concat_axis=0, tiled=True
        )
        grad_weights = jnp.einsum(
            "spd,pked->spke", grad_spread, returned, preferred_element_type=jnp.float32
        )
        grad_eout = jnp.einsum(
            "spke,spd->pked", weights_low, grad_spread, preferred_element_type=jnp.float32
        ).astype(jnp.bfloat16)
        grad_eout_recv = lax.all_to_all(
            grad_eout, "expert", split_axis=2, concat_axis=0, tiled=True
        )
        grad_hidden = jnp.einsum(
            "pked,efd->pkef", grad_eout_recv, w_second, preferred_element_type=jnp.float32
        )
        step_second = jnp.einsum(
            "pkef,pked->efd", act_low, grad_eout_recv, preferred_element_type=jnp.float32
        )
        grad_pre = gelu_pull(grad_hidden)[0].astype(jnp.bfloat16)
        step_first = jnp.einsum(
            "pked,pkef->edf", mixed_recv, grad_pre, preferred_element_type=jnp.float32
        )
        sum_first = sum_first + step_first
        sum_second = sum_second + step_second
        grad_mixed = jnp.einsum(
            "pkef,edf->pked", grad_pre, w_first, preferred_element_type=jnp.float32
        ).astype(jnp.bfloat16)
        grad_mix_groups = lax.all_to_all(
            grad_mixed, "expert", split_axis=0, concat_axis=2, tiled=True
        )
        grad_weights = grad_weights + jnp.einsum(
            "pked,spd->spke", grad_mix_groups, mix_pos, preferred_element_type=jnp.float32
        )
        grad_gates = jnp.sum(jnp.where(member[:, None, :, None], grad_weights, 0.0), axis=2)
        grad_logits = gate_pull(grad_gates)[0]
        sum_ctrl = sum_ctrl + jnp.einsum(
            "spd,spe->de", mix_pos.astype(jnp.float32), grad_logits, precision=HIGH_PRECISION
        )
        grad_mix = jnp.einsum(
            "spke,pked->spd", weights_low, grad_mix_groups, preferred_element_type=jnp.float32
        )
        grad_mix = grad_mix + jnp.einsum(
            "spe,de->spd", grad_logits, ctrl_wide, precision=HIGH_PRECISION
        )
        grad_mix_seq = lax.all_to_all(
            grad_mix.astype(jnp.bfloat16), "batch", split_axis=0, concat_axis=1, tiled=True
        )
        grad_norm_two, gain_two_step = norm_backward(
            grad_mix_seq.astype(jnp.float32), normed_two, inverse_two, gain_two
        )
        sum_gain_two = sum_gain_two + gain_two_step
        grad_resid = cot_here + grad_norm_two
        attention_gradient = grad_resid.astype(jnp.bfloat16)
        sum_out = sum_out + jnp.einsum(
            "hui,huq->iq", context_rows, attention_gradient, preferred_element_type=jnp.float32
        )
        grad_context = jnp.einsum(
            "wfh,yh->wfy", attention_gradient, output_weight, preferred_element_type=jnp.float32
        ).astype(jnp.bfloat16)
        context_heads = grad_context.reshape(seq_here, local_len, HEADS, head_dim)
        probs_full = attention_probs(query_heads, key_heads, causal, logsum, factor)
        grad_probs = jnp.einsum(
            "sqhc,skhc->shqk", context_heads, value_heads, preferred_element_type=jnp.float32
        )
        row_dots = jnp.sum(grad_probs * probs_full, -1, keepdims=True)
        grad_scores = (probs_full * (grad_probs - row_dots)).astype(jnp.bfloat16)
        grad_query = (
            jnp.einsum(
                "shqk,skhc->sqhc", grad_scores, key_heads, preferred_element_type=jnp.float32
            )
            * factor
        )
        grad_query = grad_query.reshape(seq_here, local_len, model_width)
        key_terms = (
            jnp.einsum(
                "shqk,sqhc->skhc", grad_scores, query_heads, preferred_element_type=jnp.float32
            )
            * factor
        )
        value_terms = jnp.einsum(
            "shqk,sqhc->skhc",
            probs_full.astype(jnp.bfloat16),
            context_heads,
            preferred_element_type=jnp.float32,
        )
        grad_key, grad_value = (
            lax.psum_scatter(
                key_terms.reshape(seq_here, length, model_width).astype(jnp.bfloat16),
                "expert",
                scatter_dimension=1,
                tiled=True,
            ).astype(jnp.float32),
            lax.psum_scatter(
                value_terms.reshape(seq_here, length, model_width).astype(jnp.bfloat16),
                "expert",
                scatter_dimension=1,
                tiled=True,
            ).astype(jnp.float32),
        )
        query_key_value_row_gradient = jnp.concatenate(
            [grad_query, grad_key, grad_value], axis=-1
        ).astype(jnp.bfloat16)
        sum_qkv = sum_qkv + jnp.einsum(
            "hui,huq->iq",
            attention_input,
            query_key_value_row_gradient,
            preferred_element_type=jnp.float32,
        )
        grad_attn_in = jnp.einsum(
            "wfh,yh->wfy",
            query_key_value_row_gradient,
            query_key_value_weight,
            preferred_element_type=jnp.float32,
        )
        grad_norm_one, gain_one_step = norm_backward(
            grad_attn_in, normed_one, inverse_one, gain_one
        )
        sum_gain_one = sum_gain_one + gain_one_step
        grads_in.append(grad_resid + grad_norm_one)
    grad_first, grad_second = (
        lax.psum_scatter(
            sum_first.astype(jnp.bfloat16), "batch", scatter_dimension=2, tiled=True
        ).astype(jnp.float32),
        lax.psum_scatter(
            sum_second.astype(jnp.bfloat16), "batch", scatter_dimension=1, tiled=True
        ).astype(jnp.float32),
    )
    grad_qkv, grad_out, grad_ctrl, grad_gain_one, grad_gain_two = (
        lax.psum_scatter(sum_qkv, ("batch", "expert"), scatter_dimension=0, tiled=True),
        lax.psum_scatter(sum_out, ("batch", "expert"), scatter_dimension=0, tiled=True),
        lax.psum_scatter(sum_ctrl, ("batch", "expert"), scatter_dimension=0, tiled=True),
        lax.psum_scatter(sum_gain_one, ("batch", "expert"), scatter_dimension=0, tiled=True),
        lax.psum_scatter(sum_gain_two, ("batch", "expert"), scatter_dimension=0, tiled=True),
    )
    return (
        jnp.stack(outputs),
        jnp.stack(grads_in),
        grad_qkv,
        grad_out,
        grad_ctrl,
        grad_first,
        grad_second,
        grad_gain_one,
        grad_gain_two,
    )


F32 = jnp.float32
BF16 = jnp.bfloat16
PB = 16
CHUNKS = 2
VMEM_LIMIT = 60 * 1024 * 1024
KERNEL_COST = pl.CostEstimate(flops=30_000_000_000, bytes_accessed=100_000, transcendentals=0)
SMALL_COST = pl.CostEstimate(flops=1_000_000, bytes_accessed=100_000, transcendentals=0)


def dot_nn(a, b):
    return lax.dot_general(a, b, (((1,), (0,)), ((), ())), preferred_element_type=F32)


def dot_nt(a, b):
    return lax.dot_general(a, b, (((1,), (1,)), ((), ())), preferred_element_type=F32)


def dot_tn(a, b):
    return lax.dot_general(a, b, (((0,), (0,)), ((), ())), preferred_element_type=F32)


def row_norm(rows):
    centred = rows - jnp.mean(rows, -1, keepdims=True)
    inverse = lax.rsqrt(jnp.mean(centred * centred, -1, keepdims=True) + 1e-05)
    return centred * inverse, inverse


def row_norm_back(incoming, normed, inverse, gain):
    scaled = incoming * gain
    return inverse * (
        scaled
        - jnp.mean(scaled, -1, keepdims=True)
        - normed * jnp.mean(scaled * normed, -1, keepdims=True)
    )


def head_lanes(rows, lanes, head):
    lane = lax.broadcasted_iota(jnp.int32, (rows, lanes), 1)
    return (lane < lanes // 2) if head == 0 else (lane >= lanes // 2)


def causal_tile(size):
    key = lax.broadcasted_iota(jnp.int32, (size, size), 0)
    query = lax.broadcasted_iota(jnp.int32, (size, size), 1)
    return key <= query


def attention_forward_kernel(waits, z_ref, *refs):
    quarters = 4
    parts, refs = refs[:quarters], refs[:quarters] + refs[quarters + waits:]
    (wqkv_ref, wo_ref, g1_ref, g2_ref, x_ref, qkv_ref, lse_ref, ctx_ref, attn_ref, mix_ref, more_ref) = refs[quarters:-2]
    ctx_pairs, sems = refs[-2:]
    length, width = x_ref.shape
    pairs = HEADS // 2
    lanes = width // pairs
    half = lanes // 2
    nb = mix_ref.shape[0]
    tile = length // quarters
    factor = half ** (-0.5)
    copies = []
    for k in range(quarters):
        source = lax.rem(z_ref[0] - k + quarters, quarters)
        rows = pl.ds(pl.multiple_of(source * tile, tile), tile)
        copies.append(pltpu.make_async_copy(parts[k], x_ref.at[rows, :], sems.at[k]))
        copies[-1].start()
    for copy in copies:
        copy.wait()

    def project(i, carry):
        rows = pl.ds(pl.multiple_of(i * tile, tile), tile)
        normed, _ = row_norm(x_ref[rows, :].astype(F32))
        attn_in = (normed * g1_ref[...]).astype(BF16)
        for part in range(3):
            out = dot_nn(attn_in, wqkv_ref[:, part * width:(part + 1) * width]).astype(BF16)
            for p in range(pairs):
                qkv_ref[part * pairs + p, rows, :] = out[:, p * lanes:(p + 1) * lanes]
        return carry

    lax.fori_loop(0, quarters, project, 0, unroll=True)

    def attend(p, carry):
        values_t = qkv_ref[2 * pairs + p].T
        for j in range(quarters):
            seen = (j + 1) * tile
            queries = qkv_ref[p, j * tile:seen, :] * jnp.asarray(factor, BF16)
            outs = []
            for h in range(2):
                masked = jnp.where(head_lanes(tile, lanes, h), queries, jnp.zeros((), BF16))
                scores = dot_nt(qkv_ref[pairs + p, :seen, :], masked)
                last = jnp.where(causal_tile(tile), scores[j * tile:], NEG_FILL)
                scores = jnp.concatenate([scores[:j * tile], last], 0) if j else last
                high = jnp.max(scores, 0, keepdims=True)
                weights = jnp.exp(scores - high)
                total = jnp.sum(weights, 0, keepdims=True)
                out = dot_nn(values_t[h * half:(h + 1) * half, :seen], weights.astype(BF16))
                outs.append(out / total)
                lse_ref[2 * p + h, :, j * tile:seen] = high + jnp.log(total)
            ctx_pairs[p, j * tile:seen, :] = jnp.concatenate(outs, 0).T.astype(BF16)
        return carry

    lax.fori_loop(0, pairs, attend, 0)

    def finish(i, carry):
        rows = pl.ds(pl.multiple_of(i * tile, tile), tile)
        context = jnp.concatenate([ctx_pairs[p, rows, :] for p in range(pairs)], -1)
        ctx_ref[rows, :] = context
        attn = dot_nn(context, wo_ref[...])
        attn_ref[rows, :] = attn
        normed, _ = row_norm(x_ref[rows, :].astype(F32) + attn)
        mix = (normed * g2_ref[...]).astype(BF16)
        low = attn.astype(BF16)
        for b in range(nb):
            at = b * CHUNKS * PB
            mix_ref[b, i] = mix[at:at + PB]
            more_ref[b, 0, i] = mix[at + PB:at + 2 * PB]
            more_ref[b, 1, i] = low[at:at + PB]
            more_ref[b, 2, i] = low[at + PB:at + 2 * PB]
        return carry

    lax.fori_loop(0, quarters, finish, 0, unroll=True)


def attention_forward(z, parts, wqkv, wo, g1, g2, nb, waits=()):
    quarters = len(parts)
    tile, width = parts[0].shape
    length = quarters * tile
    pairs = HEADS // 2
    lanes = width // pairs
    vmem = pl.BlockSpec(memory_space=pltpu.VMEM)
    return pl.pallas_call(
        functools.partial(attention_forward_kernel, len(waits)),
        in_specs=[pl.BlockSpec(memory_space=pltpu.SMEM)]
        + [pl.BlockSpec(memory_space=pl.ANY)] * (quarters + len(waits)) + [vmem] * 4,
        out_shape=(
            jax.ShapeDtypeStruct((length, width), BF16),
            jax.ShapeDtypeStruct((3 * pairs, length, lanes), BF16),
            jax.ShapeDtypeStruct((HEADS, 1, length), F32),
            jax.ShapeDtypeStruct((length, width), BF16),
            jax.ShapeDtypeStruct((length, width), F32),
            jax.ShapeDtypeStruct((nb, quarters, PB, width), BF16),
            jax.ShapeDtypeStruct((nb, 3, quarters, PB, width), BF16),
        ),
        scratch_shapes=[
            pltpu.VMEM((pairs, length, lanes), BF16),
            pltpu.SemaphoreType.DMA((quarters,)),
        ],
        compiler_params=pltpu.CompilerParams(vmem_limit_bytes=VMEM_LIMIT),
        cost_estimate=SMALL_COST,
        name="attention_forward",
    )(z, *parts, *waits, wqkv, wo, g1, g2)


def attention_backward_kernel(count, *refs):
    attention_backward_body(*refs[:12], *refs[12 + count:])


def attention_backward_body(gm0_ref, gm1_ref, cot_ref, x_ref, attn_ref, ctx_ref, qkv_ref, lse_ref,
                              wqkv_ref, wo_ref, g1_ref, g2_ref,
                              gin_ref, dw_ref, dg1_ref, dg2_ref,
                              delta, ga_rows, dctx, gqkv, attn_in, dk_sum, dv_sum):
    length, width = x_ref.shape
    pairs = HEADS // 2
    lanes = width // pairs
    half = lanes // 2
    nb, quarters, _, _ = gm0_ref.shape
    tile = length // quarters
    factor = half ** (-0.5)
    dg2_ref[...] = jnp.zeros_like(dg2_ref)
    dg1_ref[...] = jnp.zeros_like(dg1_ref)

    def first(i, carry):
        rows = pl.ds(pl.multiple_of(i * tile, tile), tile)
        normed, inverse = row_norm(x_ref[rows, :].astype(F32) + attn_ref[rows, :])
        grad = jnp.concatenate([r[b, i] for b in range(nb) for r in (gm0_ref, gm1_ref)], 0).astype(F32)
        dg2_ref[...] += jnp.sum(grad * normed, 0, keepdims=True)
        back = row_norm_back(grad, normed, inverse, g2_ref[...])
        delta[rows, :] = back
        cot = jnp.concatenate([cot_ref[b, i] for b in range(nb)], 0).astype(F32)
        grad_attn = (cot + back).astype(BF16)
        ga_rows[rows, :] = grad_attn
        grad_ctx = dot_nt(grad_attn, wo_ref[...]).astype(BF16)
        for p in range(pairs):
            dctx[p, rows, :] = grad_ctx[:, p * lanes:(p + 1) * lanes]
        return carry

    lax.fori_loop(0, quarters, first, 0, unroll=True)

    dw_ref[:, 3 * width:] = dot_tn(ctx_ref[...], ga_rows[...]).astype(BF16)

    def attend(p, carry):
        lane0 = pl.multiple_of(p * lanes, lanes)
        keys_t = qkv_ref[pairs + p].T
        dk_sum[...] = jnp.zeros_like(dk_sum)
        dv_sum[...] = jnp.zeros_like(dv_sum)
        for j in range(quarters):
            seen = (j + 1) * tile
            queries = qkv_ref[p, j * tile:seen, :] * jnp.asarray(factor, BF16)
            grads = dctx[p, j * tile:seen, :]
            context = ctx_ref[j * tile:seen, pl.ds(lane0, lanes)]
            products = (grads.astype(F32) * context.astype(F32)).T
            outs = []
            for h in range(2):
                inside = head_lanes(tile, lanes, h)
                q_masked = jnp.where(inside, queries, jnp.zeros((), BF16))
                g_masked = jnp.where(inside, grads, jnp.zeros((), BF16))
                dots = jnp.sum(products[h * half:(h + 1) * half], 0, keepdims=True)
                scores = dot_nt(qkv_ref[pairs + p, :seen, :], q_masked)
                probs = jnp.exp(scores - lse_ref[2 * p + h, :, j * tile:seen])
                last = jnp.where(causal_tile(tile), probs[j * tile:], 0.0)
                probs = jnp.concatenate([probs[:j * tile], last], 0) if j else last
                grad_probs = dot_nt(qkv_ref[2 * pairs + p, :seen, :], g_masked)
                grad_scores = (probs * (grad_probs - dots)).astype(BF16)
                dv_sum[:seen, :] += dot_nn(probs.astype(BF16), g_masked)
                dk_sum[:seen, :] += dot_nn(grad_scores, q_masked)
                outs.append(dot_nn(keys_t[h * half:(h + 1) * half, :seen], grad_scores))
            gqkv[p, j * tile:seen, :] = (jnp.concatenate(outs, 0).T * factor).astype(BF16)
        gqkv[pairs + p] = dk_sum[...].astype(BF16)
        gqkv[2 * pairs + p] = dv_sum[...].astype(BF16)
        return carry

    lax.fori_loop(0, pairs, attend, 0)

    def last(i, carry):
        rows = pl.ds(pl.multiple_of(i * tile, tile), tile)
        normed, inverse = row_norm(x_ref[rows, :].astype(F32))
        attn_in[rows, :] = (normed * g1_ref[...]).astype(BF16)
        grads = jnp.concatenate([gqkv[c, rows, :] for c in range(3 * pairs)], -1)
        grad = dot_nt(grads, wqkv_ref[...])
        dg1_ref[...] += jnp.sum(grad * normed, 0, keepdims=True)
        gin_ref[rows, :] = (delta[rows, :] + row_norm_back(grad, normed, inverse, g1_ref[...])).astype(BF16)
        return carry

    lax.fori_loop(0, quarters, last, 0, unroll=True)

    for c in range(3):
        grads = jnp.concatenate([gqkv[c * pairs + p] for p in range(pairs)], -1)
        dw_ref[:, c * width:(c + 1) * width] = dot_tn(attn_in[...], grads).astype(BF16)


def attention_backward(gm0, gm1, cot, x, attn, ctx, qkv, lse, wqkv, wo, g1, g2, waits=()):
    length, width = x.shape
    pairs = HEADS // 2
    lanes = width // pairs
    return pl.pallas_call(
        functools.partial(attention_backward_kernel, len(waits)),
        in_specs=[pl.BlockSpec(memory_space=pltpu.VMEM)] * 12 + [pl.BlockSpec(memory_space=pl.ANY)] * len(waits),
        out_shape=(
            jax.ShapeDtypeStruct((length, width), BF16),
            jax.ShapeDtypeStruct((width, 4 * width), BF16),
            jax.ShapeDtypeStruct((1, width), F32),
            jax.ShapeDtypeStruct((1, width), F32),
        ),
        scratch_shapes=[
            pltpu.VMEM((length, width), F32),
            pltpu.VMEM((length, width), BF16),
            pltpu.VMEM((pairs, length, lanes), BF16),
            pltpu.VMEM((3 * pairs, length, lanes), BF16),
            pltpu.VMEM((length, width), BF16),
            pltpu.VMEM((length, lanes), F32),
            pltpu.VMEM((length, lanes), F32),
        ],
        compiler_params=pltpu.CompilerParams(vmem_limit_bytes=VMEM_LIMIT),
        cost_estimate=SMALL_COST,
        name="attention_backward",
    )(gm0, gm1, cot, x, attn, ctx, qkv, lse, wqkv, wo, g1, g2, *waits)


def group_reduce(rows, mem, op, fill):
    result = jnp.zeros_like(rows)
    for k in range(mem.shape[0]):
        inside = mem[k:k + 1, :] > 0
        part = jnp.where(inside, rows, fill)
        shift = rows.shape[1] // 2
        while shift >= PB:
            part = op(part, pltpu.roll(part, shift, 1))
            shift //= 2
        result = jnp.where(inside, part, result)
    return result


def gelu_both(v):
    square = v * v
    tanh = jnp.tanh(0.7978845608028654 * v * (1.0 + 0.044715 * square))
    half = 0.5 * (1.0 + tanh)
    slope = half + v * (1.0 - tanh * tanh) * (0.3989422804014327 + 0.0535161223274472 * square)
    return v * half, slope


def start(copy):
    copy.start()


def wait(copy):
    copy.wait()


def arrivals(z, sources, sems, base, act, place):
    if len(sources) == 1:
        act(pltpu.make_async_copy(*place(sources[0], None), sems.at[base]))
        return
    n = (len(sources) + 1) // 2
    act(pltpu.make_async_copy(*place(sources[0], z), sems.at[base]))
    for k in range(1, n):
        @pl.when(z >= k)
        def _():
            act(pltpu.make_async_copy(*place(sources[k], z - k), sems.at[base + k]))

        @pl.when(z + k < n)
        def _():
            act(pltpu.make_async_copy(*place(sources[n - 1 + k], z + k), sems.at[base + n - 1 + k]))


def x_rows(xs, m, q, sl):
    planes, nb, quarters, piece, width = xs.shape
    return jnp.concatenate([xs[m * sl + s, :, q].reshape(nb * piece, width) for s in range(sl)], 0)


def g_rows(gs, m, q, sl):
    quarters, nb, planes, piece, width = gs.shape
    return jnp.concatenate([gs[q, :, m * sl + s].reshape(nb * piece, width) for s in range(sl)], 0)


def mixture_forward_kernel(chunk, parts, waits, z_ref, *refs):
    x_in, refs = refs[:parts], refs[parts + waits:]
    (a_in, ctrl_ref, mem_ref, mkl_ref, take_ref, w1_ref, w2_ref,
     spread_ref, mixed_ref, hid_ref, slope_ref, eo_ref, weights_ref, gates_ref,
     xs, attn, logits, sems) = refs
    planes, nb, quarters, piece, width = xs.shape
    micro = mem_ref.shape[0]
    sl = planes // micro
    experts = mixed_ref.shape[0]
    rows = mkl_ref.shape[1]
    e = pl.program_id(0)
    z = z_ref[0]
    x_place = lambda ref, plane: (ref, xs if plane is None else xs.at[plane])
    a_copy = pltpu.make_async_copy(a_in.at[:, 1 + chunk], attn, sems.at[parts])

    @pl.when(e == 0)
    def _():
        arrivals(z, x_in, sems, 0, start, x_place)
        a_copy.start()
        arrivals(z, x_in, sems, 0, wait, x_place)
        for m in range(micro):
            for q in range(quarters):
                logits[m, q * 8:(q + 1) * 8, :] = dot_nt(ctrl_ref[...], x_rows(xs, m, q, sl))[:8]
            mem = mem_ref[m]
            taking = take_ref[m] > 0
            values = logits[m]
            high = group_reduce(jnp.where(taking, values, NEG_FILL), mem, jnp.maximum, NEG_FILL)
            scaled = jnp.where(taking, jnp.exp(values - high), 0.0)
            gates_ref[m] = scaled / group_reduce(scaled, mem, jnp.add, 0.0)
        for m in range(micro):
            for q in range(quarters):
                block = m * quarters + q
                own = gates_ref[m, q * 8:(q + 1) * 8, :]
                w = jnp.concatenate(
                    [(mkl_ref[m] * own[j:j + 1, :]).astype(BF16) for j in range(experts)], 0)
                weights_ref[block] = w
                blended = dot_nn(w, x_rows(xs, m, q, sl)).astype(BF16)
                for j in range(experts):
                    mixed_ref[j, block * rows:(block + 1) * rows, :] = blended[j * rows:(j + 1) * rows]

    value, slope = gelu_both(dot_nn(mixed_ref[e], w1_ref[0]))
    hidden = value.astype(BF16)
    hid_ref[0] = hidden
    slope_ref[0] = slope.astype(BF16)
    eo_ref[e] = dot_nn(hidden, w2_ref[0]).astype(BF16)

    @pl.when(e == experts - 1)
    def _():
        for m in range(micro):
            for q in range(quarters):
                block = m * quarters + q
                outs = jnp.concatenate(
                    [eo_ref[j, block * rows:(block + 1) * rows, :] for j in range(experts)], 0)
                spread = dot_tn(weights_ref[block], outs).astype(BF16)
                for s in range(sl):
                    at = slice(s * nb * PB, (s + 1) * nb * PB)
                    spread_ref[q, :, 0, m * sl + s] = spread[at].reshape(nb, PB, width)
        a_copy.wait()
        for q in range(quarters):
            mine = spread_ref[q, :, 0, z].astype(F32) + attn[:, q].astype(F32)
            spread_ref[q, :, 0, z] = mine.astype(BF16)


def mixture_backward_kernel(chunk, parts, waits, z_ref, *refs):
    x_in, g_in, refs = refs[:parts], refs[parts:2 * parts], refs[2 * parts + waits:]
    (ctrl_ref, mem_ref, mkl_ref, weights_ref, gates_ref, eo_ref, slope_ref, w1_ref, w2_ref,
     gm_ref, geo_ref, gpre_ref, dctrl_ref, xs, gs, gmx, sems) = refs
    planes, nb, quarters, piece, width = xs.shape
    micro, _, lanes = mem_ref.shape
    sl = planes // micro
    experts = geo_ref.shape[0]
    rows = mkl_ref.shape[1]
    e = pl.program_id(0)
    z = z_ref[0]
    mine = pl.ds(chunk * PB, PB)
    x_place = lambda ref, plane: (ref, xs if plane is None else xs.at[plane])
    g_place = lambda ref, plane: (ref.at[..., mine, :], gs if plane is None else gs.at[plane])

    @pl.when(e == 0)
    def _():
        arrivals(z, g_in, sems, 0, start, g_place)
        arrivals(z, x_in, sems, parts, start, x_place)
        arrivals(z, g_in, sems, 0, wait, g_place)
        for m in range(micro):
            for q in range(quarters):
                block = m * quarters + q
                grads = dot_nn(weights_ref[block], g_rows(gs, m, q, sl)).astype(BF16)
                for j in range(experts):
                    geo_ref[j, block * rows:(block + 1) * rows, :] = grads[j * rows:(j + 1) * rows]
        arrivals(z, x_in, sems, parts, wait, x_place)

    grad_pre = (dot_nt(geo_ref[e], w2_ref[0]) * slope_ref[0].astype(F32)).astype(BF16)
    gpre_ref[0] = grad_pre
    gmx[e] = dot_nt(grad_pre, w1_ref[0]).astype(BF16)

    @pl.when(e == experts - 1)
    def _():
        dctrl = jnp.zeros(dctrl_ref.shape, F32)
        ctrl8 = ctrl_ref[...].astype(F32)[:8]
        ctrl_twice = jnp.concatenate([ctrl8, ctrl8], 0).astype(BF16)
        for m in range(micro):
            for q in range(quarters):
                block = m * quarters + q
                at = slice(block * rows, (block + 1) * rows)
                outs = jnp.concatenate([eo_ref[j, at, :] for j in range(experts)], 0)
                backs = jnp.concatenate([gmx[j, at, :] for j in range(experts)], 0)
                w = weights_ref[block]
                inputs = x_rows(xs, m, q, sl)
                dots = dot_nt(outs, g_rows(gs, m, q, sl)) + dot_nt(backs, inputs)
                grad_gates = [
                    jnp.sum(dots[j * rows:(j + 1) * rows] * mkl_ref[m], 0, keepdims=True)
                    for j in range(experts)]
                if experts < 8:
                    grad_gates.append(jnp.zeros((8 - experts, lanes), F32))
                grad_gates = jnp.concatenate(grad_gates, 0)
                own = gates_ref[m, q * 8:(q + 1) * 8, :]
                inner = group_reduce(own * grad_gates, mem_ref[m], jnp.add, 0.0)
                grad_logits = own * (grad_gates - inner)
                upper = grad_logits.astype(BF16).astype(F32)
                both = jnp.concatenate([upper, grad_logits - upper], 0).astype(BF16)
                grad_mix = (dot_tn(w, backs) + dot_tn(both, ctrl_twice)).astype(BF16)
                for s in range(sl):
                    part = slice(s * nb * PB, (s + 1) * nb * PB)
                    gm_ref[m * sl + s, :, q] = grad_mix[part].reshape(nb, PB, width)
                dctrl += dot_nn(both, inputs)
        dctrl_ref[...] = dctrl


def whole(shape):
    return pl.BlockSpec(shape, lambda e: (0,) * len(shape))


def by_expert(shape):
    return pl.BlockSpec((1,) + shape[1:], lambda e: (e, 0, 0))


def mixture_sizes(x_parts, mem, mkl, w1):
    nb, quarters, piece, width = x_parts[0].shape[-4:]
    planes = quarters
    experts, _, hidden_size = w1.shape
    total = mem.shape[0] * quarters * mkl.shape[1]
    back = (planes, nb, quarters, piece, width)
    return back, (experts, total, width), (experts, total, hidden_size)


def mixture_forward(chunk, z, x_parts, a_all, ctrl, mem, mkl, take, w1, w2, waits=()):
    back, narrow, wide = mixture_sizes(x_parts, mem, mkl, w1)
    micro, _, lanes = mem.shape
    quarters = back[2]
    weights = (micro * quarters, narrow[0] * mkl.shape[1], lanes)
    gates = (micro, quarters * 8, lanes)
    any_spec = pl.BlockSpec(memory_space=pl.ANY)
    return pl.pallas_call(
        functools.partial(mixture_forward_kernel, chunk, len(x_parts), len(waits)),
        grid=(narrow[0],),
        input_output_aliases={1 + len(x_parts): 0} if chunk else {},
        out_shape=(
            jax.ShapeDtypeStruct(back[:2] + (CHUNKS,) + back[2:], BF16),
            jax.ShapeDtypeStruct(narrow, BF16),
            jax.ShapeDtypeStruct(wide, BF16),
            jax.ShapeDtypeStruct(wide, BF16),
            jax.ShapeDtypeStruct(narrow, BF16),
            jax.ShapeDtypeStruct(weights, BF16),
            jax.ShapeDtypeStruct(gates, F32),
        ),
        in_specs=[pl.BlockSpec(memory_space=pltpu.SMEM)]
        + [any_spec] * (len(x_parts) + len(waits) + 1)
        + [whole(ctrl.shape), whole(mem.shape), whole(mkl.shape), whole(take.shape),
           by_expert(w1.shape), by_expert(w2.shape)],
        out_specs=(pl.BlockSpec(back[:2] + (1,) + back[2:], lambda e: (0, 0, chunk, 0, 0, 0)), whole(narrow), by_expert(wide), by_expert(wide),
                   whole(narrow), whole(weights), whole(gates)),
        scratch_shapes=[
            pltpu.VMEM(back, BF16),
            pltpu.VMEM(back[1:], BF16),
            pltpu.VMEM(gates, F32),
            pltpu.SemaphoreType.DMA((len(x_parts) + 1,)),
        ],
        compiler_params=pltpu.CompilerParams(vmem_limit_bytes=VMEM_LIMIT),
        cost_estimate=SMALL_COST,
        name="mixture_forward",
    )(z, *x_parts, *waits, a_all, ctrl, mem, mkl, take, w1, w2)


def mixture_backward(chunk, z, x_parts, g_parts, ctrl, mem, mkl, weights, gates, eo, slope, w1, w2, waits=()):
    back, narrow, wide = mixture_sizes(x_parts, mem, mkl, w1)
    parts = len(x_parts)
    any_spec = pl.BlockSpec(memory_space=pl.ANY)
    return pl.pallas_call(
        functools.partial(mixture_backward_kernel, chunk, parts, len(waits)),
        grid=(narrow[0],),
        out_shape=(
            jax.ShapeDtypeStruct(back, BF16),
            jax.ShapeDtypeStruct(narrow, BF16),
            jax.ShapeDtypeStruct(wide, BF16),
            jax.ShapeDtypeStruct((16, back[4]), F32),
        ),
        in_specs=[pl.BlockSpec(memory_space=pltpu.SMEM)]
        + [any_spec] * (2 * parts + len(waits))
        + [whole(ctrl.shape), whole(mem.shape), whole(mkl.shape), whole(weights.shape),
           whole(gates.shape), whole(narrow), by_expert(wide), by_expert(w1.shape), by_expert(w2.shape)],
        out_specs=(whole(back), whole(narrow), by_expert(wide), whole((16, back[4]))),
        scratch_shapes=[
            pltpu.VMEM(back, BF16),
            pltpu.VMEM(back, BF16),
            pltpu.VMEM(narrow, BF16),
            pltpu.SemaphoreType.DMA((2 * parts,)),
        ],
        compiler_params=pltpu.CompilerParams(vmem_limit_bytes=VMEM_LIMIT),
        cost_estimate=SMALL_COST,
        name="mixture_backward",
    )(z, *x_parts, *g_parts, *waits, ctrl, mem, mkl, weights, gates, eo, slope, w1, w2)


def weight_grads_kernel(z_ref, m0, m1, p0, p1, h0, h1, o0, o1, *refs):
    keep_ref, send_ref = refs[-2:]
    width, step = keep_ref.shape[-2:]
    crossed = pl.program_id(0) >= pl.num_programs(0) // 2
    core = lax.rem(z_ref[1], 2)
    left1 = m0[0].T, m1[0].T
    left2 = o0[0].T, o1[0].T
    for t in range(p0.shape[2] // step // 2):
        x, y = t % 2, t // 2
        hop1, hop2 = jnp.where(crossed, y, x), jnp.where(crossed, x, y)
        for ref, part in ((keep_ref, core), (send_ref, 1 - core)):
            at = pl.ds(pl.multiple_of((2 * t + part) * step, step), step)
            first = dot_nn(left1[0], p0[0, :, at]) + dot_nn(left1[1], p1[0, :, at])
            ref[0, 0, hop1, hop2, 0] = first.astype(BF16)
            second = dot_nn(left2[0], h0[0, :, at]) + dot_nn(left2[1], h1[0, :, at])
            ref[0, 0, hop1, hop2, 1] = second.astype(BF16)


def weight_grads(z, mixed, gpre, hid, geo, nb, waits=()):
    experts, total, width = mixed[0].shape
    hidden_size = gpre[0].shape[2]
    step = hidden_size // nb
    half = experts // 2
    row = pl.BlockSpec((1, total, width), lambda e: (e, 0, 0))
    wide = pl.BlockSpec((1, total, hidden_size), lambda e: (e, 0, 0))
    out = pl.BlockSpec((1, 1, 2, 2, 2, width, step), lambda e: (e // half, e % half, 0, 0, 0, 0, 0))
    return pl.pallas_call(
        weight_grads_kernel,
        grid=(experts,),
        in_specs=[pl.BlockSpec(memory_space=pltpu.SMEM)]
        + [row] * 2 + [wide] * 4 + [row] * 2 + [pl.BlockSpec(memory_space=pl.ANY)] * len(waits),
        out_shape=(jax.ShapeDtypeStruct((2, half, 2, 2, 2, width, step), BF16),) * 2,
        out_specs=(out, out),
        compiler_params=pltpu.CompilerParams(vmem_limit_bytes=VMEM_LIMIT),
        cost_estimate=SMALL_COST,
        name="weight_grads",
    )(z, *mixed, *gpre, *hid, *geo, *waits)


def pick(parts, index):
    return lax.dynamic_index_in_dim(parts, index, 0, keepdims=False)


def pass_on(*refs):
    pass


def after(value, *others):
    spec = pl.BlockSpec(memory_space=pl.ANY)
    return pl.pallas_call(
        pass_on,
        out_shape=jax.ShapeDtypeStruct(value.shape, value.dtype),
        in_specs=[spec] * (1 + len(others)),
        out_specs=spec,
        input_output_aliases={0: 0},
        name="after",
        cost_estimate=SMALL_COST,
    )(value, *others)


def line_step(ups, downs, count):
    up = [(i, i + 1) for i in range(count - 1)]
    down = [(i + 1, i) for i in range(count - 1)]
    return (ups + [lax.ppermute(ups[-1], "expert", up)],
            downs + [lax.ppermute(downs[-1], "expert", down)])


def line_scatter(parts, z, count):
    up = [(i, i + 1) for i in range(count - 1)]
    down = [(i + 1, i) for i in range(count - 1)]

    def own(index):
        return pick(parts, jnp.clip(index, 0, count - 1)).astype(F32)

    rising, falling = own(z + count - 1).astype(BF16), own(z - count + 1).astype(BF16)
    for step in range(1, count):
        rising = lax.ppermute(rising, "expert", up).astype(F32)
        falling = lax.ppermute(falling, "expert", down).astype(F32)
        if step < count - 1:
            rising = (rising + own(z + count - 1 - step)).astype(BF16)
            falling = (falling + own(z - count + 1 + step)).astype(BF16)
    return (rising + falling + own(z)).astype(BF16)


def for_planes(parts, z, count):
    return [pick(parts, lax.rem(z + k, count)) for k in range(count)]


def to_planes(picked, count):
    got = picked[:1]
    for k in range(1, count):
        got.append(lax.ppermute(picked[k], "expert", [(i, (i + k) % count) for i in range(count)]))
    return got


def swap_halves(blocks, bit, count):
    mine = lax.rem(lax.axis_index("batch") >> bit, 2)
    other = lax.ppermute(pick(blocks, 1 - mine), "batch", [(i, i ^ (1 << bit)) for i in range(count)])
    return (pick(blocks, mine).astype(F32) + other.astype(F32)).astype(BF16)


def hop_bits(half):
    return (1, 2) if half == 0 else (2, 1)


def add_blocks(*refs):
    total = refs[0][...].astype(F32)
    for ref in refs[1:]:
        total += ref[...].reshape(total.shape).astype(F32)
    return total


def first_sends_kernel(pos_ref, *refs):
    ins, outs = refs[:8], refs[-4:]
    for i, out in enumerate(outs):
        out[...] = add_blocks(*ins[2 * i:2 * i + 2]).astype(BF16).reshape(out.shape)


def first_sends(pos, keep, came, waits=()):
    halves, experts, _, _, _, rows, cols = keep.shape
    pieces = [(i, e) for i in range(halves) for e in range(experts)]

    def place(i, e):
        bit = hop_bits(i)[0]
        return lambda h, w, pos: (i, e, 1 - lax.rem(pos[1] >> bit, 2), h, w, 0, 0)

    block = (1, 1, 1, 1, 1, rows, cols)
    out = pl.BlockSpec((1, 1, rows, cols), lambda h, w, pos: (h, w, 0, 0))
    return pl.pallas_call(
        first_sends_kernel,
        grid_spec=pltpu.PrefetchScalarGridSpec(
            num_scalar_prefetch=1, grid=(2, 2),
            in_specs=[pl.BlockSpec(block, place(i, e)) for i, e in pieces for _ in range(2)]
            + [pl.BlockSpec(memory_space=pl.ANY)] * len(waits),
            out_specs=(out,) * len(pieces)),
        out_shape=(jax.ShapeDtypeStruct((2, 2, rows, cols), BF16),) * len(pieces),
        compiler_params=pltpu.CompilerParams(vmem_limit_bytes=VMEM_LIMIT),
        cost_estimate=SMALL_COST,
        name="first_sends",
    )(pos, *[array for _ in pieces for array in (keep, came)], *waits)


def second_sends_kernel(pos_ref, *refs):
    ins, outs = refs[:-4], refs[-4:]
    for i, out in enumerate(outs):
        out[...] = add_blocks(*ins[3 * i:3 * i + 3]).astype(BF16).reshape(out.shape)


def own_place(i, e, last):
    first, second = hop_bits(i)

    def place(w, pos):
        mine = lax.rem(pos[1] >> second, 2)
        return (i, e, lax.rem(pos[1] >> first, 2), jnp.where(last == 1, 1 - mine, mine), w, 0, 0)

    def place_got(w, pos):
        return place(w, pos)[3:]

    return place, place_got


def second_sends(pos, keep, came, got):
    halves, experts, _, _, _, rows, cols = keep.shape
    pieces = [(i, e) for i in range(halves) for e in range(experts)]
    specs = []
    for i, e in pieces:
        place, place_got = own_place(i, e, 1)
        specs += [pl.BlockSpec((1, 1, 1, 1, 1, rows, cols), place)] * 2
        specs += [pl.BlockSpec((1, 1, rows, cols), place_got)]
    out = pl.BlockSpec((1, rows, cols), lambda w, pos: (w, 0, 0))
    return pl.pallas_call(
        second_sends_kernel,
        grid_spec=pltpu.PrefetchScalarGridSpec(
            num_scalar_prefetch=1, grid=(2,), in_specs=specs, out_specs=(out,) * len(pieces)),
        out_shape=(jax.ShapeDtypeStruct((2, rows, cols), BF16),) * len(pieces),
        compiler_params=pltpu.CompilerParams(vmem_limit_bytes=VMEM_LIMIT),
        cost_estimate=SMALL_COST,
        name="second_sends",
    )(pos, *[array for n in range(len(pieces)) for array in (keep, came, got[n])])


def expert_sums_kernel(pos_ref, *refs):
    ins, (first_ref, second_ref) = refs[:-2], refs[-2:]
    for i in range(len(ins) // 4):
        total = add_blocks(*ins[4 * i:4 * i + 4]).reshape(ins[4 * i].shape[-3:])
        first_ref[i] = total[0]
        second_ref[i] = total[1].T


def expert_sums(pos, keep, came, got, got_last):
    halves, experts, _, _, _, rows, cols = keep.shape
    pieces = [(i, e) for i in range(halves) for e in range(experts)]
    specs = []
    for i, e in pieces:
        place, place_got = own_place(i, e, 0)
        specs += [pl.BlockSpec((1, 1, 1, 1, 2, rows, cols), place)] * 2
        specs += [pl.BlockSpec((1, 2, rows, cols), place_got)]
        specs += [pl.BlockSpec((2, rows, cols), lambda w, pos: (0, 0, 0))]
    out = lambda shape: pl.BlockSpec(shape, lambda w, pos: (0, 0, 0))
    shapes = (len(pieces), rows, cols), (len(pieces), cols, rows)
    return pl.pallas_call(
        expert_sums_kernel,
        grid_spec=pltpu.PrefetchScalarGridSpec(
            num_scalar_prefetch=1, grid=(1,), in_specs=specs, out_specs=tuple(out(s) for s in shapes)),
        out_shape=tuple(jax.ShapeDtypeStruct(s, F32) for s in shapes),
        compiler_params=pltpu.CompilerParams(vmem_limit_bytes=VMEM_LIMIT),
        cost_estimate=SMALL_COST,
        name="expert_sums",
    )(pos, *[array for n in range(len(pieces)) for array in (keep, came, got[n], got_last[n])])


def cross(block, bit):
    return lax.ppermute(block, "batch", [(j, j ^ (1 << bit)) for j in range(8)])


def add_home_kernel(z_ref, *refs):
    n = len(refs) - 4
    parts, (base_ref, out_ref, came, sems) = refs[:n], refs[n:]
    copies = [
        pltpu.make_async_copy(parts[k], came.at[lax.rem(z_ref[0] - k + n, n)], sems.at[k]) for k in range(n)]
    for copy in copies:
        copy.start()
    for copy in copies:
        copy.wait()
    out_ref[...] = base_ref[...] + came[...].astype(F32)


def add_home(z, parts, base):
    vmem = pl.BlockSpec(memory_space=pltpu.VMEM)
    return pl.pallas_call(
        add_home_kernel,
        out_shape=jax.ShapeDtypeStruct(base.shape, F32),
        in_specs=[pl.BlockSpec(memory_space=pltpu.SMEM)] + [pl.BlockSpec(memory_space=pl.ANY)] * len(parts) + [vmem],
        scratch_shapes=[pltpu.VMEM(base.shape, BF16), pltpu.SemaphoreType.DMA((len(parts),))],
        compiler_params=pltpu.CompilerParams(vmem_limit_bytes=VMEM_LIMIT),
        cost_estimate=SMALL_COST,
        name="add_home",
    )(z, *parts, base)


def body(
    tokens,
    cotangent,
    query_key_value_weight,
    output_weight,
    controller_weight,
    w_first,
    w_second,
    gain_one,
    gain_two,
    group_sizes,
    live,
):
    micro, sl, local_len, width = tokens.shape
    planes = lax.axis_size("expert")
    nb = lax.axis_size("batch")
    experts = w_first.shape[0]
    seqs = live.shape[1]
    z = lax.axis_index("expert")
    piece = local_len // nb
    if micro * sl != planes or piece != CHUNKS * PB or nb != 8:
        return body_by_position(
            tokens, cotangent, query_key_value_weight, output_weight, controller_weight,
            w_first, w_second, gain_one, gain_two, group_sizes, live)
    g1, g2 = gain_one.reshape(1, width), gain_two.reshape(1, width)

    own = lax.axis_index("batch")
    z_arr = jnp.stack([z, own]).astype(jnp.int32)
    x_parts = to_planes(for_planes(tokens.reshape(planes, local_len, width).astype(BF16), z, planes), planes)

    cot = cotangent.reshape(planes, nb, piece, width)
    pieces = []
    for k in range(nb):
        part = lax.dynamic_index_in_dim(cot, own ^ k, 1, keepdims=False).astype(BF16)
        if k:
            part = lax.ppermute(part, "batch", [(i, i ^ k) for i in range(nb)])
        pieces.append(part)
    pieces[-1] = after(pieces[-1], x_parts[2])
    cot = jnp.take(jnp.stack(pieces), own ^ jnp.arange(nb), axis=0)
    g_all = lax.all_gather(cot, "expert", axis=0, tiled=False)

    x, qkv, lse, ctx, attn, mix, more = attention_forward(
        z_arr, x_parts, query_key_value_weight, output_weight, g1, g2, nb, waits=(cot,))

    member, taking = jax.vmap(group_tables)(group_sizes, live)
    groups = member.shape[2]
    mem = member.reshape(micro, nb, sl, groups).transpose(0, 3, 2, 1).reshape(micro, groups, seqs)
    mem = jnp.repeat(mem.astype(F32), PB, axis=2)
    take = taking.reshape(micro, nb, sl).transpose(0, 2, 1).reshape(micro, 1, seqs)
    take = jnp.repeat(take.astype(F32), PB, axis=2)
    place = jnp.arange(seqs * PB, dtype=jnp.int32) % PB
    same = (jnp.arange(PB, dtype=jnp.int32)[:, None] == place[None, :]).astype(F32)
    mkl = (mem[:, :, None, :] * same).reshape(micro, groups * PB, seqs * PB)
    ctrl = lax.dynamic_slice_in_dim(controller_weight, z * experts, experts, 1).T
    ctrl = jnp.pad(ctrl, ((0, 16 - experts), (0, 0)))

    def over_batch(block):
        return lax.all_to_all(block, "batch", split_axis=0, concat_axis=0, tiled=True)

    def over_expert(blocks):
        return lax.all_to_all(blocks, "expert", split_axis=0, concat_axis=0, tiled=True)

    own0 = over_batch(mix)
    x0 = [lax.all_gather(own0, "expert", axis=0, tiled=False)]
    more = over_batch(after(more, own0))
    x1 = [lax.all_gather(more[:, 0], "expert", axis=0, tiled=False)]
    g_parts = [g_all]

    cot_own = lax.dynamic_index_in_dim(g_all, z, 2, keepdims=False).transpose(1, 0, 2, 3)
    cot_own = over_batch(cot_own)
    spread0, mixed0, hid0, slope0, eo0, weights0, gates0 = mixture_forward(
        0, z_arr, x0, more, ctrl, mem, mkl, take, w_first, w_second, waits=(cot_own,))
    back0, geo0, gpre0, dctrl0 = mixture_backward(
        0, z_arr, x0, g_parts, ctrl, mem, mkl, weights0, gates0, eo0, slope0, w_first, w_second,
        waits=())
    back0 = lax.psum_scatter(after(back0, x1[0]), "expert", scatter_dimension=0, tiled=False)
    spread, mixed1, hid1, slope1, eo1, weights1, gates1 = mixture_forward(
        1, z_arr, x1, more, ctrl, mem, mkl, take, w_first, w_second, waits=(spread0, dctrl0))
    back1, geo1, gpre1, dctrl1 = mixture_backward(
        1, z_arr, x1, g_parts, ctrl, mem, mkl, weights1, gates1, eo1, slope1, w_first, w_second)
    dctrl = dctrl0[:8] + dctrl0[8:] + dctrl1[:8] + dctrl1[8:]
    back1 = lax.psum_scatter(after(back1, back0), "expert", scatter_dimension=0, tiled=False)
    back0 = over_batch(back0)
    keep, send = weight_grads(
        z_arr, (mixed0, mixed1), (gpre0, gpre1), (hid0, hid1), (geo0, geo1), nb, waits=(back0,))
    spread = lax.psum_scatter(after(spread, back1), "expert", scatter_dimension=0, tiled=False)
    send = after(send, back1)
    back1 = over_batch(back1)
    came = lax.ppermute(send, "batch", [(i, i ^ 1) for i in range(nb)])
    sends = first_sends(z_arr, keep, came, waits=(back1,))
    gin, dw, dg1, dg2 = attention_backward(
        back0, back1, cot_own, x, attn, ctx, qkv, lse, query_key_value_weight, output_weight, g1, g2,
        waits=sends)
    firsts = [hop_bits(n // 2)[0] for n in range(4)]
    got = [cross(sends[n], firsts[n]) for n in range(4)]
    parts = to_planes(for_planes(gin.reshape(planes, local_len, width), z, planes), planes)
    seconds = second_sends(z_arr, keep, came, got)
    dw = after(dw, seconds[0])
    got_last = [cross(part, hop_bits(n // 2)[1]) for n, part in enumerate(seconds)]
    grad_first, grad_second = expert_sums(z_arr, keep, came, got, got_last)

    grad_in = add_home(z_arr, parts, cotangent.reshape(planes, local_len, width)).reshape(tokens.shape)

    dctrl_all = jnp.zeros((planes, experts, width), F32)
    dctrl_all = lax.dynamic_update_slice(dctrl_all, dctrl[None, :experts], (z, 0, 0))
    dctrl_all = dctrl_all.reshape(planes * experts, width).T
    extra = jnp.concatenate([dctrl_all, dg1.T, dg2.T], 1)
    extra = jnp.pad(extra, ((0, 0), (0, 128 - extra.shape[1]))).astype(BF16)
    flat = jnp.concatenate([dw, extra], 1)
    flat = flat.reshape(nb // 2, 2, -1, flat.shape[1]).transpose(1, 0, 2, 3)
    flat = swap_halves(flat, 0, nb)
    chips = [[c + 2 * i for i in range(nb // 2)] for c in range(2)]
    flat = lax.all_to_all(flat, "batch", split_axis=0, concat_axis=0, tiled=True, axis_index_groups=chips)
    flat = jnp.sum(flat.astype(F32), 0).astype(BF16)
    flat = after(flat, grad_in)
    spread = over_batch(after(spread, flat, *got_last))
    out = tokens + spread.transpose(2, 0, 1, 3, 4).reshape(tokens.shape).astype(F32)
    flat = flat.reshape(planes, -1, flat.shape[1])
    flat = lax.all_to_all(flat, "expert", split_axis=0, concat_axis=0, tiled=True)
    flat = jnp.sum(flat.astype(F32), 0)
    ends = [3 * width, 4 * width, 4 * width + planes * experts]
    grad_qkv, grad_out, grad_ctrl = flat[:, :ends[0]], flat[:, ends[0]:ends[1]], flat[:, ends[1]:ends[2]]
    return (out, grad_in, grad_qkv, grad_out, grad_ctrl, grad_first, grad_second,
            flat[:, ends[2]], flat[:, ends[2] + 1])


def solution(mesh):
    placed = (
        P(None, "batch", "expert", None),
        P(None, "batch", "expert", None),
        P(),
        P(),
        P(),
        P("expert", None, None),
        P("expert", None, None),
        P(),
        P(),
        P(),
        P(),
    )
    return jax.shard_map(
        body,
        mesh=mesh,
        in_specs=placed,
        out_specs=(
            P(None, "batch", "expert", None),
            P(None, "batch", "expert", None),
            P(("batch", "expert"), None),
            P(("batch", "expert"), None),
            P(("batch", "expert"), None),
            P("expert", None, "batch"),
            P("expert", "batch", None),
            P(("batch", "expert")),
            P(("batch", "expert")),
        ),
        check_vma=False,
    )
```

```python
import functools

import jax
import jax.numpy as jnp
from jax import lax
from jax.experimental import pallas as pl
from jax.experimental.pallas import tpu as pltpu
from jax.sharding import PartitionSpec as P

HEADS = 8


HIGH_PRECISION = lax.Precision.HIGHEST
NEG_FILL = -1e30


def group_tables(group_row, live_row):
    seq_count = live_row.shape[0]
    group_ends = jnp.cumsum(group_row)
    group_starts = group_ends - group_row
    numbers = jnp.arange(seq_count, dtype=jnp.int32)
    member = (numbers[:, None] >= group_starts[None, :]) & (numbers[:, None] < group_ends[None, :])
    leading = jnp.any(numbers[:, None] == group_starts[None, :], axis=1)
    taking = (live_row > 0) | leading
    return (member, taking)


def group_softmax(router_logits, member, taking):
    inside = member[:, :, None, None]
    masked = jnp.where(taking[:, None, None], router_logits, NEG_FILL)
    highest = jnp.max(jnp.where(inside, masked[:, None], NEG_FILL), axis=0)
    row_high = jnp.sum(jnp.where(inside, highest[None], 0.0), axis=1)
    scaled = jnp.where(taking[:, None, None], jnp.exp(router_logits - row_high), 0.0)
    group_sums = jnp.sum(jnp.where(inside, scaled[:, None], 0.0), axis=0)
    row_sums = jnp.sum(jnp.where(inside, group_sums[None], 0.0), axis=1)
    return scaled / row_sums


def norm_forward(values_in, scaling):
    centred = values_in - jnp.mean(values_in, -1, keepdims=True)
    inverse = lax.rsqrt(jnp.mean(centred * centred, -1, keepdims=True) + 1e-05)
    normed = centred * inverse
    return (normed * scaling, normed, inverse)


def norm_backward(incoming, normed, inverse, scaling):
    scaled_grad = incoming * scaling
    returned_grad = inverse * (
        scaled_grad
        - jnp.mean(scaled_grad, -1, keepdims=True)
        - normed * jnp.mean(scaled_grad * normed, -1, keepdims=True)
    )
    return (returned_grad, jnp.sum(incoming * normed, axis=(0, 1)))


def attention_probs(query_heads, key_heads, causal, logsum, factor):
    scores = (
        jnp.einsum("sqhc,skhc->shqk", query_heads, key_heads, preferred_element_type=jnp.float32)
        * factor
    )
    return jnp.where(causal, jnp.exp(scores - logsum), 0.0)


def body_by_position(
    tokens,
    cotangent,
    query_key_value_weight,
    output_weight,
    controller_weight,
    w_first,
    w_second,
    gain_one,
    gain_two,
    group_sizes,
    live,
):
    micro_count, seq_here, local_len, model_width = tokens.shape
    head_dim = model_width // HEADS
    factor = head_dim ** (-0.5)
    length = local_len * lax.axis_size("expert")
    query_pos = lax.axis_index("expert") * local_len + jnp.arange(local_len, dtype=jnp.int32)
    key_pos = jnp.arange(length, dtype=jnp.int32)
    causal = key_pos[None, :] <= query_pos[:, None]
    ctrl_wide = controller_weight.astype(jnp.float32)
    sum_first = jnp.zeros(w_first.shape, jnp.float32)
    sum_second = jnp.zeros(w_second.shape, jnp.float32)
    sum_qkv = jnp.zeros(query_key_value_weight.shape, jnp.float32)
    sum_out = jnp.zeros(output_weight.shape, jnp.float32)
    sum_ctrl = jnp.zeros(controller_weight.shape, jnp.float32)
    sum_gain_one = jnp.zeros(gain_one.shape, jnp.float32)
    sum_gain_two = jnp.zeros(gain_two.shape, jnp.float32)
    outputs = []
    grads_in = []
    for micro_step in range(micro_count):
        member, taking = group_tables(group_sizes[micro_step], live[micro_step])
        input_rows = tokens[micro_step]
        attn_norm, normed_one, inverse_one = norm_forward(input_rows, gain_one)
        attention_input = attn_norm.astype(jnp.bfloat16)
        projected_rows = jnp.einsum(
            "mtg,gj->mtj",
            attention_input,
            query_key_value_weight,
            preferred_element_type=jnp.float32,
        ).astype(jnp.bfloat16)
        queries = projected_rows[..., :model_width]
        keys_here = projected_rows[..., model_width : 2 * model_width]
        values_here = projected_rows[..., 2 * model_width :]
        keys_all, values_all = (
            lax.all_gather(keys_here, "expert", axis=1, tiled=True),
            lax.all_gather(values_here, "expert", axis=1, tiled=True),
        )
        query_heads = queries.reshape(seq_here, local_len, HEADS, head_dim)
        key_heads = keys_all.reshape(seq_here, length, HEADS, head_dim)
        value_heads = values_all.reshape(seq_here, length, HEADS, head_dim)
        scores = (
            jnp.einsum(
                "sqhc,skhc->shqk", query_heads, key_heads, preferred_element_type=jnp.float32
            )
            * factor
        )
        scores = jnp.where(causal, scores, NEG_FILL)
        highest = jnp.max(scores, -1, keepdims=True)
        logsum = highest + jnp.log(jnp.sum(jnp.exp(scores - highest), -1, keepdims=True))
        probs_low = jnp.exp(scores - logsum).astype(jnp.bfloat16)
        context_rows = jnp.einsum(
            "shqk,skhc->sqhc", probs_low, value_heads, preferred_element_type=jnp.float32
        )
        context_rows = context_rows.reshape(seq_here, local_len, model_width).astype(jnp.bfloat16)
        residual_stream = input_rows + jnp.einsum(
            "mtg,gj->mtj", context_rows, output_weight, preferred_element_type=jnp.float32
        )
        mix_norm, normed_two, inverse_two = norm_forward(residual_stream, gain_two)
        mix_low = mix_norm.astype(jnp.bfloat16)
        mix_pos = lax.all_to_all(mix_low, "batch", split_axis=1, concat_axis=0, tiled=True)
        router_logits = jnp.einsum(
            "spd,de->spe", mix_pos, controller_weight, preferred_element_type=jnp.float32
        )
        gate_vals, gate_pull = jax.vjp(
            functools.partial(group_softmax, member=member, taking=taking), router_logits
        )
        weights_low = jnp.where(
            member[:, None, :, None],
            gate_vals.astype(jnp.bfloat16)[:, :, None, :],
            jnp.zeros((), jnp.bfloat16),
        )
        blended_rows = jnp.einsum(
            "spke,spd->pked", weights_low, mix_pos, preferred_element_type=jnp.float32
        ).astype(jnp.bfloat16)
        mixed_recv = lax.all_to_all(blended_rows, "expert", split_axis=2, concat_axis=0, tiled=True)
        pre_act = jnp.einsum(
            "pked,edf->pkef", mixed_recv, w_first, preferred_element_type=jnp.float32
        )
        activated, gelu_pull = jax.vjp(jax.nn.gelu, pre_act)
        act_low = activated.astype(jnp.bfloat16)
        expert_output = jnp.einsum(
            "pkef,efd->pked", act_low, w_second, preferred_element_type=jnp.float32
        ).astype(jnp.bfloat16)
        returned = lax.all_to_all(expert_output, "expert", split_axis=0, concat_axis=2, tiled=True)
        dispersed_rows = jnp.einsum(
            "spke,pked->spd", weights_low, returned, preferred_element_type=jnp.float32
        ).astype(jnp.bfloat16)
        spread_seq = lax.all_to_all(
            dispersed_rows, "batch", split_axis=0, concat_axis=1, tiled=True
        )
        outputs.append(residual_stream + spread_seq.astype(jnp.float32))
        cot_here = cotangent[micro_step]
        grad_spread = lax.all_to_all(
            cot_here.astype(jnp.bfloat16), "batch", split_axis=1, concat_axis=0, tiled=True
        )
        grad_weights = jnp.einsum(
            "spd,pked->spke", grad_spread, returned, preferred_element_type=jnp.float32
        )
        grad_eout = jnp.einsum(
            "spke,spd->pked", weights_low, grad_spread, preferred_element_type=jnp.float32
        ).astype(jnp.bfloat16)
        grad_eout_recv = lax.all_to_all(
            grad_eout, "expert", split_axis=2, concat_axis=0, tiled=True
        )
        grad_hidden = jnp.einsum(
            "pked,efd->pkef", grad_eout_recv, w_second, preferred_element_type=jnp.float32
        )
        step_second = jnp.einsum(
            "pkef,pked->efd", act_low, grad_eout_recv, preferred_element_type=jnp.float32
        )
        grad_pre = gelu_pull(grad_hidden)[0].astype(jnp.bfloat16)
        step_first = jnp.einsum(
            "pked,pkef->edf", mixed_recv, grad_pre, preferred_element_type=jnp.float32
        )
        sum_first = sum_first + step_first
        sum_second = sum_second + step_second
        grad_mixed = jnp.einsum(
            "pkef,edf->pked", grad_pre, w_first, preferred_element_type=jnp.float32
        ).astype(jnp.bfloat16)
        grad_mix_groups = lax.all_to_all(
            grad_mixed, "expert", split_axis=0, concat_axis=2, tiled=True
        )
        grad_weights = grad_weights + jnp.einsum(
            "pked,spd->spke", grad_mix_groups, mix_pos, preferred_element_type=jnp.float32
        )
        grad_gates = jnp.sum(jnp.where(member[:, None, :, None], grad_weights, 0.0), axis=2)
        grad_logits = gate_pull(grad_gates)[0]
        sum_ctrl = sum_ctrl + jnp.einsum(
            "spd,spe->de", mix_pos.astype(jnp.float32), grad_logits, precision=HIGH_PRECISION
        )
        grad_mix = jnp.einsum(
            "spke,pked->spd", weights_low, grad_mix_groups, preferred_element_type=jnp.float32
        )
        grad_mix = grad_mix + jnp.einsum(
            "spe,de->spd", grad_logits, ctrl_wide, precision=HIGH_PRECISION
        )
        grad_mix_seq = lax.all_to_all(
            grad_mix.astype(jnp.bfloat16), "batch", split_axis=0, concat_axis=1, tiled=True
        )
        grad_norm_two, gain_two_step = norm_backward(
            grad_mix_seq.astype(jnp.float32), normed_two, inverse_two, gain_two
        )
        sum_gain_two = sum_gain_two + gain_two_step
        grad_resid = cot_here + grad_norm_two
        attention_gradient = grad_resid.astype(jnp.bfloat16)
        sum_out = sum_out + jnp.einsum(
            "hui,huq->iq", context_rows, attention_gradient, preferred_element_type=jnp.float32
        )
        grad_context = jnp.einsum(
            "wfh,yh->wfy", attention_gradient, output_weight, preferred_element_type=jnp.float32
        ).astype(jnp.bfloat16)
        context_heads = grad_context.reshape(seq_here, local_len, HEADS, head_dim)
        probs_full = attention_probs(query_heads, key_heads, causal, logsum, factor)
        grad_probs = jnp.einsum(
            "sqhc,skhc->shqk", context_heads, value_heads, preferred_element_type=jnp.float32
        )
        row_dots = jnp.sum(grad_probs * probs_full, -1, keepdims=True)
        grad_scores = (probs_full * (grad_probs - row_dots)).astype(jnp.bfloat16)
        grad_query = (
            jnp.einsum(
                "shqk,skhc->sqhc", grad_scores, key_heads, preferred_element_type=jnp.float32
            )
            * factor
        )
        grad_query = grad_query.reshape(seq_here, local_len, model_width)
        key_terms = (
            jnp.einsum(
                "shqk,sqhc->skhc", grad_scores, query_heads, preferred_element_type=jnp.float32
            )
            * factor
        )
        value_terms = jnp.einsum(
            "shqk,sqhc->skhc",
            probs_full.astype(jnp.bfloat16),
            context_heads,
            preferred_element_type=jnp.float32,
        )
        grad_key, grad_value = (
            lax.psum_scatter(
                key_terms.reshape(seq_here, length, model_width).astype(jnp.bfloat16),
                "expert",
                scatter_dimension=1,
                tiled=True,
            ).astype(jnp.float32),
            lax.psum_scatter(
                value_terms.reshape(seq_here, length, model_width).astype(jnp.bfloat16),
                "expert",
                scatter_dimension=1,
                tiled=True,
            ).astype(jnp.float32),
        )
        query_key_value_row_gradient = jnp.concatenate(
            [grad_query, grad_key, grad_value], axis=-1
        ).astype(jnp.bfloat16)
        sum_qkv = sum_qkv + jnp.einsum(
            "hui,huq->iq",
            attention_input,
            query_key_value_row_gradient,
            preferred_element_type=jnp.float32,
        )
        grad_attn_in = jnp.einsum(
            "wfh,yh->wfy",
            query_key_value_row_gradient,
            query_key_value_weight,
            preferred_element_type=jnp.float32,
        )
        grad_norm_one, gain_one_step = norm_backward(
            grad_attn_in, normed_one, inverse_one, gain_one
        )
        sum_gain_one = sum_gain_one + gain_one_step
        grads_in.append(grad_resid + grad_norm_one)
    grad_first, grad_second = (
        lax.psum_scatter(
            sum_first.astype(jnp.bfloat16), "batch", scatter_dimension=2, tiled=True
        ).astype(jnp.float32),
        lax.psum_scatter(
            sum_second.astype(jnp.bfloat16), "batch", scatter_dimension=1, tiled=True
        ).astype(jnp.float32),
    )
    grad_qkv, grad_out, grad_ctrl, grad_gain_one, grad_gain_two = (
        lax.psum_scatter(sum_qkv, ("batch", "expert"), scatter_dimension=0, tiled=True),
        lax.psum_scatter(sum_out, ("batch", "expert"), scatter_dimension=0, tiled=True),
        lax.psum_scatter(sum_ctrl, ("batch", "expert"), scatter_dimension=0, tiled=True),
        lax.psum_scatter(sum_gain_one, ("batch", "expert"), scatter_dimension=0, tiled=True),
        lax.psum_scatter(sum_gain_two, ("batch", "expert"), scatter_dimension=0, tiled=True),
    )
    return (
        jnp.stack(outputs),
        jnp.stack(grads_in),
        grad_qkv,
        grad_out,
        grad_ctrl,
        grad_first,
        grad_second,
        grad_gain_one,
        grad_gain_two,
    )


F32 = jnp.float32
BF16 = jnp.bfloat16
PB = 16
CHUNKS = 2
VMEM_LIMIT = 60 * 1024 * 1024
KERNEL_COST = pl.CostEstimate(flops=30_000_000_000, bytes_accessed=100_000, transcendentals=0)
SMALL_COST = pl.CostEstimate(flops=1_000_000, bytes_accessed=100_000, transcendentals=0)


def dot_nn(a, b):
    return lax.dot_general(a, b, (((1,), (0,)), ((), ())), preferred_element_type=F32)


def dot_nt(a, b):
    return lax.dot_general(a, b, (((1,), (1,)), ((), ())), preferred_element_type=F32)


def dot_tn(a, b):
    return lax.dot_general(a, b, (((0,), (0,)), ((), ())), preferred_element_type=F32)


def row_norm(rows):
    centred = rows - jnp.mean(rows, -1, keepdims=True)
    inverse = lax.rsqrt(jnp.mean(centred * centred, -1, keepdims=True) + 1e-05)
    return centred * inverse, inverse


def row_norm_back(incoming, normed, inverse, gain):
    scaled = incoming * gain
    return inverse * (
        scaled
        - jnp.mean(scaled, -1, keepdims=True)
        - normed * jnp.mean(scaled * normed, -1, keepdims=True)
    )


def head_lanes(rows, lanes, head):
    lane = lax.broadcasted_iota(jnp.int32, (rows, lanes), 1)
    return (lane < lanes // 2) if head == 0 else (lane >= lanes // 2)


def causal_tile(size):
    key = lax.broadcasted_iota(jnp.int32, (size, size), 0)
    query = lax.broadcasted_iota(jnp.int32, (size, size), 1)
    return key <= query


def attention_forward_kernel(waits, z_ref, *refs):
    quarters = 4
    parts, refs = refs[:quarters], refs[:quarters] + refs[quarters + waits:]
    (wqkv_ref, wo_ref, g1_ref, g2_ref, x_ref, qkv_ref, lse_ref, ctx_ref, attn_ref, mix_ref, more_ref) = refs[quarters:-2]
    ctx_pairs, sems = refs[-2:]
    length, width = x_ref.shape
    pairs = HEADS // 2
    lanes = width // pairs
    half = lanes // 2
    nb = mix_ref.shape[0]
    tile = length // quarters
    factor = half ** (-0.5)
    copies = []
    for k in range(quarters):
        source = lax.rem(z_ref[0] - k + quarters, quarters)
        rows = pl.ds(pl.multiple_of(source * tile, tile), tile)
        copies.append(pltpu.make_async_copy(parts[k], x_ref.at[rows, :], sems.at[k]))
        copies[-1].start()
    for copy in copies:
        copy.wait()

    def project(i, carry):
        rows = pl.ds(pl.multiple_of(i * tile, tile), tile)
        normed, _ = row_norm(x_ref[rows, :].astype(F32))
        attn_in = (normed * g1_ref[...]).astype(BF16)
        for part in range(3):
            out = dot_nn(attn_in, wqkv_ref[:, part * width:(part + 1) * width]).astype(BF16)
            for p in range(pairs):
                qkv_ref[part * pairs + p, rows, :] = out[:, p * lanes:(p + 1) * lanes]
        return carry

    lax.fori_loop(0, quarters, project, 0, unroll=True)

    def attend(p, carry):
        values_t = qkv_ref[2 * pairs + p].T
        for j in range(quarters):
            seen = (j + 1) * tile
            queries = qkv_ref[p, j * tile:seen, :] * jnp.asarray(factor, BF16)
            outs = []
            for h in range(2):
                masked = jnp.where(head_lanes(tile, lanes, h), queries, jnp.zeros((), BF16))
                scores = dot_nt(qkv_ref[pairs + p, :seen, :], masked)
                last = jnp.where(causal_tile(tile), scores[j * tile:], NEG_FILL)
                scores = jnp.concatenate([scores[:j * tile], last], 0) if j else last
                high = jnp.max(scores, 0, keepdims=True)
                weights = jnp.exp(scores - high)
                total = jnp.sum(weights, 0, keepdims=True)
                out = dot_nn(values_t[h * half:(h + 1) * half, :seen], weights.astype(BF16))
                outs.append(out / total)
                lse_ref[2 * p + h, :, j * tile:seen] = high + jnp.log(total)
            ctx_pairs[p, j * tile:seen, :] = jnp.concatenate(outs, 0).T.astype(BF16)
        return carry

    lax.fori_loop(0, pairs, attend, 0)

    def finish(i, carry):
        rows = pl.ds(pl.multiple_of(i * tile, tile), tile)
        context = jnp.concatenate([ctx_pairs[p, rows, :] for p in range(pairs)], -1)
        ctx_ref[rows, :] = context
        attn = dot_nn(context, wo_ref[...])
        attn_ref[rows, :] = attn
        normed, _ = row_norm(x_ref[rows, :].astype(F32) + attn)
        mix = (normed * g2_ref[...]).astype(BF16)
        low = attn.astype(BF16)
        for b in range(nb):
            at = b * CHUNKS * PB
            mix_ref[b, i] = mix[at:at + PB]
            more_ref[b, 0, i] = mix[at + PB:at + 2 * PB]
            more_ref[b, 1, i] = low[at:at + PB]
            more_ref[b, 2, i] = low[at + PB:at + 2 * PB]
        return carry

    lax.fori_loop(0, quarters, finish, 0, unroll=True)


def attention_forward(z, parts, wqkv, wo, g1, g2, nb, waits=()):
    quarters = len(parts)
    tile, width = parts[0].shape
    length = quarters * tile
    pairs = HEADS // 2
    lanes = width // pairs
    vmem = pl.BlockSpec(memory_space=pltpu.VMEM)
    return pl.pallas_call(
        functools.partial(attention_forward_kernel, len(waits)),
        in_specs=[pl.BlockSpec(memory_space=pltpu.SMEM)]
        + [pl.BlockSpec(memory_space=pl.ANY)] * (quarters + len(waits)) + [vmem] * 4,
        out_shape=(
            jax.ShapeDtypeStruct((length, width), BF16),
            jax.ShapeDtypeStruct((3 * pairs, length, lanes), BF16),
            jax.ShapeDtypeStruct((HEADS, 1, length), F32),
            jax.ShapeDtypeStruct((length, width), BF16),
            jax.ShapeDtypeStruct((length, width), F32),
            jax.ShapeDtypeStruct((nb, quarters, PB, width), BF16),
            jax.ShapeDtypeStruct((nb, 3, quarters, PB, width), BF16),
        ),
        scratch_shapes=[
            pltpu.VMEM((pairs, length, lanes), BF16),
            pltpu.SemaphoreType.DMA((quarters,)),
        ],
        compiler_params=pltpu.CompilerParams(vmem_limit_bytes=VMEM_LIMIT),
        cost_estimate=SMALL_COST,
        name="attention_forward",
    )(z, *parts, *waits, wqkv, wo, g1, g2)


def attention_backward_kernel(count, *refs):
    attention_backward_body(*refs[:12], *refs[12 + count:])


def attention_backward_body(gm0_ref, gm1_ref, cot_ref, x_ref, attn_ref, ctx_ref, qkv_ref, lse_ref,
                              wqkv_ref, wo_ref, g1_ref, g2_ref,
                              gin_ref, dw_ref, dg1_ref, dg2_ref,
                              delta, ga_rows, dctx, gqkv, attn_in, dk_sum, dv_sum):
    length, width = x_ref.shape
    pairs = HEADS // 2
    lanes = width // pairs
    half = lanes // 2
    nb, quarters, _, _ = gm0_ref.shape
    tile = length // quarters
    factor = half ** (-0.5)
    dg2_ref[...] = jnp.zeros_like(dg2_ref)
    dg1_ref[...] = jnp.zeros_like(dg1_ref)

    def first(i, carry):
        rows = pl.ds(pl.multiple_of(i * tile, tile), tile)
        normed, inverse = row_norm(x_ref[rows, :].astype(F32) + attn_ref[rows, :])
        grad = jnp.concatenate([r[b, i] for b in range(nb) for r in (gm0_ref, gm1_ref)], 0).astype(F32)
        dg2_ref[...] += jnp.sum(grad * normed, 0, keepdims=True)
        back = row_norm_back(grad, normed, inverse, g2_ref[...])
        delta[rows, :] = back
        cot = jnp.concatenate([cot_ref[b, i] for b in range(nb)], 0).astype(F32)
        grad_attn = (cot + back).astype(BF16)
        ga_rows[rows, :] = grad_attn
        grad_ctx = dot_nt(grad_attn, wo_ref[...]).astype(BF16)
        for p in range(pairs):
            dctx[p, rows, :] = grad_ctx[:, p * lanes:(p + 1) * lanes]
        return carry

    lax.fori_loop(0, quarters, first, 0, unroll=True)

    dw_ref[:, 3 * width:] = dot_tn(ctx_ref[...], ga_rows[...]).astype(BF16)

    def attend(p, carry):
        lane0 = pl.multiple_of(p * lanes, lanes)
        keys_t = qkv_ref[pairs + p].T
        dk_sum[...] = jnp.zeros_like(dk_sum)
        dv_sum[...] = jnp.zeros_like(dv_sum)
        for j in range(quarters):
            seen = (j + 1) * tile
            queries = qkv_ref[p, j * tile:seen, :] * jnp.asarray(factor, BF16)
            grads = dctx[p, j * tile:seen, :]
            context = ctx_ref[j * tile:seen, pl.ds(lane0, lanes)]
            products = (grads.astype(F32) * context.astype(F32)).T
            outs = []
            for h in range(2):
                inside = head_lanes(tile, lanes, h)
                q_masked = jnp.where(inside, queries, jnp.zeros((), BF16))
                g_masked = jnp.where(inside, grads, jnp.zeros((), BF16))
                dots = jnp.sum(products[h * half:(h + 1) * half], 0, keepdims=True)
                scores = dot_nt(qkv_ref[pairs + p, :seen, :], q_masked)
                probs = jnp.exp(scores - lse_ref[2 * p + h, :, j * tile:seen])
                last = jnp.where(causal_tile(tile), probs[j * tile:], 0.0)
                probs = jnp.concatenate([probs[:j * tile], last], 0) if j else last
                grad_probs = dot_nt(qkv_ref[2 * pairs + p, :seen, :], g_masked)
                grad_scores = (probs * (grad_probs - dots)).astype(BF16)
                dv_sum[:seen, :] += dot_nn(probs.astype(BF16), g_masked)
                dk_sum[:seen, :] += dot_nn(grad_scores, q_masked)
                outs.append(dot_nn(keys_t[h * half:(h + 1) * half, :seen], grad_scores))
            gqkv[p, j * tile:seen, :] = (jnp.concatenate(outs, 0).T * factor).astype(BF16)
        gqkv[pairs + p] = dk_sum[...].astype(BF16)
        gqkv[2 * pairs + p] = dv_sum[...].astype(BF16)
        return carry

    lax.fori_loop(0, pairs, attend, 0)

    def last(i, carry):
        rows = pl.ds(pl.multiple_of(i * tile, tile), tile)
        normed, inverse = row_norm(x_ref[rows, :].astype(F32))
        attn_in[rows, :] = (normed * g1_ref[...]).astype(BF16)
        grads = jnp.concatenate([gqkv[c, rows, :] for c in range(3 * pairs)], -1)
        grad = dot_nt(grads, wqkv_ref[...])
        dg1_ref[...] += jnp.sum(grad * normed, 0, keepdims=True)
        gin_ref[rows, :] = (delta[rows, :] + row_norm_back(grad, normed, inverse, g1_ref[...])).astype(BF16)
        return carry

    lax.fori_loop(0, quarters, last, 0, unroll=True)

    for c in range(3):
        grads = jnp.concatenate([gqkv[c * pairs + p] for p in range(pairs)], -1)
        dw_ref[:, c * width:(c + 1) * width] = dot_tn(attn_in[...], grads).astype(BF16)


def attention_backward(gm0, gm1, cot, x, attn, ctx, qkv, lse, wqkv, wo, g1, g2, waits=()):
    length, width = x.shape
    pairs = HEADS // 2
    lanes = width // pairs
    return pl.pallas_call(
        functools.partial(attention_backward_kernel, len(waits)),
        in_specs=[pl.BlockSpec(memory_space=pltpu.VMEM)] * 12 + [pl.BlockSpec(memory_space=pl.ANY)] * len(waits),
        out_shape=(
            jax.ShapeDtypeStruct((length, width), BF16),
            jax.ShapeDtypeStruct((width, 4 * width), BF16),
            jax.ShapeDtypeStruct((1, width), F32),
            jax.ShapeDtypeStruct((1, width), F32),
        ),
        scratch_shapes=[
            pltpu.VMEM((length, width), F32),
            pltpu.VMEM((length, width), BF16),
            pltpu.VMEM((pairs, length, lanes), BF16),
            pltpu.VMEM((3 * pairs, length, lanes), BF16),
            pltpu.VMEM((length, width), BF16),
            pltpu.VMEM((length, lanes), F32),
            pltpu.VMEM((length, lanes), F32),
        ],
        compiler_params=pltpu.CompilerParams(vmem_limit_bytes=VMEM_LIMIT),
        cost_estimate=SMALL_COST,
        name="attention_backward",
    )(gm0, gm1, cot, x, attn, ctx, qkv, lse, wqkv, wo, g1, g2, *waits)


def group_reduce(rows, mem, op, fill):
    result = jnp.zeros_like(rows)
    for k in range(mem.shape[0]):
        inside = mem[k:k + 1, :] > 0
        part = jnp.where(inside, rows, fill)
        shift = rows.shape[1] // 2
        while shift >= PB:
            part = op(part, pltpu.roll(part, shift, 1))
            shift //= 2
        result = jnp.where(inside, part, result)
    return result


def gelu_both(v):
    square = v * v
    tanh = jnp.tanh(0.7978845608028654 * v * (1.0 + 0.044715 * square))
    half = 0.5 * (1.0 + tanh)
    slope = half + v * (1.0 - tanh * tanh) * (0.3989422804014327 + 0.0535161223274472 * square)
    return v * half, slope


def start(copy):
    copy.start()


def wait(copy):
    copy.wait()


def arrivals(z, sources, sems, base, act, place):
    if len(sources) == 1:
        act(pltpu.make_async_copy(*place(sources[0], None), sems.at[base]))
        return
    n = (len(sources) + 1) // 2
    act(pltpu.make_async_copy(*place(sources[0], z), sems.at[base]))
    for k in range(1, n):
        @pl.when(z >= k)
        def _():
            act(pltpu.make_async_copy(*place(sources[k], z - k), sems.at[base + k]))

        @pl.when(z + k < n)
        def _():
            act(pltpu.make_async_copy(*place(sources[n - 1 + k], z + k), sems.at[base + n - 1 + k]))


def x_rows(xs, m, q, sl):
    planes, nb, quarters, piece, width = xs.shape
    return jnp.concatenate([xs[m * sl + s, :, q].reshape(nb * piece, width) for s in range(sl)], 0)


def g_rows(gs, m, q, sl):
    quarters, nb, planes, piece, width = gs.shape
    return jnp.concatenate([gs[q, :, m * sl + s].reshape(nb * piece, width) for s in range(sl)], 0)


def mixture_forward_kernel(chunk, parts, waits, z_ref, *refs):
    x_in, refs = refs[:parts], refs[parts + waits:]
    (a_in, ctrl_ref, mem_ref, mkl_ref, take_ref, w1_ref, w2_ref,
     spread_ref, mixed_ref, hid_ref, slope_ref, eo_ref, weights_ref, gates_ref,
     xs, attn, logits, sems) = refs
    planes, nb, quarters, piece, width = xs.shape
    micro = mem_ref.shape[0]
    sl = planes // micro
    experts = mixed_ref.shape[0]
    rows = mkl_ref.shape[1]
    e = pl.program_id(0)
    z = z_ref[0]
    x_place = lambda ref, plane: (ref, xs if plane is None else xs.at[plane])
    a_copy = pltpu.make_async_copy(a_in.at[:, 1 + chunk], attn, sems.at[parts])

    @pl.when(e == 0)
    def _():
        arrivals(z, x_in, sems, 0, start, x_place)
        a_copy.start()
        arrivals(z, x_in, sems, 0, wait, x_place)
        for m in range(micro):
            for q in range(quarters):
                logits[m, q * 8:(q + 1) * 8, :] = dot_nt(ctrl_ref[...], x_rows(xs, m, q, sl))[:8]
            mem = mem_ref[m]
            taking = take_ref[m] > 0
            values = logits[m]
            high = group_reduce(jnp.where(taking, values, NEG_FILL), mem, jnp.maximum, NEG_FILL)
            scaled = jnp.where(taking, jnp.exp(values - high), 0.0)
            gates_ref[m] = scaled / group_reduce(scaled, mem, jnp.add, 0.0)
        for m in range(micro):
            for q in range(quarters):
                block = m * quarters + q
                own = gates_ref[m, q * 8:(q + 1) * 8, :]
                w = jnp.concatenate(
                    [(mkl_ref[m] * own[j:j + 1, :]).astype(BF16) for j in range(experts)], 0)
                weights_ref[block] = w
                blended = dot_nn(w, x_rows(xs, m, q, sl)).astype(BF16)
                for j in range(experts):
                    mixed_ref[j, block * rows:(block + 1) * rows, :] = blended[j * rows:(j + 1) * rows]

    value, slope = gelu_both(dot_nn(mixed_ref[e], w1_ref[0]))
    hidden = value.astype(BF16)
    hid_ref[0] = hidden
    slope_ref[0] = slope.astype(BF16)
    eo_ref[e] = dot_nn(hidden, w2_ref[0]).astype(BF16)

    @pl.when(e == experts - 1)
    def _():
        for m in range(micro):
            for q in range(quarters):
                block = m * quarters + q
                outs = jnp.concatenate(
                    [eo_ref[j, block * rows:(block + 1) * rows, :] for j in range(experts)], 0)
                spread = dot_tn(weights_ref[block], outs).astype(BF16)
                for s in range(sl):
                    at = slice(s * nb * PB, (s + 1) * nb * PB)
                    spread_ref[q, :, 0, m * sl + s] = spread[at].reshape(nb, PB, width)
        a_copy.wait()
        for q in range(quarters):
            mine = spread_ref[q, :, 0, z].astype(F32) + attn[:, q].astype(F32)
            spread_ref[q, :, 0, z] = mine.astype(BF16)


def mixture_backward_kernel(chunk, parts, waits, z_ref, *refs):
    x_in, g_in, refs = refs[:parts], refs[parts:2 * parts], refs[2 * parts + waits:]
    (ctrl_ref, mem_ref, mkl_ref, weights_ref, gates_ref, eo_ref, slope_ref, w1_ref, w2_ref,
     gm_ref, geo_ref, gpre_ref, dctrl_ref, xs, gs, gmx, sems) = refs
    planes, nb, quarters, piece, width = xs.shape
    micro, _, lanes = mem_ref.shape
    sl = planes // micro
    experts = geo_ref.shape[0]
    rows = mkl_ref.shape[1]
    e = pl.program_id(0)
    z = z_ref[0]
    mine = pl.ds(chunk * PB, PB)
    x_place = lambda ref, plane: (ref, xs if plane is None else xs.at[plane])
    g_place = lambda ref, plane: (ref.at[..., mine, :], gs if plane is None else gs.at[plane])

    @pl.when(e == 0)
    def _():
        arrivals(z, g_in, sems, 0, start, g_place)
        arrivals(z, x_in, sems, parts, start, x_place)
        arrivals(z, g_in, sems, 0, wait, g_place)
        for m in range(micro):
            for q in range(quarters):
                block = m * quarters + q
                grads = dot_nn(weights_ref[block], g_rows(gs, m, q, sl)).astype(BF16)
                for j in range(experts):
                    geo_ref[j, block * rows:(block + 1) * rows, :] = grads[j * rows:(j + 1) * rows]
        arrivals(z, x_in, sems, parts, wait, x_place)

    grad_pre = (dot_nt(geo_ref[e], w2_ref[0]) * slope_ref[0].astype(F32)).astype(BF16)
    gpre_ref[0] = grad_pre
    gmx[e] = dot_nt(grad_pre, w1_ref[0]).astype(BF16)

    @pl.when(e == experts - 1)
    def _():
        dctrl = jnp.zeros(dctrl_ref.shape, F32)
        ctrl8 = ctrl_ref[...].astype(F32)[:8]
        ctrl_twice = jnp.concatenate([ctrl8, ctrl8], 0).astype(BF16)
        for m in range(micro):
            for q in range(quarters):
                block = m * quarters + q
                at = slice(block * rows, (block + 1) * rows)
                outs = jnp.concatenate([eo_ref[j, at, :] for j in range(experts)], 0)
                backs = jnp.concatenate([gmx[j, at, :] for j in range(experts)], 0)
                w = weights_ref[block]
                inputs = x_rows(xs, m, q, sl)
                dots = dot_nt(outs, g_rows(gs, m, q, sl)) + dot_nt(backs, inputs)
                grad_gates = [
                    jnp.sum(dots[j * rows:(j + 1) * rows] * mkl_ref[m], 0, keepdims=True)
                    for j in range(experts)]
                if experts < 8:
                    grad_gates.append(jnp.zeros((8 - experts, lanes), F32))
                grad_gates = jnp.concatenate(grad_gates, 0)
                own = gates_ref[m, q * 8:(q + 1) * 8, :]
                inner = group_reduce(own * grad_gates, mem_ref[m], jnp.add, 0.0)
                grad_logits = own * (grad_gates - inner)
                upper = grad_logits.astype(BF16).astype(F32)
                both = jnp.concatenate([upper, grad_logits - upper], 0).astype(BF16)
                grad_mix = (dot_tn(w, backs) + dot_tn(both, ctrl_twice)).astype(BF16)
                for s in range(sl):
                    part = slice(s * nb * PB, (s + 1) * nb * PB)
                    gm_ref[m * sl + s, :, q] = grad_mix[part].reshape(nb, PB, width)
                dctrl += dot_nn(both, inputs)
        dctrl_ref[...] = dctrl


def whole(shape):
    return pl.BlockSpec(shape, lambda e: (0,) * len(shape))


def by_expert(shape):
    return pl.BlockSpec((1,) + shape[1:], lambda e: (e, 0, 0))


def mixture_sizes(x_parts, mem, mkl, w1):
    nb, quarters, piece, width = x_parts[0].shape[-4:]
    planes = quarters
    experts, _, hidden_size = w1.shape
    total = mem.shape[0] * quarters * mkl.shape[1]
    back = (planes, nb, quarters, piece, width)
    return back, (experts, total, width), (experts, total, hidden_size)


def mixture_forward(chunk, z, x_parts, a_all, ctrl, mem, mkl, take, w1, w2, waits=()):
    back, narrow, wide = mixture_sizes(x_parts, mem, mkl, w1)
    micro, _, lanes = mem.shape
    quarters = back[2]
    weights = (micro * quarters, narrow[0] * mkl.shape[1], lanes)
    gates = (micro, quarters * 8, lanes)
    any_spec = pl.BlockSpec(memory_space=pl.ANY)
    return pl.pallas_call(
        functools.partial(mixture_forward_kernel, chunk, len(x_parts), len(waits)),
        grid=(narrow[0],),
        input_output_aliases={1 + len(x_parts): 0} if chunk else {},
        out_shape=(
            jax.ShapeDtypeStruct(back[:2] + (CHUNKS,) + back[2:], BF16),
            jax.ShapeDtypeStruct(narrow, BF16),
            jax.ShapeDtypeStruct(wide, BF16),
            jax.ShapeDtypeStruct(wide, BF16),
            jax.ShapeDtypeStruct(narrow, BF16),
            jax.ShapeDtypeStruct(weights, BF16),
            jax.ShapeDtypeStruct(gates, F32),
        ),
        in_specs=[pl.BlockSpec(memory_space=pltpu.SMEM)]
        + [any_spec] * (len(x_parts) + len(waits) + 1)
        + [whole(ctrl.shape), whole(mem.shape), whole(mkl.shape), whole(take.shape),
           by_expert(w1.shape), by_expert(w2.shape)],
        out_specs=(pl.BlockSpec(back[:2] + (1,) + back[2:], lambda e: (0, 0, chunk, 0, 0, 0)), whole(narrow), by_expert(wide), by_expert(wide),
                   whole(narrow), whole(weights), whole(gates)),
        scratch_shapes=[
            pltpu.VMEM(back, BF16),
            pltpu.VMEM(back[1:], BF16),
            pltpu.VMEM(gates, F32),
            pltpu.SemaphoreType.DMA((len(x_parts) + 1,)),
        ],
        compiler_params=pltpu.CompilerParams(vmem_limit_bytes=VMEM_LIMIT),
        cost_estimate=SMALL_COST,
        name="mixture_forward",
    )(z, *x_parts, *waits, a_all, ctrl, mem, mkl, take, w1, w2)


def mixture_backward(chunk, z, x_parts, g_parts, ctrl, mem, mkl, weights, gates, eo, slope, w1, w2, waits=()):
    back, narrow, wide = mixture_sizes(x_parts, mem, mkl, w1)
    parts = len(x_parts)
    any_spec = pl.BlockSpec(memory_space=pl.ANY)
    return pl.pallas_call(
        functools.partial(mixture_backward_kernel, chunk, parts, len(waits)),
        grid=(narrow[0],),
        out_shape=(
            jax.ShapeDtypeStruct(back, BF16),
            jax.ShapeDtypeStruct(narrow, BF16),
            jax.ShapeDtypeStruct(wide, BF16),
            jax.ShapeDtypeStruct((16, back[4]), F32),
        ),
        in_specs=[pl.BlockSpec(memory_space=pltpu.SMEM)]
        + [any_spec] * (2 * parts + len(waits))
        + [whole(ctrl.shape), whole(mem.shape), whole(mkl.shape), whole(weights.shape),
           whole(gates.shape), whole(narrow), by_expert(wide), by_expert(w1.shape), by_expert(w2.shape)],
        out_specs=(whole(back), whole(narrow), by_expert(wide), whole((16, back[4]))),
        scratch_shapes=[
            pltpu.VMEM(back, BF16),
            pltpu.VMEM(back, BF16),
            pltpu.VMEM(narrow, BF16),
            pltpu.SemaphoreType.DMA((2 * parts,)),
        ],
        compiler_params=pltpu.CompilerParams(vmem_limit_bytes=VMEM_LIMIT),
        cost_estimate=SMALL_COST,
        name="mixture_backward",
    )(z, *x_parts, *g_parts, *waits, ctrl, mem, mkl, weights, gates, eo, slope, w1, w2)


def weight_grads_kernel(z_ref, m0, m1, p0, p1, h0, h1, o0, o1, *refs):
    keep_ref, send_ref = refs[-2:]
    width, step = keep_ref.shape[-2:]
    crossed = pl.program_id(0) >= pl.num_programs(0) // 2
    core = lax.rem(z_ref[1], 2)
    left1 = m0[0].T, m1[0].T
    left2 = o0[0].T, o1[0].T
    for t in range(p0.shape[2] // step // 2):
        x, y = t % 2, t // 2
        hop1, hop2 = jnp.where(crossed, y, x), jnp.where(crossed, x, y)
        for ref, part in ((keep_ref, core), (send_ref, 1 - core)):
            at = pl.ds(pl.multiple_of((2 * t + part) * step, step), step)
            first = dot_nn(left1[0], p0[0, :, at]) + dot_nn(left1[1], p1[0, :, at])
            ref[0, 0, hop1, hop2, 0] = first.astype(BF16)
            second = dot_nn(left2[0], h0[0, :, at]) + dot_nn(left2[1], h1[0, :, at])
            ref[0, 0, hop1, hop2, 1] = second.astype(BF16)


def weight_grads(z, mixed, gpre, hid, geo, nb, waits=()):
    experts, total, width = mixed[0].shape
    hidden_size = gpre[0].shape[2]
    step = hidden_size // nb
    half = experts // 2
    row = pl.BlockSpec((1, total, width), lambda e: (e, 0, 0))
    wide = pl.BlockSpec((1, total, hidden_size), lambda e: (e, 0, 0))
    out = pl.BlockSpec((1, 1, 2, 2, 2, width, step), lambda e: (e // half, e % half, 0, 0, 0, 0, 0))
    return pl.pallas_call(
        weight_grads_kernel,
        grid=(experts,),
        in_specs=[pl.BlockSpec(memory_space=pltpu.SMEM)]
        + [row] * 2 + [wide] * 4 + [row] * 2 + [pl.BlockSpec(memory_space=pl.ANY)] * len(waits),
        out_shape=(jax.ShapeDtypeStruct((2, half, 2, 2, 2, width, step), BF16),) * 2,
        out_specs=(out, out),
        compiler_params=pltpu.CompilerParams(vmem_limit_bytes=VMEM_LIMIT),
        cost_estimate=SMALL_COST,
        name="weight_grads",
    )(z, *mixed, *gpre, *hid, *geo, *waits)


def pick(parts, index):
    return lax.dynamic_index_in_dim(parts, index, 0, keepdims=False)


def pass_on(*refs):
    pass


def after(value, *others):
    spec = pl.BlockSpec(memory_space=pl.ANY)
    return pl.pallas_call(
        pass_on,
        out_shape=jax.ShapeDtypeStruct(value.shape, value.dtype),
        in_specs=[spec] * (1 + len(others)),
        out_specs=spec,
        input_output_aliases={0: 0},
        name="after",
        cost_estimate=SMALL_COST,
    )(value, *others)


def line_step(ups, downs, count):
    up = [(i, i + 1) for i in range(count - 1)]
    down = [(i + 1, i) for i in range(count - 1)]
    return (ups + [lax.ppermute(ups[-1], "expert", up)],
            downs + [lax.ppermute(downs[-1], "expert", down)])


def line_scatter(parts, z, count):
    up = [(i, i + 1) for i in range(count - 1)]
    down = [(i + 1, i) for i in range(count - 1)]

    def own(index):
        return pick(parts, jnp.clip(index, 0, count - 1)).astype(F32)

    rising, falling = own(z + count - 1).astype(BF16), own(z - count + 1).astype(BF16)
    for step in range(1, count):
        rising = lax.ppermute(rising, "expert", up).astype(F32)
        falling = lax.ppermute(falling, "expert", down).astype(F32)
        if step < count - 1:
            rising = (rising + own(z + count - 1 - step)).astype(BF16)
            falling = (falling + own(z - count + 1 + step)).astype(BF16)
    return (rising + falling + own(z)).astype(BF16)


def for_planes(parts, z, count):
    return [pick(parts, lax.rem(z + k, count)) for k in range(count)]


def to_planes(picked, count):
    got = picked[:1]
    for k in range(1, count):
        got.append(lax.ppermute(picked[k], "expert", [(i, (i + k) % count) for i in range(count)]))
    return got


def swap_halves(blocks, bit, count):
    mine = lax.rem(lax.axis_index("batch") >> bit, 2)
    other = lax.ppermute(pick(blocks, 1 - mine), "batch", [(i, i ^ (1 << bit)) for i in range(count)])
    return (pick(blocks, mine).astype(F32) + other.astype(F32)).astype(BF16)


def hop_bits(half):
    return (1, 2) if half == 0 else (2, 1)


def add_blocks(*refs):
    total = refs[0][...].astype(F32)
    for ref in refs[1:]:
        total += ref[...].reshape(total.shape).astype(F32)
    return total


def first_sends_kernel(pos_ref, *refs):
    ins, outs = refs[:8], refs[-4:]
    for i, out in enumerate(outs):
        out[...] = add_blocks(*ins[2 * i:2 * i + 2]).astype(BF16).reshape(out.shape)


def first_sends(pos, keep, came, waits=()):
    halves, experts, _, _, _, rows, cols = keep.shape
    pieces = [(i, e) for i in range(halves) for e in range(experts)]

    def place(i, e):
        bit = hop_bits(i)[0]
        return lambda h, w, pos: (i, e, 1 - lax.rem(pos[1] >> bit, 2), h, w, 0, 0)

    block = (1, 1, 1, 1, 1, rows, cols)
    out = pl.BlockSpec((1, 1, rows, cols), lambda h, w, pos: (h, w, 0, 0))
    return pl.pallas_call(
        first_sends_kernel,
        grid_spec=pltpu.PrefetchScalarGridSpec(
            num_scalar_prefetch=1, grid=(2, 2),
            in_specs=[pl.BlockSpec(block, place(i, e)) for i, e in pieces for _ in range(2)]
            + [pl.BlockSpec(memory_space=pl.ANY)] * len(waits),
            out_specs=(out,) * len(pieces)),
        out_shape=(jax.ShapeDtypeStruct((2, 2, rows, cols), BF16),) * len(pieces),
        compiler_params=pltpu.CompilerParams(vmem_limit_bytes=VMEM_LIMIT),
        cost_estimate=SMALL_COST,
        name="first_sends",
    )(pos, *[array for _ in pieces for array in (keep, came)], *waits)


def second_sends_kernel(pos_ref, *refs):
    ins, outs = refs[:-4], refs[-4:]
    for i, out in enumerate(outs):
        out[...] = add_blocks(*ins[3 * i:3 * i + 3]).astype(BF16).reshape(out.shape)


def own_place(i, e, last):
    first, second = hop_bits(i)

    def place(w, pos):
        mine = lax.rem(pos[1] >> second, 2)
        return (i, e, lax.rem(pos[1] >> first, 2), jnp.where(last == 1, 1 - mine, mine), w, 0, 0)

    def place_got(w, pos):
        return place(w, pos)[3:]

    return place, place_got


def second_sends(pos, keep, came, got):
    halves, experts, _, _, _, rows, cols = keep.shape
    pieces = [(i, e) for i in range(halves) for e in range(experts)]
    specs = []
    for i, e in pieces:
        place, place_got = own_place(i, e, 1)
        specs += [pl.BlockSpec((1, 1, 1, 1, 1, rows, cols), place)] * 2
        specs += [pl.BlockSpec((1, 1, rows, cols), place_got)]
    out = pl.BlockSpec((1, rows, cols), lambda w, pos: (w, 0, 0))
    return pl.pallas_call(
        second_sends_kernel,
        grid_spec=pltpu.PrefetchScalarGridSpec(
            num_scalar_prefetch=1, grid=(2,), in_specs=specs, out_specs=(out,) * len(pieces)),
        out_shape=(jax.ShapeDtypeStruct((2, rows, cols), BF16),) * len(pieces),
        compiler_params=pltpu.CompilerParams(vmem_limit_bytes=VMEM_LIMIT),
        cost_estimate=SMALL_COST,
        name="second_sends",
    )(pos, *[array for n in range(len(pieces)) for array in (keep, came, got[n])])


def expert_sums_kernel(pos_ref, *refs):
    ins, (first_ref, second_ref) = refs[:-2], refs[-2:]
    for i in range(len(ins) // 4):
        total = add_blocks(*ins[4 * i:4 * i + 4]).reshape(ins[4 * i].shape[-3:])
        first_ref[i] = total[0]
        second_ref[i] = total[1].T


def expert_sums(pos, keep, came, got, got_last):
    halves, experts, _, _, _, rows, cols = keep.shape
    pieces = [(i, e) for i in range(halves) for e in range(experts)]
    specs = []
    for i, e in pieces:
        place, place_got = own_place(i, e, 0)
        specs += [pl.BlockSpec((1, 1, 1, 1, 2, rows, cols), place)] * 2
        specs += [pl.BlockSpec((1, 2, rows, cols), place_got)]
        specs += [pl.BlockSpec((2, rows, cols), lambda w, pos: (0, 0, 0))]
    out = lambda shape: pl.BlockSpec(shape, lambda w, pos: (0, 0, 0))
    shapes = (len(pieces), rows, cols), (len(pieces), cols, rows)
    return pl.pallas_call(
        expert_sums_kernel,
        grid_spec=pltpu.PrefetchScalarGridSpec(
            num_scalar_prefetch=1, grid=(1,), in_specs=specs, out_specs=tuple(out(s) for s in shapes)),
        out_shape=tuple(jax.ShapeDtypeStruct(s, F32) for s in shapes),
        compiler_params=pltpu.CompilerParams(vmem_limit_bytes=VMEM_LIMIT),
        cost_estimate=SMALL_COST,
        name="expert_sums",
    )(pos, *[array for n in range(len(pieces)) for array in (keep, came, got[n], got_last[n])])


def cross(block, bit):
    return lax.ppermute(block, "batch", [(j, j ^ (1 << bit)) for j in range(8)])


def add_home_kernel(z_ref, *refs):
    n = len(refs) - 4
    parts, (base_ref, out_ref, came, sems) = refs[:n], refs[n:]
    copies = [
        pltpu.make_async_copy(parts[k], came.at[lax.rem(z_ref[0] - k + n, n)], sems.at[k]) for k in range(n)]
    for copy in copies:
        copy.start()
    for copy in copies:
        copy.wait()
    out_ref[...] = base_ref[...] + came[...].astype(F32)


def add_home(z, parts, base):
    vmem = pl.BlockSpec(memory_space=pltpu.VMEM)
    return pl.pallas_call(
        add_home_kernel,
        out_shape=jax.ShapeDtypeStruct(base.shape, F32),
        in_specs=[pl.BlockSpec(memory_space=pltpu.SMEM)] + [pl.BlockSpec(memory_space=pl.ANY)] * len(parts) + [vmem],
        scratch_shapes=[pltpu.VMEM(base.shape, BF16), pltpu.SemaphoreType.DMA((len(parts),))],
        compiler_params=pltpu.CompilerParams(vmem_limit_bytes=VMEM_LIMIT),
        cost_estimate=SMALL_COST,
        name="add_home",
    )(z, *parts, base)


def body(
    tokens,
    cotangent,
    query_key_value_weight,
    output_weight,
    controller_weight,
    w_first,
    w_second,
    gain_one,
    gain_two,
    group_sizes,
    live,
):
    micro, sl, local_len, width = tokens.shape
    planes = lax.axis_size("expert")
    nb = lax.axis_size("batch")
    experts = w_first.shape[0]
    seqs = live.shape[1]
    z = lax.axis_index("expert")
    piece = local_len // nb
    if micro * sl != planes or piece != CHUNKS * PB or nb != 8:
        return body_by_position(
            tokens, cotangent, query_key_value_weight, output_weight, controller_weight,
            w_first, w_second, gain_one, gain_two, group_sizes, live)
    g1, g2 = gain_one.reshape(1, width), gain_two.reshape(1, width)

    own = lax.axis_index("batch")
    z_arr = jnp.stack([z, own]).astype(jnp.int32)
    x_parts = to_planes(for_planes(tokens.reshape(planes, local_len, width).astype(BF16), z, planes), planes)

    cot = cotangent.reshape(planes, nb, piece, width)
    pieces = []
    for k in range(nb):
        part = lax.dynamic_index_in_dim(cot, own ^ k, 1, keepdims=False).astype(BF16)
        if k:
            part = lax.ppermute(part, "batch", [(i, i ^ k) for i in range(nb)])
        pieces.append(part)
    pieces[-1] = after(pieces[-1], x_parts[2])
    cot = jnp.take(jnp.stack(pieces), own ^ jnp.arange(nb), axis=0)
    g_all = lax.all_gather(cot, "expert", axis=0, tiled=False)

    x, qkv, lse, ctx, attn, mix, more = attention_forward(
        z_arr, x_parts, query_key_value_weight, output_weight, g1, g2, nb, waits=(cot,))

    member, taking = jax.vmap(group_tables)(group_sizes, live)
    groups = member.shape[2]
    mem = member.reshape(micro, nb, sl, groups).transpose(0, 3, 2, 1).reshape(micro, groups, seqs)
    mem = jnp.repeat(mem.astype(F32), PB, axis=2)
    take = taking.reshape(micro, nb, sl).transpose(0, 2, 1).reshape(micro, 1, seqs)
    take = jnp.repeat(take.astype(F32), PB, axis=2)
    place = jnp.arange(seqs * PB, dtype=jnp.int32) % PB
    same = (jnp.arange(PB, dtype=jnp.int32)[:, None] == place[None, :]).astype(F32)
    mkl = (mem[:, :, None, :] * same).reshape(micro, groups * PB, seqs * PB)
    ctrl = lax.dynamic_slice_in_dim(controller_weight, z * experts, experts, 1).T
    ctrl = jnp.pad(ctrl, ((0, 16 - experts), (0, 0)))

    def over_batch(block):
        return lax.all_to_all(block, "batch", split_axis=0, concat_axis=0, tiled=True)

    def over_expert(blocks):
        return lax.all_to_all(blocks, "expert", split_axis=0, concat_axis=0, tiled=True)

    own0 = over_batch(mix)
    x0 = [lax.all_gather(own0, "expert", axis=0, tiled=False)]
    more = over_batch(after(more, own0))
    x1 = [lax.all_gather(more[:, 0], "expert", axis=0, tiled=False)]
    g_parts = [g_all]

    cot_own = lax.dynamic_index_in_dim(g_all, z, 2, keepdims=False).transpose(1, 0, 2, 3)
    cot_own = over_batch(cot_own)
    spread0, mixed0, hid0, slope0, eo0, weights0, gates0 = mixture_forward(
        0, z_arr, x0, more, ctrl, mem, mkl, take, w_first, w_second, waits=(cot_own,))
    back0, geo0, gpre0, dctrl0 = mixture_backward(
        0, z_arr, x0, g_parts, ctrl, mem, mkl, weights0, gates0, eo0, slope0, w_first, w_second,
        waits=())
    back0 = lax.psum_scatter(after(back0, x1[0]), "expert", scatter_dimension=0, tiled=False)
    spread, mixed1, hid1, slope1, eo1, weights1, gates1 = mixture_forward(
        1, z_arr, x1, more, ctrl, mem, mkl, take, w_first, w_second, waits=(spread0, dctrl0))
    back1, geo1, gpre1, dctrl1 = mixture_backward(
        1, z_arr, x1, g_parts, ctrl, mem, mkl, weights1, gates1, eo1, slope1, w_first, w_second)
    dctrl = dctrl0[:8] + dctrl0[8:] + dctrl1[:8] + dctrl1[8:]
    back1 = lax.psum_scatter(after(back1, back0), "expert", scatter_dimension=0, tiled=False)
    back0 = over_batch(back0)
    keep, send = weight_grads(
        z_arr, (mixed0, mixed1), (gpre0, gpre1), (hid0, hid1), (geo0, geo1), nb, waits=(back0,))
    spread = lax.psum_scatter(after(spread, back1), "expert", scatter_dimension=0, tiled=False)
    send = after(send, back1)
    back1 = over_batch(back1)
    came = lax.ppermute(send, "batch", [(i, i ^ 1) for i in range(nb)])
    sends = first_sends(z_arr, keep, came, waits=(back1,))
    gin, dw, dg1, dg2 = attention_backward(
        back0, back1, cot_own, x, attn, ctx, qkv, lse, query_key_value_weight, output_weight, g1, g2,
        waits=sends)
    firsts = [hop_bits(n // 2)[0] for n in range(4)]
    got = [cross(sends[n], firsts[n]) for n in range(4)]
    parts = to_planes(for_planes(gin.reshape(planes, local_len, width), z, planes), planes)
    seconds = second_sends(z_arr, keep, came, got)
    dw = after(dw, seconds[0])
    got_last = [cross(part, hop_bits(n // 2)[1]) for n, part in enumerate(seconds)]
    grad_first, grad_second = expert_sums(z_arr, keep, came, got, got_last)

    grad_in = add_home(z_arr, parts, cotangent.reshape(planes, local_len, width)).reshape(tokens.shape)

    dctrl_all = jnp.zeros((planes, experts, width), F32)
    dctrl_all = lax.dynamic_update_slice(dctrl_all, dctrl[None, :experts], (z, 0, 0))
    dctrl_all = dctrl_all.reshape(planes * experts, width).T
    extra = jnp.concatenate([dctrl_all, dg1.T, dg2.T], 1)
    extra = jnp.pad(extra, ((0, 0), (0, 128 - extra.shape[1]))).astype(BF16)
    flat = jnp.concatenate([dw, extra], 1)
    flat = flat.reshape(nb // 2, 2, -1, flat.shape[1]).transpose(1, 0, 2, 3)
    flat = swap_halves(flat, 0, nb)
    chips = [[c + 2 * i for i in range(nb // 2)] for c in range(2)]
    flat = lax.all_to_all(flat, "batch", split_axis=0, concat_axis=0, tiled=True, axis_index_groups=chips)
    flat = jnp.sum(flat.astype(F32), 0).astype(BF16)
    flat = after(flat, *parts[1:])
    spread = over_batch(after(spread, flat, *got_last))
    out = tokens + spread.transpose(2, 0, 1, 3, 4).reshape(tokens.shape).astype(F32)
    flat = flat.reshape(planes, -1, flat.shape[1])
    flat = lax.all_to_all(flat, "expert", split_axis=0, concat_axis=0, tiled=True)
    flat = jnp.sum(flat.astype(F32), 0)
    ends = [3 * width, 4 * width, 4 * width + planes * experts]
    grad_qkv, grad_out, grad_ctrl = flat[:, :ends[0]], flat[:, ends[0]:ends[1]], flat[:, ends[1]:ends[2]]
    return (out, grad_in, grad_qkv, grad_out, grad_ctrl, grad_first, grad_second,
            flat[:, ends[2]], flat[:, ends[2] + 1])


def solution(mesh):
    placed = (
        P(None, "batch", "expert", None),
        P(None, "batch", "expert", None),
        P(),
        P(),
        P(),
        P("expert", None, None),
        P("expert", None, None),
        P(),
        P(),
        P(),
        P(),
    )
    return jax.shard_map(
        body,
        mesh=mesh,
        in_specs=placed,
        out_specs=(
            P(None, "batch", "expert", None),
            P(None, "batch", "expert", None),
            P(("batch", "expert"), None),
            P(("batch", "expert"), None),
            P(("batch", "expert"), None),
            P("expert", None, "batch"),
            P("expert", "batch", None),
            P(("batch", "expert")),
            P(("batch", "expert")),
        ),
        check_vma=False,
    )
```
